32 devices in a mesh: segment: 4 (over z), band: 8 (over y, x, core).
Axes of the slice: x: 2, y: 2, z: 4, core: 2. Of those that a mesh axis runs over, the one named last changes fastest.
Arguments:
- clip: bfloat16 [2, 32, 160, 128], P(None, 'band'), may hold values from -6 to 6
- caches: bfloat16 [4, 4, 2, 32, 160, 128], P('segment', None, None, 'band'), may hold values from -4 to 4
- weights: bfloat16 [4, 4, 9, 3, 128, 128], P('segment'), may hold values from -0.109375 to 0.109375
- biases: float32 [4, 4, 128], P('segment'), may hold values from -2 to 2
- section_layers: int32 [4], P('segment'), may hold values from 1 to 4, as said below
Outputs:
- section_out: bfloat16 [4, 2, 32, 160, 128], P('segment', None, 'band')
The draws below stay inside these ranges and needn't reach their ends.
Inputs may be any that keep to these rules, and one draw needn't show every extreme that they name: `section_layers`: each section has 1 to 4 layers, and some section has exactly 4.
All inputs are finite; a program needn't handle non-finite values.
Results may differ from the reference program's by a relative error of at most 0.024.
Values may be sent and summed in bfloat16 or wider, within the bound.
No kernel may reach another device: no remote copies, remote signals or barrier semaphores. Data moves between devices by JAX's collectives and lax.ppermute only.
A program may use at most 128 MiB of HBM per device.

```python
import jax
import jax.numpy as jnp

C = 128
W = 160
LMAX = 4
FRAMES = 2
SECTIONS = 4
ROWS = 32


def draw_section_layers(key, part):
    base = jax.random.randint(jax.random.fold_in(key, 11), (SECTIONS,), 1, LMAX + 1)
    chosen = jax.random.randint(jax.random.fold_in(key, 12), (), 0, SECTIONS)
    return jnp.where(jnp.arange(SECTIONS) == chosen, LMAX, base).astype(jnp.int32)


def block_levels(stream_key, dims, split, smallest, top_value):
    factor_of, own = 1.0, jax.random.fold_in(stream_key, 6)
    for dim, shards_of in split:
        steps = jnp.exp(jax.random.uniform(jax.random.fold_in(own, dim), (shards_of,), jnp.float32, smallest / len(split), top_value / len(split)))
        factor_of = factor_of * jnp.repeat(steps, dims[dim] // shards_of).reshape([-1 if axis == dim else 1 for axis in range(len(dims))])
    return factor_of


def bell_draw(rng, dims, deviation, bound, split=(), held_as=jnp.bfloat16):
    level = block_levels(rng, dims, split, -0.22, 0.18) if split else 1.0
    drawn = jax.random.normal(rng, dims, jnp.float32) * deviation * level
    return jnp.minimum(jnp.maximum(drawn, -bound), bound).astype(held_as)


def setup_inputs(seed: int = 0) -> dict:
    key_list = jax.random.split(jax.random.key(seed), 6)
    clip = bell_draw(key_list[0], (FRAMES, ROWS, W, C), 1.0, 6.0, ((1, 8),))
    caches = bell_draw(key_list[1], (SECTIONS, LMAX, 2, ROWS, W, C), 0.5, 4.0, ((0, 4), (3, 8)))
    weights = bell_draw(key_list[2], (SECTIONS, LMAX, 9, 3, C, C), (27 * C) ** -0.5, 0.109375, ((0, 4),))
    biases = bell_draw(key_list[3], (SECTIONS, LMAX, C), 0.3, 2.0, ((0, 4),), jnp.float32)
    section_layers = draw_section_layers(jax.random.fold_in(key_list[5], 71), 0)
    return dict(clip=clip, caches=caches, weights=weights, biases=biases, section_layers=section_layers)


def conv_layer(x, past, kernel, bias):
    act = jax.nn.silu(x.astype(jnp.float32)).astype(jnp.bfloat16)
    stack = jnp.concatenate([past, act[None]], axis=0)
    padded = jnp.pad(stack, ((0, 0), (1, 1), (1, 1), (0, 0)))
    rows = x.shape[0]
    width = x.shape[1]
    total = jnp.zeros(x.shape, jnp.float32)
    for k in range(9):
        row_tap = k // 3
        col_tap = k % 3
        piece = padded[:, row_tap:row_tap + rows, col_tap:col_tap + width, :]
        total = total + jnp.einsum("trwc,tcd->rwd", piece.astype(jnp.float32), kernel[k].astype(jnp.float32))
    result = (x.astype(jnp.float32) + total + bias).astype(jnp.bfloat16)
    return result, jnp.concatenate([past[1:], act[None]], axis=0)


def reference(clip, caches, weights, biases, section_layers):
    inputs = clip
    results = []
    for section in range(SECTIONS):
        history = [caches[section, layer] for layer in range(LMAX)]
        produced = []
        for frame in range(FRAMES):
            x = inputs[frame]
            for layer in range(LMAX):
                result, renewed = conv_layer(x, history[layer], weights[section, layer], biases[section, layer])
                live = layer < section_layers[section]
                x = jnp.where(live, result, x)
                history[layer] = jnp.where(live, renewed, history[layer])
            produced.append(x)
        inputs = jnp.stack(produced)
        results.append(inputs)
    return jnp.stack(results)
```

```python
import functools

import jax
import jax.numpy as jnp
from jax import lax
from jax.experimental import pallas as pl
from jax.experimental.pallas import tpu as pltpu
from jax.sharding import PartitionSpec as P

LIMIT = 32 * 1024 * 1024


def out_rows(rows, layer):
    return 3 * rows - 2 - 2 * layer


def offsets(rows, layers):
    starts = [0]
    for layer in range(layers):
        starts.append(starts[-1] + out_rows(rows, layer))
    return starts


def taps_into(s_ref, row, a):
    width, channels = a.shape
    column = lax.broadcasted_iota(jnp.int32, a.shape, 0)
    left = jnp.where(column == 0, 0.0, pltpu.roll(a, 1, 0))
    right = jnp.where(column == width - 1, 0.0, pltpu.roll(a, width - 1, 0))
    s_ref[row, :, 0:channels] = left.astype(jnp.bfloat16)
    s_ref[row, :, channels : 2 * channels] = a.astype(jnp.bfloat16)
    s_ref[row, :, 2 * channels : 3 * channels] = right.astype(jnp.bfloat16)


def patches(s_ref, first, count):
    width, depth = s_ref.shape[1:]
    return jnp.concatenate(
        [s_ref[first + i - 1 : first + i - 1 + count].reshape(count * width, depth) for i in range(3)], axis=1
    )


def kernel_of(w_ref, layer, times):
    return jnp.concatenate(
        [jnp.concatenate([w_ref[layer, k, t] for t in times], axis=1) for k in range(9)], axis=0
    )


def chunks(first, count):
    step = 5 if count % 5 == 0 else (4 if count % 4 == 0 else (6 if count % 6 == 0 else 2))
    return [(start, step) for start in range(first, first + count, step)]


def history_kernel(flags, own, intra, cross, w, p0, p1, ce, s0, s1, wb, pb, sems):
    layers, _, rows, width, channels = own.shape
    starts = offsets(rows, layers)
    weight_copies = [pltpu.make_async_copy(w.at[l, :, 0:2], wb.at[l], sems.at[l]) for l in range(layers)]
    for copy in weight_copies:
        copy.start()
    own_copy = pltpu.make_async_copy(own, ce.at[:, :, rows : 2 * rows], sems.at[layers])
    own_copy.start()

    def edges(above, below):
        found = []
        at = 0
        for l in range(layers):
            reach = layers - l
            for f in range(2):
                found.append(
                    (above.at[at : at + reach], ce.at[l, f, rows - reach : rows])
                )
                found.append(
                    (below.at[at : at + reach], ce.at[l, f, 2 * rows : 2 * rows + reach])
                )
                at += reach
        return [pltpu.make_async_copy(a, b, sems.at[layers + 1]) for a, b in found]

    @pl.when(flags[2] == 0)
    def _():
        for copy in edges(cross, intra):
            copy.start()
        for copy in edges(cross, intra):
            copy.wait()

    @pl.when(flags[2] != 0)
    def _():
        for copy in edges(intra, cross):
            copy.start()
        for copy in edges(intra, cross):
            copy.wait()

    own_copy.wait()
    for l in range(layers):
        def build(row, _, l=l):
            taps_into(s0, row, ce[l, 0, row].astype(jnp.float32))
            taps_into(s1, row, ce[l, 1, row].astype(jnp.float32))
            return 0

        lax.fori_loop(l + rows - layers, 3 * rows - l - (rows - layers), build, 0)
        weight_copies[l].wait()
        both = kernel_of(wb, l, (1, 0))
        oldest = kernel_of(wb, l, (0,))
        for first, count in chunks(l + 1, out_rows(rows, l)):
            at = starts[l] + first - l - 1
            newer = jnp.dot(patches(s1, first, count), both, preferred_element_type=jnp.float32)
            older = jnp.dot(patches(s0, first, count), oldest, preferred_element_type=jnp.float32)
            pb[0, at : at + count] = (
                (newer[:, :channels] + older).reshape(count, width, channels).astype(jnp.bfloat16)
            )
            pb[1, at : at + count] = newer[:, channels:].reshape(count, width, channels).astype(jnp.bfloat16)
    out0 = pltpu.make_async_copy(pb.at[0], p0, sems.at[0])
    out1 = pltpu.make_async_copy(pb.at[1], p1, sems.at[1])
    out0.start()
    out1.start()
    out0.wait()
    out1.wait()


def frame_kernel(tick, frame, flags, own, intra, cross, w, bias, *refs):
    if frame == 0:
        part, later, done, x_out, later_out, done_out, xe, s, wb, pb, qb, sems = refs
    else:
        part, done, x_out, done_out, xe, s, wb, pb, sems = refs
    rows, width, channels = own.shape
    layers = w.shape[0]
    starts = offsets(rows, layers)
    first_frame = frame == 0
    times = (1, 0) if first_frame else (0,)

    @pl.when(flags[0] == tick)
    def _():
        tap = 1 if first_frame else 2
        weight_copies = [
            pltpu.make_async_copy(w.at[l, :, tap:3], wb.at[l], sems.at[l]) for l in range(layers)
        ]
        own_copy = pltpu.make_async_copy(own, xe.at[rows : 2 * rows], sems.at[layers])
        own_copy.start()

        @pl.when(flags[2] == 0)
        def _():
            pltpu.make_async_copy(cross, xe.at[0:rows], sems.at[layers + 1]).start()
            pltpu.make_async_copy(intra, xe.at[2 * rows : 3 * rows], sems.at[layers + 2]).start()

        @pl.when(flags[2] != 0)
        def _():
            pltpu.make_async_copy(intra, xe.at[0:rows], sems.at[layers + 1]).start()
            pltpu.make_async_copy(cross, xe.at[2 * rows : 3 * rows], sems.at[layers + 2]).start()

        part_copy = pltpu.make_async_copy(part, pb, sems.at[layers + 3])
        weight_copies[0].start()
        part_copy.start()
        for copy in weight_copies[1:]:
            copy.start()
        if first_frame:
            later_copy = pltpu.make_async_copy(later, qb, sems.at[layers + 4])
            later_copy.start()
        own_copy.wait()
        pltpu.make_async_copy(intra, xe.at[0:rows], sems.at[layers + 1]).wait()
        pltpu.make_async_copy(intra, xe.at[2 * rows : 3 * rows], sems.at[layers + 2]).wait()
        low = flags[3]
        high = flags[4]
        for l in range(layers):
            weight_copies[l].wait()
            if l == 0:
                part_copy.wait()
                if first_frame:
                    later_copy.wait()

            @pl.when(l < flags[1])
            def _(l=l):
                def build(row, _):
                    v = xe[row].astype(jnp.float32)
                    inside = jnp.logical_and(row >= low, row < high).astype(jnp.float32)
                    act = v / (1.0 + jnp.exp(-v)) * inside
                    taps_into(s, row, act)
                    return 0

                lax.fori_loop(l, 3 * rows - l, build, 0)
                weights = kernel_of(wb, l, times)
                for first, count in chunks(l + 1, out_rows(rows, l)):
                    at = starts[l] + first - l - 1
                    total = jnp.dot(patches(s, first, count), weights, preferred_element_type=jnp.float32)
                    mine = total[:, :channels].reshape(count, width, channels)
                    x_now = xe[first : first + count].astype(jnp.float32)
                    known = pb[at : at + count].astype(jnp.float32) + bias[l : l + 1, :].reshape(1, 1, channels)
                    xe[first : first + count] = (x_now + (mine + known)).astype(jnp.bfloat16)
                    if first_frame:
                        ahead = total[:, channels:].reshape(count, width, channels)
                        qb[at : at + count] = (qb[at : at + count].astype(jnp.float32) + ahead).astype(jnp.bfloat16)

        result = xe.at[rows : 2 * rows]
        copies = [
            pltpu.make_async_copy(result, x_out, sems.at[0]),
            pltpu.make_async_copy(result, done_out.at[frame], sems.at[1]),
        ]
        if first_frame:
            copies.append(pltpu.make_async_copy(qb, later_out, sems.at[2]))
        for copy in copies:
            copy.start()
        for copy in copies:
            copy.wait()


def any_spec():
    return pl.BlockSpec(memory_space=pl.ANY)


def smem_spec():
    return pl.BlockSpec(memory_space=pltpu.SMEM)


def history_call(flags, caches, intra, cross, weights):
    layers, _, rows, width, channels = caches.shape
    total = offsets(rows, layers)[-1]
    part = jax.ShapeDtypeStruct((total, width, channels), jnp.bfloat16)
    pixels = total * width
    return pl.pallas_call(
        history_kernel,
        out_shape=(part, part),
        in_specs=[smem_spec()] + [any_spec()] * 4,
        out_specs=(any_spec(), any_spec()),
        scratch_shapes=[
            pltpu.VMEM((layers, 2, 3 * rows, width, channels), jnp.bfloat16),
            pltpu.VMEM((3 * rows, width, 3 * channels), jnp.bfloat16),
            pltpu.VMEM((3 * rows, width, 3 * channels), jnp.bfloat16),
            pltpu.VMEM((layers, 9, 2, channels, channels), jnp.bfloat16),
            pltpu.VMEM((2, total, width, channels), jnp.bfloat16),
            pltpu.SemaphoreType.DMA((layers + 2,)),
        ],
        compiler_params=pltpu.CompilerParams(vmem_limit_bytes=LIMIT),
        cost_estimate=pl.CostEstimate(flops=pixels * 27 * 2 * channels * channels, bytes_accessed=8000000, transcendentals=0),
        name="history",
    )(flags, caches, intra, cross, weights)


def frame_call(tick, frame, flags, own, intra, cross, weights, biases, part, done, later=None):
    rows, width, channels = own.shape
    layers = weights.shape[0]
    total = offsets(rows, layers)[-1]
    times = 2 if frame == 0 else 1
    pixels = total * width
    ahead = [later] if frame == 0 else []
    like = [jax.ShapeDtypeStruct(a.shape, jnp.bfloat16) for a in [own] + ahead + [done]]
    kept = [pltpu.VMEM((total, width, channels), jnp.bfloat16) for _ in [part] + ahead]
    return pl.pallas_call(
        functools.partial(frame_kernel, tick, frame),
        out_shape=tuple(like),
        in_specs=[smem_spec()] + [any_spec()] * 4 + [pl.BlockSpec(memory_space=pltpu.VMEM)] + [any_spec()] * len(like),
        out_specs=tuple(any_spec() for _ in like),
        scratch_shapes=[
            pltpu.VMEM((3 * rows, width, channels), jnp.bfloat16),
            pltpu.VMEM((3 * rows, width, 3 * channels), jnp.bfloat16),
            pltpu.VMEM((layers, 9, times, channels, channels), jnp.bfloat16),
            *kept,
            pltpu.SemaphoreType.DMA((layers + 5,)),
        ],
        input_output_aliases={7: 1, 8: 2} if frame == 0 else {7: 1},
        compiler_params=pltpu.CompilerParams(vmem_limit_bytes=LIMIT),
        cost_estimate=pl.CostEstimate(
            flops=pixels * 9 * 2 * times * channels * channels, bytes_accessed=5000000, transcendentals=pixels * channels
        ),
        name="frame0" if frame == 0 else "frame1",
    )(flags, own, intra, cross, weights, biases, part, *ahead, done)


def per_device(clip, caches, weights, biases, section_layers):
    segments = lax.axis_size("segment")
    bands = lax.axis_size("band")
    segment = lax.axis_index("segment")
    band = lax.axis_index("band")
    rows = clip.shape[1]
    layers = weights.shape[1]
    caches, weights, biases = caches[0], weights[0], biases[0]
    parity = band % 2
    flags = jnp.stack(
        [
            segment,
            section_layers[0],
            parity,
            jnp.where(band == 0, rows, 0),
            jnp.where(band == bands - 1, 2 * rows, 3 * rows),
        ]
    ).astype(jnp.int32)
    axes = ("segment", "band")

    def swap(value, pairs, chosen):
        links = []
        for s in chosen:
            for low in pairs:
                links.append((s * bands + low, s * bands + low + 1))
                links.append((s * bands + low + 1, s * bands + low))
        return lax.ppermute(value, axes, links)

    in_chip = range(0, bands - 1, 2)
    between = range(1, bands - 1, 2)

    def both_sides(value, chosen):
        return swap(value, in_chip, chosen), swap(value, between, chosen)

    def shift(value, source):
        return lax.ppermute(
            value, axes, [(source * bands + b, (source + 1) * bands + b) for b in range(bands)]
        )

    def edge(at_end):
        pieces = []
        for l in range(layers):
            reach = layers - l
            start = jnp.where(at_end, rows - reach, 0)
            for f in range(2):
                pieces.append(lax.dynamic_slice_in_dim(caches[l, f], start, reach, 0))
        return jnp.concatenate(pieces, axis=0)

    everyone = range(segments)
    x0, x1 = clip[0], clip[1]
    x0_sides = both_sides(x0, [0])
    history_intra = swap(edge(parity == 0), in_chip, everyone)
    history_cross = swap(edge(parity == 1), between, everyone)
    x1_sides = both_sides(x1, [0])
    p0, p1 = history_call(flags, caches, history_intra, history_cross, weights)
    done = jnp.zeros((2,) + clip.shape[1:], jnp.bfloat16)
    for tick in range(segments):
        x0, p1, done = frame_call(tick, 0, flags, x0, *x0_sides, weights, biases, p0, done, p1)
        if tick + 1 < segments:
            x0 = shift(x0, tick)
            x0_sides = both_sides(x0, [tick + 1])
        x1, done = frame_call(tick, 1, flags, x1, *x1_sides, weights, biases, p1, done)
        if tick + 1 < segments:
            x1 = shift(x1, tick)
            x1_sides = both_sides(x1, [tick + 1])
    return done[None]


def solution(mesh):
    placed = (
        P(None, "band", None, None),
        P("segment", None, None, "band", None, None),
        P("segment", None, None, None, None, None),
        P("segment", None, None),
        P("segment"),
    )
    return jax.shard_map(
        per_device,
        mesh=mesh,
        in_specs=placed,
        out_specs=P("segment", None, "band", None, None),
        check_vma=False,
    )
```

```python
import functools

import jax
import jax.numpy as jnp
from jax import lax
from jax.experimental import pallas as pl
from jax.experimental.pallas import tpu as pltpu
from jax.sharding import PartitionSpec as P

LIMIT = 24 * 1024 * 1024
F32 = jnp.float32
BF16 = jnp.bfloat16


def message_starts(layers):
    starts = [0]
    for level in range(layers):
        starts.append(starts[-1] + layers - level)
    return starts


def taps_into(s_ref, row, a):
    width, channels = a.shape
    column = lax.broadcasted_iota(jnp.int32, a.shape, 0)
    left = jnp.where(column == 0, 0.0, pltpu.roll(a, 1, 0))
    right = jnp.where(column == width - 1, 0.0, pltpu.roll(a, width - 1, 0))
    s_ref[row, :, 0:channels] = left.astype(BF16)
    s_ref[row, :, channels : 2 * channels] = a.astype(BF16)
    s_ref[row, :, 2 * channels : 3 * channels] = right.astype(BF16)


def patches(s_ref, first):
    width, depth = s_ref.shape[1:]
    return jnp.concatenate([s_ref[pl.ds(first + i, 2)].reshape(2 * width, depth) for i in range(3)], axis=1)


def kernel_of(w, layer, times):
    return jnp.concatenate([jnp.concatenate([w[layer, k, t] for t in times], axis=1) for k in range(9)], axis=0)


def history_kernel(flags, clip, caches, w, sums0, sums1, in0, cross0, in1, cross1, done, s0, s1):
    layers, _, rows, width, channels = caches.shape
    begin = layers - flags[2]
    for s in (s0, s1):
        s[0:2] = jnp.zeros((2,) + s.shape[1:], BF16)
        s[rows + 2 : rows + 4] = jnp.zeros((2,) + s.shape[1:], BF16)

    def level_step(level, _):
        layer = level - begin

        def build(row, _):
            taps_into(s0, row + 2, caches[layer, 0, row].astype(F32))
            taps_into(s1, row + 2, caches[layer, 1, row].astype(F32))
            return 0

        lax.fori_loop(0, rows, build, 0)

        def chunk(c, _):
            at = 2 * c
            newer = jnp.dot(patches(s1, at), kernel_of(w, layer, (1, 0)), preferred_element_type=F32)
            older = jnp.dot(patches(s0, at), kernel_of(w, layer, (0,)), preferred_element_type=F32)
            sums0[level, pl.ds(at, 2)] = (newer[:, :channels] + older).reshape(2, width, channels).astype(BF16)
            sums1[level, pl.ds(at, 2)] = newer[:, channels:].reshape(2, width, channels).astype(BF16)
            return 0

        lax.fori_loop(0, (rows + 2) // 2, chunk, 0)
        return 0

    lax.fori_loop(begin, layers, level_step, 0)
    starts = message_starts(layers)

    def messages(up0, up1, down0, down1):
        for frame, sums, up, down in ((0, sums0, up0, down0), (1, sums1, up1, down1)):
            for level in range(layers):
                reach = layers - level
                up[starts[level] : starts[level + 1]] = sums[level, 0:reach]
                down[starts[level] : starts[level + 1]] = sums[level, rows + 2 - reach : rows + 2]
            for message in (up, down):
                message[starts[-1] : starts[-1] + rows] = clip[frame]

    @pl.when(flags[1] % 2 == 0)
    def _():
        messages(cross0, cross1, in0, in1)

    @pl.when(flags[1] % 2 != 0)
    def _():
        messages(in0, in1, cross0, cross1)


def frame_kernel(tick, frame, bands, flags, own, inner, cross, w, bias, sums, sums_in, sums_cross, *refs):
    if frame == 0:
        done, x_out, ahead, done_out, x, s, part, sem = refs
    else:
        behind, done, x_out, done_out, x, s, part, sem = refs
    rows, width, channels = x_out.shape
    layers = w.shape[0]
    starts = message_starts(layers)
    times = (2, 1) if frame == 0 else (2,)

    @pl.when(flags[0] == tick)
    def _():
        band = flags[1]
        begin = layers - flags[2]
        low = jnp.where(band == 0, rows, 0)
        high = jnp.where(band == bands - 1, 2 * rows, 3 * rows)
        halo = starts[-1] if tick == 0 else 0
        x[rows : 2 * rows] = own[frame] if tick == 0 else own[...]

        def gather(above, below, sums_above, sums_below):
            x[0:rows] = above[halo : halo + rows]
            x[2 * rows : 3 * rows] = below[halo : halo + rows]
            for level in range(layers):

                @pl.when(level >= begin)
                def _(level=level):
                    reach = layers - level
                    part[level, rows + 1 - reach : rows + 1] = sums_above[starts[level] : starts[level + 1]]
                    part[level, 2 * rows - 1 : 2 * rows - 1 + reach] = sums_below[starts[level] : starts[level + 1]]
                    part[level, rows + 1 : 2 * rows - 1] = sums[level, 2:rows]
                    part[level, rows] += sums[level, 1]
                    part[level, 2 * rows - 1] += sums[level, rows]
                    if reach > 1:
                        part[level, rows - 1] += sums[level, 0]
                        part[level, 2 * rows] += sums[level, rows + 1]

        @pl.when(band % 2 == 0)
        def _():
            gather(cross, inner, sums_cross, sums_in)

        @pl.when(band % 2 != 0)
        def _():
            gather(inner, cross, sums_in, sums_cross)

        def build(row):
            half = x[row].astype(F32) * 0.5
            inside = jnp.logical_and(row >= low, row < high).astype(F32)
            taps_into(s, row, (half + half * jnp.tanh(half)) * inside)

        def level_step(level, _):
            layer = level - begin
            first = rows - layers + 1 + level

            def early(i, _):
                build(first - 1 + i)
                return 0

            lax.fori_loop(0, 4, early, 0)
            offset = bias[pl.ds(layer, 1), :].reshape(1, 1, channels)

            def chunk(c, _):
                at = first + 2 * c
                total = jnp.dot(patches(s, at - 1), kernel_of(w, layer, times), preferred_element_type=F32)
                build(at + 3)
                build(at + 4)
                mine = total[:, :channels].reshape(2, width, channels)
                known = part[level, pl.ds(at, 2)].astype(F32) + offset
                if frame == 0:
                    ahead[level, pl.ds(at, 2)] = total[:, channels:].reshape(2, width, channels).astype(BF16)
                else:
                    known = known + behind[level, pl.ds(at, 2)].astype(F32)
                x[pl.ds(at, 2)] = (x[pl.ds(at, 2)].astype(F32) + (mine + known)).astype(BF16)
                return 0

            lax.fori_loop(0, rows // 2 + layers - 1 - level, chunk, 0)
            return 0

        lax.fori_loop(begin, layers, level_step, 0)
        x_out[...] = x[rows : 2 * rows]
        copy = pltpu.make_async_copy(x.at[rows : 2 * rows], done_out.at[frame], sem)
        copy.start()
        copy.wait()


def in_vmem(count):
    return [pl.BlockSpec(memory_space=pltpu.VMEM)] * count


def anywhere():
    return pl.BlockSpec(memory_space=pl.ANY)


def in_smem():
    return pl.BlockSpec(memory_space=pltpu.SMEM)


def history_call(flags, clip, caches, weights):
    layers, _, rows, width, channels = caches.shape
    sums = jax.ShapeDtypeStruct((layers, rows + 2, width, channels), BF16)
    message = jax.ShapeDtypeStruct((message_starts(layers)[-1] + rows, width, channels), BF16)
    pixels = layers * (rows + 2) * width
    return pl.pallas_call(
        history_kernel,
        out_shape=(sums, sums, message, message, message, message, jax.ShapeDtypeStruct(clip.shape, BF16)),
        in_specs=[in_smem()] + in_vmem(3),
        out_specs=tuple(in_vmem(6) + [anywhere()]),
        scratch_shapes=[pltpu.VMEM((rows + 4, width, 3 * channels), BF16)] * 2,
        compiler_params=pltpu.CompilerParams(vmem_limit_bytes=LIMIT),
        cost_estimate=pl.CostEstimate(
            flops=pixels * 27 * 2 * channels * channels, bytes_accessed=8000000, transcendentals=0
        ),
        name="history",
    )(flags, clip, caches, weights)


def frame_call(tick, frame, bands, flags, own, inner, cross, weights, biases, sums, sums_in, sums_cross, done, behind=None):
    layers, _, _, channels, _ = weights.shape
    rows, width = done.shape[1:3]
    every = (layers, 3 * rows, width, channels)
    pixels = sum(rows + 2 * level for level in range(layers)) * width
    x_out = jax.ShapeDtypeStruct((rows, width, channels), BF16)
    ahead = jax.ShapeDtypeStruct(every, BF16)
    done_out = jax.ShapeDtypeStruct(done.shape, BF16)
    extra = [] if frame == 0 else [behind]
    return pl.pallas_call(
        functools.partial(frame_kernel, tick, frame, bands),
        out_shape=(x_out, ahead, done_out) if frame == 0 else (x_out, done_out),
        in_specs=[in_smem()] + in_vmem(8 + len(extra)) + [anywhere()],
        out_specs=tuple(in_vmem(2 - frame) + [anywhere()]),
        scratch_shapes=[
            pltpu.VMEM((3 * rows + 2, width, channels), BF16),
            pltpu.VMEM((3 * rows + 2, width, 3 * channels), BF16),
            pltpu.VMEM(every, BF16),
            pltpu.SemaphoreType.DMA,
        ],
        input_output_aliases={9: 2} if frame == 0 else {10: 1},
        compiler_params=pltpu.CompilerParams(vmem_limit_bytes=LIMIT),
        cost_estimate=pl.CostEstimate(
            flops=pixels * 9 * 2 * (2 - frame) * channels * channels, bytes_accessed=5000000, transcendentals=pixels * channels
        ),
        name="frame0" if frame == 0 else "frame1",
    )(flags, own, inner, cross, weights, biases, sums, sums_in, sums_cross, *extra, done)


def per_device(clip, caches, weights, biases, section_layers):
    segments = lax.axis_size("segment")
    bands = lax.axis_size("band")
    caches, weights, biases = caches[0], weights[0], biases[0]
    flags = jnp.stack([lax.axis_index("segment"), lax.axis_index("band"), section_layers[0]]).astype(jnp.int32)
    axes = ("segment", "band")
    in_chip = [(b, b ^ 1) for b in range(bands)]
    between = [(b, b + 1) for b in range(1, bands - 1, 2)] + [(b + 1, b) for b in range(1, bands - 1, 2)]
    straight = [(b, b) for b in range(bands)]

    def swap(value, pairs, chosen):
        return lax.ppermute(value, axes, [(s * bands + a, s * bands + b) for s in chosen for a, b in pairs])

    def ahead(value, pairs, source):
        return lax.ppermute(value, axes, [(source * bands + a, (source + 1) * bands + b) for a, b in pairs])

    everyone = range(segments)
    sums0, sums1, in0, cross0, in1, cross1, done = history_call(flags, clip, caches, weights)
    cross0 = swap(cross0, between, everyone)
    in0 = swap(in0, in_chip, everyone)
    cross1 = swap(cross1, between, everyone)
    in1 = swap(in1, in_chip, everyone)
    first = (clip, in0, cross0)
    second = (clip, in1, cross1)
    for tick in range(segments):
        x0, behind, done = frame_call(tick, 0, bands, flags, *first, weights, biases, sums0, in0, cross0, done)
        if tick > 0:
            own1, x0, behind = lax.optimization_barrier((own1, x0, behind))
            second = (own1, swap(own1, in_chip, [tick]), diagonal1)
        if tick + 1 < segments:
            own0, diagonal0 = ahead(x0, straight, tick), ahead(x0, between, tick)
            first = (own0, swap(own0, in_chip, [tick + 1]), diagonal0)
        x1, done = frame_call(tick, 1, bands, flags, *second, weights, biases, sums1, in1, cross1, done, behind)
        if tick + 1 < segments:
            own1, diagonal1 = ahead(x1, straight, tick), ahead(x1, between, tick)
    return done[None]


def solution(mesh):
    placed = (
        P(None, "band", None, None),
        P("segment", None, None, "band", None, None),
        P("segment", None, None, None, None, None),
        P("segment", None, None),
        P("segment"),
    )
    return jax.shard_map(
        per_device,
        mesh=mesh,
        in_specs=placed,
        out_specs=P("segment", None, "band", None, None),
        check_vma=False,
    )
```

```python
import functools

import jax
import jax.numpy as jnp
from jax import lax
from jax.experimental import pallas as pl
from jax.experimental.pallas import tpu as pltpu
from jax.sharding import PartitionSpec as P

LIMIT = 24 * 1024 * 1024
F32 = jnp.float32
BF16 = jnp.bfloat16


def message_starts(layers):
    starts = [0]
    for level in range(layers):
        starts.append(starts[-1] + layers - level)
    return starts


def taps_into(s_ref, row, a):
    width, channels = a.shape
    tile = 16
    place = lax.broadcasted_iota(jnp.int32, (tile, channels), 0)
    left = pltpu.roll(a, 1, 0)
    right = pltpu.roll(a, width - 1, 0)
    s_ref[row, 0:tile, 0:channels] = jnp.where(place == 0, 0.0, left[:tile]).astype(BF16)
    s_ref[row, tile:, 0:channels] = left[tile:].astype(BF16)
    s_ref[row, :, channels : 2 * channels] = a.astype(BF16)
    s_ref[row, : width - tile, 2 * channels : 3 * channels] = right[: width - tile].astype(BF16)
    s_ref[row, width - tile :, 2 * channels : 3 * channels] = jnp.where(
        place == tile - 1, 0.0, right[width - tile :]
    ).astype(BF16)


def rows_dot(s_ref, first, count, w, layer, times):
    width, depth = s_ref.shape[1:]
    taps = jnp.concatenate([s_ref[pl.ds(first + i, count)].reshape(count * width, depth) for i in range(3)], axis=1)
    weights = jnp.concatenate([jnp.concatenate([w[layer, k, t] for t in times], axis=1) for k in range(9)], axis=0)
    return jnp.dot(taps, weights, preferred_element_type=F32)


def pairs_dot(s_ref, first, count, w, layer, time):
    width, depth = s_ref.shape[1:]
    channels = depth // 3
    taps = jnp.concatenate(
        [jnp.concatenate([s_ref[first + i + 2 * p] for p in range(count)], axis=0) for i in range(4)], axis=1
    )
    zero = jnp.zeros((channels, channels), BF16)

    def tap(i, j):
        return w[layer, 3 * i + j, time] if 0 <= i < 3 else zero

    weights = jnp.concatenate(
        [jnp.concatenate([tap(i, j), tap(i - 1, j)], axis=1) for i in range(4) for j in range(3)], axis=0
    )
    total = jnp.dot(taps, weights, preferred_element_type=F32)
    upper = total[:, :channels].reshape(count, 1, width, channels)
    lower = total[:, channels:].reshape(count, 1, width, channels)
    return jnp.concatenate([upper, lower], axis=1)


def history_kernel(flags, clip, caches, w, sums0, sums1, in0, cross0, in1, cross1, done, s0, s1):
    layers, _, rows, width, channels = caches.shape
    begin = layers - flags[2]
    for s in (s0, s1):
        s[0:2] = jnp.zeros((2,) + s.shape[1:], BF16)
        s[rows + 2 : rows + 4] = jnp.zeros((2,) + s.shape[1:], BF16)

    def level_step(level, _):
        layer = level - begin

        def build(row, _):
            taps_into(s0, row + 2, caches[layer, 0, row].astype(F32))
            taps_into(s1, row + 2, caches[layer, 1, row].astype(F32))
            return 0

        lax.fori_loop(0, rows, build, 0)
        newer = rows_dot(s1, 0, rows + 2, w, layer, (1, 0))
        older = pairs_dot(s0, 0, (rows + 2) // 2, w, layer, 0).reshape(rows + 2, width, channels)
        sums0[level] = (newer[:, :channels].reshape(rows + 2, width, channels) + older).astype(BF16)
        sums1[level] = newer[:, channels:].reshape(rows + 2, width, channels).astype(BF16)
        return 0

    lax.fori_loop(begin, layers, level_step, 0)
    starts = message_starts(layers)

    def messages(up0, up1, down0, down1):
        for frame, sums, up, down in ((0, sums0, up0, down0), (1, sums1, up1, down1)):
            for level in range(layers):
                reach = layers - level
                up[starts[level] : starts[level + 1]] = sums[level, 0:reach]
                down[starts[level] : starts[level + 1]] = sums[level, rows + 2 - reach : rows + 2]
            for message in (up, down):
                message[starts[-1] : starts[-1] + rows] = clip[frame]

    @pl.when(flags[1] % 2 == 0)
    def _():
        messages(cross0, cross1, in0, in1)

    @pl.when(flags[1] % 2 != 0)
    def _():
        messages(in0, in1, cross0, cross1)


def pieces(count):
    parts, at = [], 0
    while at < count:
        step = 4 if count - at in (4, 8) else min(6, count - at)
        parts.append((at, step))
        at += step
    return parts


def frame_kernel(tick, frame, bands, flags, own, inner, cross, w, bias, sums, sums_in, sums_cross, *refs):
    if frame == 0:
        done, x_out, ahead, done_out, x, s, part, sem = refs
    else:
        behind, done, x_out, done_out, x, s, part, sem = refs
    rows, width, channels = x_out.shape
    layers = w.shape[0]
    starts = message_starts(layers)

    @pl.when(flags[0] == tick)
    def _():
        band = flags[1]
        begin = layers - flags[2]
        low = jnp.where(band == 0, rows, 0)
        high = jnp.where(band == bands - 1, 2 * rows, 3 * rows)

        halo = starts[-1] if tick == 0 else 0
        x[rows : 2 * rows] = own[frame] if tick == 0 else own[...]

        def gather(above, below, sums_above, sums_below):
            x[0:rows] = above[halo : halo + rows]
            x[2 * rows : 3 * rows] = below[halo : halo + rows]
            for level in range(layers):

                @pl.when(level >= begin)
                def _(level=level):
                    reach = layers - level
                    part[level, rows + 1 - reach : rows + 1] = sums_above[starts[level] : starts[level + 1]]
                    part[level, 2 * rows - 1 : 2 * rows - 1 + reach] = sums_below[starts[level] : starts[level + 1]]
                    part[level, rows + 1 : 2 * rows - 1] = sums[level, 2:rows]
                    part[level, rows] += sums[level, 1]
                    part[level, 2 * rows - 1] += sums[level, rows]
                    if reach > 1:
                        part[level, rows - 1] += sums[level, 0]
                        part[level, 2 * rows] += sums[level, rows + 1]

        @pl.when(band % 2 == 0)
        def _():
            gather(cross, inner, sums_cross, sums_in)

        @pl.when(band % 2 != 0)
        def _():
            gather(inner, cross, sums_in, sums_cross)

        def build(row):
            half = x[row].astype(F32) * 0.5
            inside = jnp.logical_and(row >= low, row < high).astype(F32)
            taps_into(s, row, (half + half * jnp.tanh(half)) * inside)

        for level in range(layers):

            @pl.when(level >= begin)
            def _(level=level):
                layer = level - begin
                first = rows - layers + 1 + level
                count = rows + 2 * (layers - 1 - level)

                def two(i, _):
                    build(first - 1 + 2 * i)
                    build(first + 2 * i)
                    return 0

                lax.fori_loop(0, count // 2 + 1, two, 0)
                offset = bias[pl.ds(layer, 1), :].reshape(1, 1, channels)
                for start, step in pieces(count):
                    at = first + start
                    known = part[level, at : at + step].astype(F32) + offset
                    if frame == 0:
                        total = rows_dot(s, at - 1, step, w, layer, (2, 1))
                        mine = total[:, :channels].reshape(step, width, channels)
                        ahead[level, at : at + step] = total[:, channels:].reshape(step, width, channels).astype(BF16)
                    else:
                        mine = pairs_dot(s, at - 1, step // 2, w, layer, 2).reshape(step, width, channels)
                        known = known + behind[level, at : at + step].astype(F32)
                    x[at : at + step] = (x[at : at + step].astype(F32) + (mine + known)).astype(BF16)

        x_out[...] = x[rows : 2 * rows]
        copy = pltpu.make_async_copy(x.at[rows : 2 * rows], done_out.at[frame], sem)
        copy.start()
        copy.wait()


def in_vmem(count):
    return [pl.BlockSpec(memory_space=pltpu.VMEM)] * count


def anywhere():
    return pl.BlockSpec(memory_space=pl.ANY)


def in_smem():
    return pl.BlockSpec(memory_space=pltpu.SMEM)


def history_call(flags, clip, caches, weights):
    layers, _, rows, width, channels = caches.shape
    sums = jax.ShapeDtypeStruct((layers, rows + 2, width, channels), BF16)
    message = jax.ShapeDtypeStruct((message_starts(layers)[-1] + rows, width, channels), BF16)
    pixels = layers * (rows + 2) * width
    return pl.pallas_call(
        history_kernel,
        out_shape=(sums, sums, message, message, message, message, jax.ShapeDtypeStruct(clip.shape, BF16)),
        in_specs=[in_smem()] + in_vmem(3),
        out_specs=tuple(in_vmem(6) + [anywhere()]),
        scratch_shapes=[pltpu.VMEM((rows + 4, width, 3 * channels), BF16)] * 2,
        compiler_params=pltpu.CompilerParams(vmem_limit_bytes=LIMIT),
        cost_estimate=pl.CostEstimate(
            flops=pixels * 27 * 2 * channels * channels, bytes_accessed=8000000, transcendentals=0
        ),
        name="history",
    )(flags, clip, caches, weights)


def frame_call(tick, frame, bands, flags, own, inner, cross, weights, biases, sums, sums_in, sums_cross, done, behind=None):
    layers, _, _, channels, _ = weights.shape
    rows, width = done.shape[1:3]
    every = (layers, 3 * rows, width, channels)
    pixels = sum(rows + 2 * level for level in range(layers)) * width
    x_out = jax.ShapeDtypeStruct((rows, width, channels), BF16)
    ahead = jax.ShapeDtypeStruct(every, BF16)
    done_out = jax.ShapeDtypeStruct(done.shape, BF16)
    extra = [] if frame == 0 else [behind]
    return pl.pallas_call(
        functools.partial(frame_kernel, tick, frame, bands),
        out_shape=(x_out, ahead, done_out) if frame == 0 else (x_out, done_out),
        in_specs=[in_smem()] + in_vmem(8 + len(extra)) + [anywhere()],
        out_specs=tuple(in_vmem(2 - frame) + [anywhere()]),
        scratch_shapes=[
            pltpu.VMEM((3 * rows + 2, width, channels), BF16),
            pltpu.VMEM((3 * rows + 2, width, 3 * channels), BF16),
            pltpu.VMEM(every, BF16),
            pltpu.SemaphoreType.DMA,
        ],
        input_output_aliases={9: 2} if frame == 0 else {10: 1},
        compiler_params=pltpu.CompilerParams(vmem_limit_bytes=LIMIT),
        cost_estimate=pl.CostEstimate(
            flops=pixels * 9 * 2 * (2 - frame) * channels * channels, bytes_accessed=5000000, transcendentals=pixels * channels
        ),
        name="frame0" if frame == 0 else "frame1",
    )(flags, own, inner, cross, weights, biases, sums, sums_in, sums_cross, *extra, done)


def per_device(clip, caches, weights, biases, section_layers):
    segments = lax.axis_size("segment")
    bands = lax.axis_size("band")
    caches, weights, biases = caches[0], weights[0], biases[0]
    flags = jnp.stack([lax.axis_index("segment"), lax.axis_index("band"), section_layers[0]]).astype(jnp.int32)
    axes = ("segment", "band")
    in_chip = [(b, b ^ 1) for b in range(bands)]
    between = [(b, b + 1) for b in range(1, bands - 1, 2)] + [(b + 1, b) for b in range(1, bands - 1, 2)]
    straight = [(b, b) for b in range(bands)]

    def swap(value, pairs, chosen):
        return lax.ppermute(value, axes, [(s * bands + a, s * bands + b) for s in chosen for a, b in pairs])

    def ahead(value, pairs, source):
        return lax.ppermute(value, axes, [(source * bands + a, (source + 1) * bands + b) for a, b in pairs])

    everyone = range(segments)
    sums0, sums1, in0, cross0, in1, cross1, done = history_call(flags, clip, caches, weights)
    cross0 = swap(cross0, between, everyone)
    in0 = swap(in0, in_chip, everyone)
    cross1 = swap(cross1, between, everyone)
    in1 = swap(in1, in_chip, everyone)
    first = (clip, in0, cross0)
    second = (clip, in1, cross1)
    for tick in range(segments):
        x0, behind, done = frame_call(tick, 0, bands, flags, *first, weights, biases, sums0, in0, cross0, done)
        if tick + 1 < segments:
            own0, diagonal0 = ahead(x0, straight, tick), ahead(x0, between, tick)
        if tick > 0:
            before = (x0, own0) if tick + 1 < segments else (x0,)
            own1, diagonal1, behind, x0, *before = lax.optimization_barrier((own1, diagonal1, behind) + before)
            if tick + 1 < segments:
                (own0,) = before
        if tick + 1 < segments:
            inner0 = swap(own0, in_chip, [tick + 1])
            first = (own0, inner0, diagonal0)
        if tick > 0:
            if tick + 1 < segments:
                own1, _, _ = lax.optimization_barrier((own1, inner0, diagonal0))
            second = (own1, swap(own1, in_chip, [tick]), diagonal1)
        x1, done = frame_call(tick, 1, bands, flags, *second, weights, biases, sums1, in1, cross1, done, behind)
        if tick + 1 < segments:
            own1, diagonal1 = ahead(x1, straight, tick), ahead(x1, between, tick)
    return done[None]


def solution(mesh):
    placed = (
        P(None, "band", None, None),
        P("segment", None, None, "band", None, None),
        P("segment", None, None, None, None, None),
        P("segment", None, None),
        P("segment"),
    )
    return jax.shard_map(
        per_device,
        mesh=mesh,
        in_specs=placed,
        out_specs=P("segment", None, "band", None, None),
        check_vma=False,
    )
```

```python
import functools

import jax
import jax.numpy as jnp
from jax import lax
from jax.experimental import pallas as pl
from jax.experimental.pallas import tpu as pltpu
from jax.sharding import PartitionSpec as P

LIMIT = 24 * 1024 * 1024
F32 = jnp.float32
BF16 = jnp.bfloat16


def message_starts(layers, first=0, last=None):
    starts = [0]
    for level in range(first, layers if last is None else last):
        starts.append(starts[-1] + layers - level)
    return starts


def taps_into(s_ref, row, a):
    width, channels = a.shape
    tile = 16
    place = lax.broadcasted_iota(jnp.int32, (tile, channels), 0)
    left = pltpu.roll(a, 1, 0)
    right = pltpu.roll(a, width - 1, 0)
    s_ref[row, 0:tile, 0:channels] = jnp.where(place == 0, 0.0, left[:tile]).astype(BF16)
    s_ref[row, tile:, 0:channels] = left[tile:].astype(BF16)
    s_ref[row, :, channels : 2 * channels] = a.astype(BF16)
    s_ref[row, : width - tile, 2 * channels : 3 * channels] = right[: width - tile].astype(BF16)
    s_ref[row, width - tile :, 2 * channels : 3 * channels] = jnp.where(
        place == tile - 1, 0.0, right[width - tile :]
    ).astype(BF16)


def rows_dot(s_ref, first, count, w, layer, times):
    width, depth = s_ref.shape[1:]
    taps = jnp.concatenate([s_ref[pl.ds(first + i, count)].reshape(count * width, depth) for i in range(3)], axis=1)
    weights = jnp.concatenate([jnp.concatenate([w[layer, k, t] for t in times], axis=1) for k in range(9)], axis=0)
    return jnp.dot(taps, weights, preferred_element_type=F32)


def pairs_dot(s_ref, first, count, w, layer, time):
    width, depth = s_ref.shape[1:]
    channels = depth // 3
    taps = jnp.concatenate(
        [jnp.concatenate([s_ref[first + i + 2 * p] for p in range(count)], axis=0) for i in range(4)], axis=1
    )
    zero = jnp.zeros((channels, channels), BF16)

    def tap(i, j):
        return w[layer, 3 * i + j, time] if 0 <= i < 3 else zero

    weights = jnp.concatenate(
        [jnp.concatenate([tap(i, j), tap(i - 1, j)], axis=1) for i in range(4) for j in range(3)], axis=0
    )
    total = jnp.dot(taps, weights, preferred_element_type=F32)
    upper = total[:, :channels].reshape(count, 1, width, channels)
    lower = total[:, channels:].reshape(count, 1, width, channels)
    return jnp.concatenate([upper, lower], axis=1)


def history_kernel(first, last, flags, caches, w, *refs):
    layers, _, rows, width, channels = caches.shape
    if last < layers:
        sums0, sums1, in0, cross0, done, s0, s1 = refs
    else:
        clip, former, sums0, sums1, in0, cross0, in1, cross1, s0, s1 = refs
    begin = layers - flags[2]
    for s in (s0, s1):
        s[0:2] = jnp.zeros((2,) + s.shape[1:], BF16)
        s[rows + 2 : rows + 4] = jnp.zeros((2,) + s.shape[1:], BF16)

    def level_step(level, _):
        layer = level - begin

        def build(row, _):
            taps_into(s0, row + 2, caches[layer, 0, row].astype(F32))
            taps_into(s1, row + 2, caches[layer, 1, row].astype(F32))
            return 0

        lax.fori_loop(0, rows, build, 0)
        newer = rows_dot(s1, 0, rows + 2, w, layer, (1, 0))
        older = pairs_dot(s0, 0, (rows + 2) // 2, w, layer, 0).reshape(rows + 2, width, channels)
        sums0[level - first] = (newer[:, :channels].reshape(rows + 2, width, channels) + older).astype(BF16)
        sums1[level - first] = newer[:, channels:].reshape(rows + 2, width, channels).astype(BF16)
        return 0

    lax.fori_loop(jnp.maximum(begin, first), last, level_step, 0)

    def pack(of_level, starts, levels, up, down):
        for i, level in enumerate(levels):
            reach = layers - level
            sums, at = of_level(level)
            up[starts[i] : starts[i + 1]] = sums[at, 0:reach]
            down[starts[i] : starts[i + 1]] = sums[at, rows + 2 - reach : rows + 2]

    def messages(up0, down0, up1, down1):
        pack(lambda level: (sums0, level - first), message_starts(layers, first, last), range(first, last), up0, down0)
        if last == layers:
            starts = message_starts(layers)
            pack(
                lambda level: (former, level) if level < first else (sums1, level - first),
                starts, range(layers), up1, down1,
            )
            for message in (up1, down1):
                message[starts[-1] : starts[-1] + rows] = clip[1]

    @pl.when(flags[1] % 2 == 0)
    def _():
        if last == layers:
            messages(cross0, in0, cross1, in1)
        else:
            messages(cross0, in0, None, None)

    @pl.when(flags[1] % 2 != 0)
    def _():
        if last == layers:
            messages(in0, cross0, in1, cross1)
        else:
            messages(in0, cross0, None, None)


def pieces(count):
    parts, at = [], 0
    while at < count:
        step = 4 if count - at in (4, 8) else min(6, count - at)
        parts.append((at, step))
        at += step
    return parts


def tick_kernel(tick, segments, bands, cut, flags, clip, own, inner, cross, w, bias, *refs):
    zero, one = tick < segments, tick > 0
    refs = list(refs)

    def take(count):
        found, refs[:count] = refs[:count], []
        return found

    sums0 = take(6) if zero else None
    sums1 = take(4) if one else None
    behind = take(1)[0] if one else None
    done = take(1)
    x_out = take(1)[0]
    ahead = take(1)[0] if zero else None
    done_out, x, s, part, sem = refs
    rows, width, channels = x_out.shape
    layers = w.shape[0]
    band = flags[1]
    begin = layers - flags[2]
    low = jnp.where(band == 0, rows, 0)
    high = jnp.where(band == bands - 1, 2 * rows, 3 * rows)

    def run(frame, fresh, own, inner, cross, halo, level_sums, level_messages):
        x[rows : 2 * rows] = own[frame] if fresh else own[...]

        def gather(above, below, side_above, side_below):
            x[0:rows] = above[halo : halo + rows]
            x[2 * rows : 3 * rows] = below[halo : halo + rows]
            for level in range(layers):

                @pl.when(level >= begin)
                def _(level=level):
                    reach = layers - level
                    sums, at = level_sums(level)
                    start, sums_above, sums_below = level_messages(level, side_above, side_below)
                    part[level, rows + 1 - reach : rows + 1] = sums_above[start : start + reach]
                    part[level, 2 * rows - 1 : 2 * rows - 1 + reach] = sums_below[start : start + reach]
                    part[level, rows + 1 : 2 * rows - 1] = sums[at, 2:rows]
                    part[level, rows] += sums[at, 1]
                    part[level, 2 * rows - 1] += sums[at, rows]
                    if reach > 1:
                        part[level, rows - 1] += sums[at, 0]
                        part[level, 2 * rows] += sums[at, rows + 1]

        @pl.when(band % 2 == 0)
        def _():
            gather(cross, inner, 1, 0)

        @pl.when(band % 2 != 0)
        def _():
            gather(inner, cross, 0, 1)

        def build(row):
            half = x[row].astype(F32) * 0.5
            inside = jnp.logical_and(row >= low, row < high).astype(F32)
            taps_into(s, row, (half + half * jnp.tanh(half)) * inside)

        for level in range(layers):

            @pl.when(level >= begin)
            def _(level=level):
                layer = level - begin
                first = rows - layers + 1 + level
                count = rows + 2 * (layers - 1 - level)

                def two(i, _):
                    build(first - 1 + 2 * i)
                    build(first + 2 * i)
                    return 0

                lax.fori_loop(0, count // 2 + 1, two, 0)
                offset = bias[pl.ds(layer, 1), :].reshape(1, 1, channels)
                for start, step in pieces(count):
                    at = first + start
                    known = part[level, at : at + step].astype(F32) + offset
                    if frame == 0:
                        total = rows_dot(s, at - 1, step, w, layer, (2, 1))
                        mine = total[:, :channels].reshape(step, width, channels)
                        ahead[level, at : at + step] = total[:, channels:].reshape(step, width, channels).astype(BF16)
                    else:
                        mine = pairs_dot(s, at - 1, step // 2, w, layer, 2).reshape(step, width, channels)
                        known = known + behind[level, at : at + step].astype(F32)
                    x[at : at + step] = (x[at : at + step].astype(F32) + (mine + known)).astype(BF16)

        copy = pltpu.make_async_copy(x.at[rows : 2 * rows], done_out.at[frame], sem)
        copy.start()
        x_out[...] = x[rows : 2 * rows]
        copy.wait()

    if zero:
        sums_a, sums_b, in_a, cross_a, in_b, cross_b = sums0
        starts_a, starts_b = message_starts(layers, 0, cut), message_starts(layers, cut)

        def messages0(level, above, below):
            if level < cut:
                return starts_a[level], (in_a, cross_a)[above], (in_a, cross_a)[below]
            return starts_b[level - cut], (in_b, cross_b)[above], (in_b, cross_b)[below]

        @pl.when(flags[0] == tick)
        def _():
            run(
                0, tick == 0, clip if tick == 0 else own, inner, cross, 0,
                lambda level: (sums_a, level) if level < cut else (sums_b, level - cut), messages0,
            )

    if one:
        sums_c, sums_d, in1, cross1 = sums1
        starts = message_starts(layers)

        def messages1(level, above, below):
            return starts[level], (in1, cross1)[above], (in1, cross1)[below]

        @pl.when(flags[0] == tick - 1)
        def _():
            fresh = tick == 1
            run(
                1, fresh, clip if fresh else own, in1 if fresh else inner, cross1 if fresh else cross,
                starts[-1] if fresh else 0,
                lambda level: (sums_c, level) if level < cut else (sums_d, level - cut), messages1,
            )


def in_vmem(count):
    return [pl.BlockSpec(memory_space=pltpu.VMEM)] * count


def anywhere():
    return pl.BlockSpec(memory_space=pl.ANY)


def in_smem():
    return pl.BlockSpec(memory_space=pltpu.SMEM)


def history_call(first, last, flags, caches, weights, *more):
    layers, _, rows, width, channels = caches.shape
    sums = jax.ShapeDtypeStruct((last - first, rows + 2, width, channels), BF16)
    message = jax.ShapeDtypeStruct((message_starts(layers, first, last)[-1], width, channels), BF16)
    outs = [sums, sums, message, message]
    specs = in_vmem(4)
    if last < layers:
        outs.append(jax.ShapeDtypeStruct((2, rows, width, channels), BF16))
        specs.append(anywhere())
    else:
        outs += [jax.ShapeDtypeStruct((message_starts(layers)[-1] + rows, width, channels), BF16)] * 2
        specs += in_vmem(2)
    pixels = (last - first) * (rows + 2) * width
    return pl.pallas_call(
        functools.partial(history_kernel, first, last),
        out_shape=tuple(outs),
        in_specs=[in_smem()] + in_vmem(2 + len(more)),
        out_specs=tuple(specs),
        scratch_shapes=[pltpu.VMEM((rows + 4, width, 3 * channels), BF16)] * 2,
        compiler_params=pltpu.CompilerParams(vmem_limit_bytes=LIMIT),
        cost_estimate=pl.CostEstimate(
            flops=pixels * 27 * 2 * channels * channels, bytes_accessed=4000000, transcendentals=0
        ),
        name="history",
    )(flags, caches, weights, *more)


def tick_call(tick, segments, bands, cut, flags, clip, own, inner, cross, weights, biases, sums0, sums1, behind, done):
    layers, _, _, channels, _ = weights.shape
    rows, width = clip.shape[1:3]
    every = (layers, 3 * rows, width, channels)
    pixels = sum(rows + 2 * level for level in range(layers)) * width
    zero, one = tick < segments, tick > 0
    extra = (list(sums0) if zero else []) + (list(sums1) + [behind] if one else [])
    outs = [jax.ShapeDtypeStruct((rows, width, channels), BF16)]
    if zero:
        outs.append(jax.ShapeDtypeStruct(every, BF16))
    specs = in_vmem(len(outs)) + [anywhere()]
    outs.append(jax.ShapeDtypeStruct(done.shape, BF16))
    return pl.pallas_call(
        functools.partial(tick_kernel, tick, segments, bands, cut),
        out_shape=tuple(outs),
        in_specs=[in_smem()] + in_vmem(6 + len(extra)) + [anywhere()],
        out_specs=tuple(specs),
        scratch_shapes=[
            pltpu.VMEM((3 * rows, width, channels), BF16),
            pltpu.VMEM((3 * rows, width, 3 * channels), BF16),
            pltpu.VMEM(every, BF16),
            pltpu.SemaphoreType.DMA,
        ],
        input_output_aliases={7 + len(extra): len(outs) - 1},
        compiler_params=pltpu.CompilerParams(vmem_limit_bytes=LIMIT),
        cost_estimate=pl.CostEstimate(
            flops=pixels * 18 * 2 * channels * channels, bytes_accessed=4000000, transcendentals=pixels * channels
        ),
        name="tick",
    )(flags, clip, own, inner, cross, weights, biases, *extra, done)


def per_device(clip, caches, weights, biases, section_layers):
    segments = lax.axis_size("segment")
    bands = lax.axis_size("band")
    caches, weights, biases = caches[0], weights[0], biases[0]
    layers = weights.shape[0]
    cut = layers // 2
    flags = jnp.stack([lax.axis_index("segment"), lax.axis_index("band"), section_layers[0]]).astype(jnp.int32)
    axes = ("segment", "band")
    in_chip = [(b, b ^ 1) for b in range(bands)]
    between = [(b, b + 1) for b in range(1, bands - 1, 2)] + [(b + 1, b) for b in range(1, bands - 1, 2)]
    straight = [(b, b) for b in range(bands)]

    def swap(value, pairs, chosen):
        return lax.ppermute(value, axes, [(s * bands + a, s * bands + b) for s in chosen for a, b in pairs])

    def ahead(value, pairs, sources):
        return lax.ppermute(value, axes, [(s * bands + a, (s + 1) * bands + b) for s in sources for a, b in pairs])

    everyone = range(segments)
    cross = swap(clip[0], between, [0])
    inner = swap(clip[0], in_chip, [0])
    sums0a, sums1a, in0a, cross0a, done = history_call(0, cut, flags, caches, weights)
    cross0a = swap(cross0a, between, everyone)
    in0a = swap(in0a, in_chip, everyone)
    former, cross, inner = lax.optimization_barrier((sums1a, cross, inner))
    sums0b, sums1b, in0b, cross0b, in1, cross1 = history_call(cut, layers, flags, caches, weights, clip, former)
    cross0b = swap(cross0b, between, everyone)
    in0b = swap(in0b, in_chip, everyone)
    cross1 = swap(cross1, between, everyone)
    in1 = swap(in1, in_chip, everyone)
    sums0 = (sums0a, sums0b, in0a, cross0a, in0b, cross0b)
    sums1 = (sums1a, sums1b, in1, cross1)
    own = clip[0]
    behind = None
    for tick in range(segments + 1):
        x, *later, done = tick_call(
            tick, segments, bands, cut, flags, clip, own, inner, cross, weights, biases, sums0, sums1, behind, done
        )
        if tick < segments:
            (behind,) = later
            sources = [s for s in (tick, tick - 1) if 0 <= s < segments - 1]
            own, cross = ahead(x, straight, sources), ahead(x, between, sources)
            inner = swap(own, in_chip, [s + 1 for s in sources])
    return done[None]


def solution(mesh):
    placed = (
        P(None, "band", None, None),
        P("segment", None, None, "band", None, None),
        P("segment", None, None, None, None, None),
        P("segment", None, None),
        P("segment"),
    )
    return jax.shard_map(
        per_device,
        mesh=mesh,
        in_specs=placed,
        out_specs=P("segment", None, "band", None, None),
        check_vma=False,
    )
```

```python
import functools

import jax
import jax.numpy as jnp
from jax import lax
from jax.experimental import pallas as pl
from jax.experimental.pallas import tpu as pltpu
from jax.sharding import PartitionSpec as P

LIMIT = 28 * 1024 * 1024
HISTORY_LIMIT = 52 * 1024 * 1024
F32 = jnp.float32
BF16 = jnp.bfloat16


def message_starts(layers, first=0, last=None):
    starts = [0]
    for level in range(first, layers if last is None else last):
        starts.append(starts[-1] + layers - level)
    return starts


def taps_into(s_ref, row, a):
    width, channels = a.shape
    tile = 16
    place = lax.broadcasted_iota(jnp.int32, (tile, channels), 0)
    left = pltpu.roll(a, 1, 0)
    right = pltpu.roll(a, width - 1, 0)
    s_ref[row, 0:tile, 0:channels] = jnp.where(place == 0, 0.0, left[:tile]).astype(BF16)
    s_ref[row, tile:, 0:channels] = left[tile:].astype(BF16)
    s_ref[row, :, channels : 2 * channels] = a.astype(BF16)
    s_ref[row, : width - tile, 2 * channels : 3 * channels] = right[: width - tile].astype(BF16)
    s_ref[row, width - tile :, 2 * channels : 3 * channels] = jnp.where(
        place == tile - 1, 0.0, right[width - tile :]
    ).astype(BF16)


def rows_dot(s_ref, first, count, w, layer, times):
    width, depth = s_ref.shape[1:]
    taps = jnp.concatenate([s_ref[pl.ds(first + i, count)].reshape(count * width, depth) for i in range(3)], axis=1)
    weights = jnp.concatenate([jnp.concatenate([w[layer, k, t] for t in times], axis=1) for k in range(9)], axis=0)
    return jnp.dot(taps, weights, preferred_element_type=F32)


def pairs_dot(s_ref, first, count, w, layer, time):
    width, depth = s_ref.shape[1:]
    channels = depth // 3
    taps = jnp.concatenate(
        [jnp.concatenate([s_ref[first + i + 2 * p] for p in range(count)], axis=0) for i in range(4)], axis=1
    )
    zero = jnp.zeros((channels, channels), BF16)

    def tap(i, j):
        return w[layer, 3 * i + j, time] if 0 <= i < 3 else zero

    weights = jnp.concatenate(
        [jnp.concatenate([tap(i, j), tap(i - 1, j)], axis=1) for i in range(4) for j in range(3)], axis=0
    )
    total = jnp.dot(taps, weights, preferred_element_type=F32)
    upper = total[:, :channels].reshape(count, 1, width, channels)
    lower = total[:, channels:].reshape(count, 1, width, channels)
    return jnp.concatenate([upper, lower], axis=1)


def history_kernel(first, last, flags, clip, caches, w, *refs):
    layers, _, rows, width, channels = caches.shape
    final = last == layers
    if final:
        former, sums0, sums1, in0, cross0, in1, cross1, c, wb, s, sems = refs
    else:
        sums0, sums1, in0, cross0, done, c, wb, s, sems = refs

    band_start = message_starts(layers)[-1] if final else message_starts(layers, first, last)[-1]
    clip_copies = [
        pltpu.make_async_copy(clip.at[int(final)], message.at[band_start : band_start + rows], sems.at[i, 2])
        for i, message in enumerate((in1, cross1) if final else (in0, cross0))
    ]
    for copy in clip_copies:
        copy.start()

    def load(slot, layer):
        return [
            pltpu.make_async_copy(caches.at[layer], c.at[slot], sems.at[slot, 0]),
            pltpu.make_async_copy(w.at[layer, :, 0:2], wb.at[slot], sems.at[slot, 1]),
        ]

    def run(levels, layer_of):
        loads = [load(i, layer_of(level)) for i, level in enumerate(levels)]
        for copies in loads:
            for copy in copies:
                copy.start()
        for i, level in enumerate(levels):
            for f in range(2):
                s[i, f, 0:2] = jnp.zeros((2,) + s.shape[3:], BF16)
                s[i, f, rows + 2 : rows + 4] = jnp.zeros((2,) + s.shape[3:], BF16)
        for i, level in enumerate(levels):
            for copy in loads[i]:
                copy.wait()
            for f in (1, 0):
                for row in range(rows):
                    taps_into(s.at[i, f], row + 2, c[i, f, row].astype(F32))
            newer = rows_dot(s.at[i, 1], 0, rows + 2, wb, i, (1, 0))
            older = pairs_dot(s.at[i, 0], 0, (rows + 2) // 2, wb, i, 0).reshape(rows + 2, width, channels)
            sums0[level - first] = (newer[:, :channels].reshape(rows + 2, width, channels) + older).astype(BF16)
            sums1[level - first] = newer[:, channels:].reshape(rows + 2, width, channels).astype(BF16)

    cases = {}
    for amount in range(1, layers + 1):
        levels = tuple(level for level in range(first, last) if level >= layers - amount)
        cases.setdefault(levels, []).append(amount)
    for levels, amounts in cases.items():
        if levels:

            @pl.when(jnp.logical_and(flags[2] >= amounts[0], flags[2] <= amounts[-1]))
            def _(levels=levels):
                run(levels, lambda level: level - (layers - flags[2]))

    def pack(of_level, starts, levels, up, down):
        for i, level in enumerate(levels):
            reach = layers - level
            sums, at = of_level(level)
            up[starts[i] : starts[i + 1]] = sums[at, 0:reach]
            down[starts[i] : starts[i + 1]] = sums[at, rows + 2 - reach : rows + 2]

    def messages(up0, down0, up1, down1):
        starts = message_starts(layers, first, last)
        pack(lambda level: (sums0, level - first), starts, range(first, last), up0, down0)
        if final:
            starts = message_starts(layers)
            pack(
                lambda level: (former, level) if level < first else (sums1, level - first),
                starts, range(layers), up1, down1,
            )
    @pl.when(flags[1] % 2 == 0)
    def _():
        messages(cross0, in0, *((cross1, in1) if final else (None, None)))

    @pl.when(flags[1] % 2 != 0)
    def _():
        messages(in0, cross0, *((in1, cross1) if final else (None, None)))

    for copy in clip_copies:
        copy.wait()


def pieces(count):
    parts, at = [], 0
    while at < count:
        step = 4 if count - at in (4, 8) else min(6, count - at)
        parts.append((at, step))
        at += step
    return parts


def tick_kernel(tick, segments, bands, cut, flags, clip, own, inner, cross, w, bias, *refs):
    zero, one = tick < segments, tick > 0
    refs = list(refs)

    def take(count):
        found, refs[:count] = refs[:count], []
        return found

    sums0 = take(6) if zero else None
    sums1 = take(4) if one else None
    behind = take(1)[0] if one else None
    done = take(1)
    x_out = take(1)[0]
    ahead = take(1)[0] if zero else None
    done_out, x, s, part, sem = refs
    rows, width, channels = x_out.shape
    layers = w.shape[0]
    band = flags[1]
    begin = layers - flags[2]
    low = jnp.where(band == 0, rows, 0)
    high = jnp.where(band == bands - 1, 2 * rows, 3 * rows)

    def run(frame, fresh, own, inner, cross, halo, level_sums, level_messages):
        x[rows : 2 * rows] = own[frame] if fresh else own[...]

        def gather(above, below, side_above, side_below):
            x[0:rows] = above[halo : halo + rows]
            x[2 * rows : 3 * rows] = below[halo : halo + rows]
            for level in range(layers):

                @pl.when(level >= begin)
                def _(level=level):
                    reach = layers - level
                    sums, at = level_sums(level)
                    start, sums_above, sums_below = level_messages(level, side_above, side_below)
                    part[level, rows + 1 - reach : rows + 1] = sums_above[start : start + reach]
                    part[level, 2 * rows - 1 : 2 * rows - 1 + reach] = sums_below[start : start + reach]
                    part[level, rows + 1 : 2 * rows - 1] = sums[at, 2:rows]
                    part[level, rows] += sums[at, 1]
                    part[level, 2 * rows - 1] += sums[at, rows]
                    if reach > 1:
                        part[level, rows - 1] += sums[at, 0]
                        part[level, 2 * rows] += sums[at, rows + 1]

        @pl.when(band % 2 == 0)
        def _():
            gather(cross, inner, 1, 0)

        @pl.when(band % 2 != 0)
        def _():
            gather(inner, cross, 0, 1)

        def activate(level, row, value):
            half = value * 0.5
            act = half + half * jnp.tanh(half)
            if not rows <= row < 2 * rows:
                act = act * jnp.logical_and(row >= low, row < high).astype(F32)
            taps_into(s.at[level], row, act)

        def straight(amount):
            begin = layers - amount
            for row in range(rows - layers + begin, 2 * rows + layers - begin):
                activate(begin, row, x[row].astype(F32))
            for level in range(begin, layers):
                layer = level - begin
                first = rows - layers + 1 + level
                count = rows + 2 * (layers - 1 - level)
                offset = bias[layer : layer + 1, :]
                for start, step in pieces(count):
                    at = first + start
                    if frame == 0:
                        total = rows_dot(s.at[level], at - 1, step, w, layer, (2, 1))
                        mine = total[:, :channels].reshape(step, width, channels)
                        ahead[level, at : at + step] = total[:, channels:].reshape(step, width, channels).astype(BF16)
                    else:
                        mine = pairs_dot(s.at[level], at - 1, step // 2, w, layer, 2).reshape(step, width, channels)
                    for i in range(step):
                        row = at + i
                        known = part[level, row].astype(F32) + offset
                        if frame == 1:
                            known = known + behind[level, row].astype(F32)
                        value = (x[row].astype(F32) + (mine[i] + known)).astype(BF16)
                        x[row] = value
                        if level + 1 < layers:
                            activate(level + 1, row, value.astype(F32))

        for amount in range(1, layers + 1):

            @pl.when(flags[2] == amount)
            def _(amount=amount):
                straight(amount)

        copy = pltpu.make_async_copy(x.at[rows : 2 * rows], done_out.at[frame], sem)
        copy.start()
        x_out[...] = x[rows : 2 * rows]
        copy.wait()

    if zero:
        sums_a, sums_b, in_a, cross_a, in_b, cross_b = sums0
        starts_a, starts_b = message_starts(layers, 0, cut), message_starts(layers, cut)

        def messages0(level, above, below):
            if level < cut:
                return starts_a[level], (in_a, cross_a)[above], (in_a, cross_a)[below]
            return starts_b[level - cut], (in_b, cross_b)[above], (in_b, cross_b)[below]

        @pl.when(flags[0] == tick)
        def _():
            run(
                0, tick == 0, clip if tick == 0 else own, inner, cross, starts_a[-1] if tick == 0 else 0,
                lambda level: (sums_a, level) if level < cut else (sums_b, level - cut), messages0,
            )

    if one:
        sums_c, sums_d, in1, cross1 = sums1
        starts = message_starts(layers)

        def messages1(level, above, below):
            return starts[level], (in1, cross1)[above], (in1, cross1)[below]

        @pl.when(flags[0] == tick - 1)
        def _():
            fresh = tick == 1
            run(
                1, fresh, clip if fresh else own, in1 if fresh else inner, cross1 if fresh else cross,
                starts[-1] if fresh else 0,
                lambda level: (sums_c, level) if level < cut else (sums_d, level - cut), messages1,
            )


def in_vmem(count):
    return [pl.BlockSpec(memory_space=pltpu.VMEM)] * count


def anywhere():
    return pl.BlockSpec(memory_space=pl.ANY)


def in_smem():
    return pl.BlockSpec(memory_space=pltpu.SMEM)


def history_call(first, last, flags, clip, caches, weights, *more):
    layers, _, rows, width, channels = caches.shape
    count = last - first
    sums = jax.ShapeDtypeStruct((count, rows + 2, width, channels), BF16)
    final = last == layers

    def message(band, *levels):
        return [jax.ShapeDtypeStruct((message_starts(layers, *levels)[-1] + band, width, channels), BF16)] * 2

    outs = [sums, sums] + message(0 if final else rows, first, last) + (message(rows) if final else [])
    specs = in_vmem(len(outs))
    if not final:
        outs.append(jax.ShapeDtypeStruct(clip.shape, BF16))
        specs.append(anywhere())
    pixels = count * (rows + 2) * width
    return pl.pallas_call(
        functools.partial(history_kernel, first, last),
        out_shape=tuple(outs),
        in_specs=[in_smem(), anywhere(), anywhere(), anywhere()] + in_vmem(len(more)),
        out_specs=tuple(specs),
        scratch_shapes=[
            pltpu.VMEM((count,) + caches.shape[1:], BF16),
            pltpu.VMEM((count, 9, 2, channels, channels), BF16),
            pltpu.VMEM((count, 2, rows + 4, width, 3 * channels), BF16),
            pltpu.SemaphoreType.DMA((max(count, 2), 3)),
        ],
        compiler_params=pltpu.CompilerParams(vmem_limit_bytes=HISTORY_LIMIT),
        cost_estimate=pl.CostEstimate(
            flops=pixels * 27 * 2 * channels * channels, bytes_accessed=4000000, transcendentals=0
        ),
        name="history",
    )(flags, clip, caches, weights, *more)


def tick_call(tick, segments, bands, cut, flags, clip, own, inner, cross, weights, biases, sums0, sums1, behind, done):
    layers, _, _, channels, _ = weights.shape
    rows, width = clip.shape[1:3]
    every = (layers, 3 * rows, width, channels)
    pixels = sum(rows + 2 * level for level in range(layers)) * width
    zero, one = tick < segments, tick > 0
    extra = (list(sums0) if zero else []) + (list(sums1) + [behind] if one else [])
    outs = [jax.ShapeDtypeStruct((rows, width, channels), BF16)]
    if zero:
        outs.append(jax.ShapeDtypeStruct(every, BF16))
    specs = in_vmem(len(outs)) + [anywhere()]
    outs.append(jax.ShapeDtypeStruct(done.shape, BF16))
    return pl.pallas_call(
        functools.partial(tick_kernel, tick, segments, bands, cut),
        out_shape=tuple(outs),
        in_specs=[in_smem()] + in_vmem(6 + len(extra)) + [anywhere()],
        out_specs=tuple(specs),
        scratch_shapes=[
            pltpu.VMEM((3 * rows, width, channels), BF16),
            pltpu.VMEM((layers, 3 * rows, width, 3 * channels), BF16),
            pltpu.VMEM(every, BF16),
            pltpu.SemaphoreType.DMA,
        ],
        input_output_aliases={7 + len(extra): len(outs) - 1},
        compiler_params=pltpu.CompilerParams(vmem_limit_bytes=LIMIT),
        cost_estimate=pl.CostEstimate(
            flops=pixels * 18 * 2 * channels * channels, bytes_accessed=4000000, transcendentals=pixels * channels
        ),
        name="tick",
    )(flags, clip, own, inner, cross, weights, biases, *extra, done)


def per_device(clip, caches, weights, biases, section_layers):
    segments = lax.axis_size("segment")
    bands = lax.axis_size("band")
    caches, weights, biases = caches[0], weights[0], biases[0]
    layers = weights.shape[0]
    cut = layers // 2
    flags = jnp.stack([lax.axis_index("segment"), lax.axis_index("band"), section_layers[0]]).astype(jnp.int32)
    axes = ("segment", "band")
    in_chip = [(b, b ^ 1) for b in range(bands)]
    between = [(b, b + 1) for b in range(1, bands - 1, 2)] + [(b + 1, b) for b in range(1, bands - 1, 2)]
    straight = [(b, b) for b in range(bands)]

    def swap(value, pairs, chosen):
        return lax.ppermute(value, axes, [(s * bands + a, s * bands + b) for s in chosen for a, b in pairs])

    def ahead(value, pairs, sources):
        return lax.ppermute(value, axes, [(s * bands + a, (s + 1) * bands + b) for s in sources for a, b in pairs])

    everyone = range(segments)
    sums0a, sums1a, in0a, cross0a, done = history_call(0, cut, flags, clip, caches, weights)
    cross0a = swap(cross0a, between, everyone)
    in0a = swap(in0a, in_chip, everyone)
    sums0b, sums1b, in0b, cross0b, in1, cross1 = history_call(cut, layers, flags, clip, caches, weights, sums1a)
    cross0b = swap(cross0b, between, everyone)
    in0b = swap(in0b, in_chip, everyone)
    cross1 = swap(cross1, between, everyone)
    in1 = swap(in1, in_chip, everyone)
    sums0 = (sums0a, sums0b, in0a, cross0a, in0b, cross0b)
    sums1 = (sums1a, sums1b, in1, cross1)
    own, inner, cross = clip, in0a, cross0a
    behind = None
    for tick in range(segments + 1):
        x, *later, done = tick_call(
            tick, segments, bands, cut, flags, clip, own, inner, cross, weights, biases, sums0, sums1, behind, done
        )
        if tick < segments:
            (behind,) = later
            sources = [s for s in (tick, tick - 1) if 0 <= s < segments - 1]
            own, cross = ahead(x, straight, sources), ahead(x, between, sources)
            inner = swap(own, in_chip, [s + 1 for s in sources])
    return done[None]


def solution(mesh):
    placed = (
        P(None, "band", None, None),
        P("segment", None, None, "band", None, None),
        P("segment", None, None, None, None, None),
        P("segment", None, None),
        P("segment"),
    )
    return jax.shard_map(
        per_device,
        mesh=mesh,
        in_specs=placed,
        out_specs=P("segment", None, "band", None, None),
        check_vma=False,
    )
```

```python
import functools

import jax
import jax.numpy as jnp
from jax import lax
from jax.experimental import pallas as pl
from jax.experimental.pallas import tpu as pltpu
from jax.sharding import PartitionSpec as P

LIMIT = 28 * 1024 * 1024
HISTORY_LIMIT = 52 * 1024 * 1024
F32 = jnp.float32
BF16 = jnp.bfloat16


def message_starts(layers, first=0, last=None):
    starts = [0]
    for level in range(first, layers if last is None else last):
        starts.append(starts[-1] + layers - level)
    return starts


def taps_into(s_ref, row, a):
    width, channels = a.shape
    tile = 16
    place = lax.broadcasted_iota(jnp.int32, (tile, channels), 0)
    left = pltpu.roll(a, 1, 0)
    right = pltpu.roll(a, width - 1, 0)
    s_ref[row, 0:tile, 0:channels] = jnp.where(place == 0, 0.0, left[:tile]).astype(BF16)
    s_ref[row, tile:, 0:channels] = left[tile:].astype(BF16)
    s_ref[row, :, channels : 2 * channels] = a.astype(BF16)
    s_ref[row, : width - tile, 2 * channels : 3 * channels] = right[: width - tile].astype(BF16)
    s_ref[row, width - tile :, 2 * channels : 3 * channels] = jnp.where(
        place == tile - 1, 0.0, right[width - tile :]
    ).astype(BF16)


def rows_dot(s_ref, first, count, w, layer, times):
    width, depth = s_ref.shape[1:]
    taps = jnp.concatenate([s_ref[pl.ds(first + i, count)].reshape(count * width, depth) for i in range(3)], axis=1)
    weights = jnp.concatenate([jnp.concatenate([w[layer, k, t] for t in times], axis=1) for k in range(9)], axis=0)
    return jnp.dot(taps, weights, preferred_element_type=F32)


def pairs_dot(s_ref, first, count, w, layer, time):
    width, depth = s_ref.shape[1:]
    channels = depth // 3
    taps = jnp.concatenate(
        [jnp.concatenate([s_ref[first + i + 2 * p] for p in range(count)], axis=0) for i in range(4)], axis=1
    )
    zero = jnp.zeros((channels, channels), BF16)

    def tap(i, j):
        return w[layer, 3 * i + j, time] if 0 <= i < 3 else zero

    weights = jnp.concatenate(
        [jnp.concatenate([tap(i, j), tap(i - 1, j)], axis=1) for i in range(4) for j in range(3)], axis=0
    )
    total = jnp.dot(taps, weights, preferred_element_type=F32)
    upper = total[:, :channels].reshape(count, 1, width, channels)
    lower = total[:, channels:].reshape(count, 1, width, channels)
    return jnp.concatenate([upper, lower], axis=1)


def history_kernel(first, last, flags, clip, caches, w, *refs):
    layers, _, rows, width, channels = caches.shape
    final = last == layers
    if final:
        former, sums0, sums1, in0, cross0, in1, cross1, c, wb, s, sems = refs
    else:
        sums0, sums1, in0, cross0, done, c, wb, s, sems = refs

    band_start = message_starts(layers)[-1] if final else message_starts(layers, first, last)[-1]
    clip_copies = [
        pltpu.make_async_copy(clip.at[int(final)], message.at[band_start : band_start + rows], sems.at[i, 2])
        for i, message in enumerate((in1, cross1) if final else (in0, cross0))
    ]
    for copy in clip_copies:
        copy.start()

    begin = layers - flags[2]

    def loads(slot, layer):
        return [
            pltpu.make_async_copy(caches.at[layer], c.at[slot], sems.at[slot, 0]),
            pltpu.make_async_copy(w.at[layer, :, 0:2], wb.at[slot], sems.at[slot, 1]),
        ]

    for level in range(first, last):

        @pl.when(level >= begin)
        def _(level=level):
            for copy in loads(level - first, level - begin):
                copy.start()

    for f in range(2):
        s[f, 0:2] = jnp.zeros((2,) + s.shape[2:], BF16)
        s[f, rows + 2 : rows + 4] = jnp.zeros((2,) + s.shape[2:], BF16)

    def level_step(level, _):
        slot = level - first
        for copy in loads(slot, level - begin):
            copy.wait()

        def build(row, _):
            taps_into(s.at[0], row + 2, c[slot, 0, row].astype(F32))
            taps_into(s.at[1], row + 2, c[slot, 1, row].astype(F32))
            return 0

        lax.fori_loop(0, rows, build, 0)
        newer = rows_dot(s.at[1], 0, rows + 2, wb, slot, (1, 0))
        older = pairs_dot(s.at[0], 0, (rows + 2) // 2, wb, slot, 0).reshape(rows + 2, width, channels)
        sums0[slot] = (newer[:, :channels].reshape(rows + 2, width, channels) + older).astype(BF16)
        sums1[slot] = newer[:, channels:].reshape(rows + 2, width, channels).astype(BF16)
        return 0

    lax.fori_loop(jnp.maximum(begin, first), last, level_step, 0)

    def pack(of_level, starts, levels, up, down):
        for i, level in enumerate(levels):
            reach = layers - level
            sums, at = of_level(level)
            up[starts[i] : starts[i + 1]] = sums[at, 0:reach]
            down[starts[i] : starts[i + 1]] = sums[at, rows + 2 - reach : rows + 2]

    def messages(up0, down0, up1, down1):
        starts = message_starts(layers, first, last)
        pack(lambda level: (sums0, level - first), starts, range(first, last), up0, down0)
        if final:
            starts = message_starts(layers)
            pack(
                lambda level: (former, level) if level < first else (sums1, level - first),
                starts, range(layers), up1, down1,
            )
    @pl.when(flags[1] % 2 == 0)
    def _():
        messages(cross0, in0, *((cross1, in1) if final else (None, None)))

    @pl.when(flags[1] % 2 != 0)
    def _():
        messages(in0, cross0, *((in1, cross1) if final else (None, None)))

    for copy in clip_copies:
        copy.wait()


def pieces(count):
    parts, at = [], 0
    while at < count:
        step = 4 if count - at in (4, 8) else min(6, count - at)
        parts.append((at, step))
        at += step
    return parts


def tick_kernel(tick, segments, bands, cut, flags, clip, own, inner, cross, w, bias, *refs):
    zero, one = tick < segments, tick > 0
    refs = list(refs)

    def take(count):
        found, refs[:count] = refs[:count], []
        return found

    sums0 = take(6) if zero else None
    sums1 = take(4) if one else None
    behind = take(1)[0] if one else None
    done = take(1)
    x_out = take(1)[0]
    ahead = take(1)[0] if zero else None
    done_out, x, s, part, sem = refs
    rows, width, channels = x_out.shape
    layers = w.shape[0]
    band = flags[1]
    begin = layers - flags[2]
    low = jnp.where(band == 0, rows, 0)
    high = jnp.where(band == bands - 1, 2 * rows, 3 * rows)

    def run(frame, fresh, own, inner, cross, halo, level_sums, level_messages):
        x[rows : 2 * rows] = own[frame] if fresh else own[...]

        def gather(above, below, side_above, side_below):
            x[0:rows] = above[halo : halo + rows]
            x[2 * rows : 3 * rows] = below[halo : halo + rows]
            for level in range(layers):

                @pl.when(level >= begin)
                def _(level=level):
                    reach = layers - level
                    sums, at = level_sums(level)
                    start, sums_above, sums_below = level_messages(level, side_above, side_below)
                    part[level, rows + 1 - reach : rows + 1] = sums_above[start : start + reach]
                    part[level, 2 * rows - 1 : 2 * rows - 1 + reach] = sums_below[start : start + reach]
                    part[level, rows + 1 : 2 * rows - 1] = sums[at, 2:rows]
                    part[level, rows] += sums[at, 1]
                    part[level, 2 * rows - 1] += sums[at, rows]
                    if reach > 1:
                        part[level, rows - 1] += sums[at, 0]
                        part[level, 2 * rows] += sums[at, rows + 1]

        @pl.when(band % 2 == 0)
        def _():
            gather(cross, inner, 1, 0)

        @pl.when(band % 2 != 0)
        def _():
            gather(inner, cross, 0, 1)

        def build(row):
            half = x[row].astype(F32) * 0.5
            inside = jnp.logical_and(row >= low, row < high).astype(F32)
            taps_into(s, row, (half + half * jnp.tanh(half)) * inside)

        for level in range(layers):

            @pl.when(level >= begin)
            def _(level=level):
                layer = level - begin
                first = rows - layers + 1 + level
                count = rows + 2 * (layers - 1 - level)

                def two(i, _):
                    build(first - 1 + 2 * i)
                    build(first + 2 * i)
                    return 0

                lax.fori_loop(0, count // 2 + 1, two, 0)
                offset = bias[pl.ds(layer, 1), :].reshape(1, 1, channels)
                for start, step in pieces(count):
                    at = first + start
                    known = part[level, at : at + step].astype(F32) + offset
                    if frame == 0:
                        total = rows_dot(s, at - 1, step, w, layer, (2, 1))
                        mine = total[:, :channels].reshape(step, width, channels)
                        ahead[level, at : at + step] = total[:, channels:].reshape(step, width, channels).astype(BF16)
                    else:
                        mine = pairs_dot(s, at - 1, step // 2, w, layer, 2).reshape(step, width, channels)
                        known = known + behind[level, at : at + step].astype(F32)
                    x[at : at + step] = (x[at : at + step].astype(F32) + (mine + known)).astype(BF16)

        copy = pltpu.make_async_copy(x.at[rows : 2 * rows], done_out.at[frame], sem)
        copy.start()
        x_out[...] = x[rows : 2 * rows]
        copy.wait()

    if zero:
        sums_a, sums_b, in_a, cross_a, in_b, cross_b = sums0
        starts_a, starts_b = message_starts(layers, 0, cut), message_starts(layers, cut)

        def messages0(level, above, below):
            if level < cut:
                return starts_a[level], (in_a, cross_a)[above], (in_a, cross_a)[below]
            return starts_b[level - cut], (in_b, cross_b)[above], (in_b, cross_b)[below]

        @pl.when(flags[0] == tick)
        def _():
            run(
                0, tick == 0, clip if tick == 0 else own, inner, cross, starts_a[-1] if tick == 0 else 0,
                lambda level: (sums_a, level) if level < cut else (sums_b, level - cut), messages0,
            )

    if one:
        sums_c, sums_d, in1, cross1 = sums1
        starts = message_starts(layers)

        def messages1(level, above, below):
            return starts[level], (in1, cross1)[above], (in1, cross1)[below]

        @pl.when(flags[0] == tick - 1)
        def _():
            fresh = tick == 1
            run(
                1, fresh, clip if fresh else own, in1 if fresh else inner, cross1 if fresh else cross,
                starts[-1] if fresh else 0,
                lambda level: (sums_c, level) if level < cut else (sums_d, level - cut), messages1,
            )


def in_vmem(count):
    return [pl.BlockSpec(memory_space=pltpu.VMEM)] * count


def anywhere():
    return pl.BlockSpec(memory_space=pl.ANY)


def in_smem():
    return pl.BlockSpec(memory_space=pltpu.SMEM)


def history_call(first, last, flags, clip, caches, weights, *more):
    layers, _, rows, width, channels = caches.shape
    count = last - first
    sums = jax.ShapeDtypeStruct((count, rows + 2, width, channels), BF16)
    final = last == layers

    def message(band, *levels):
        return [jax.ShapeDtypeStruct((message_starts(layers, *levels)[-1] + band, width, channels), BF16)] * 2

    outs = [sums, sums] + message(0 if final else rows, first, last) + (message(rows) if final else [])
    specs = in_vmem(len(outs))
    if not final:
        outs.append(jax.ShapeDtypeStruct(clip.shape, BF16))
        specs.append(anywhere())
    pixels = count * (rows + 2) * width
    return pl.pallas_call(
        functools.partial(history_kernel, first, last),
        out_shape=tuple(outs),
        in_specs=[in_smem(), anywhere(), anywhere(), anywhere()] + in_vmem(len(more)),
        out_specs=tuple(specs),
        scratch_shapes=[
            pltpu.VMEM((count,) + caches.shape[1:], BF16),
            pltpu.VMEM((count, 9, 2, channels, channels), BF16),
            pltpu.VMEM((2, rows + 4, width, 3 * channels), BF16),
            pltpu.SemaphoreType.DMA((max(count, 2), 3)),
        ],
        compiler_params=pltpu.CompilerParams(vmem_limit_bytes=HISTORY_LIMIT),
        cost_estimate=pl.CostEstimate(
            flops=pixels * 27 * 2 * channels * channels, bytes_accessed=4000000, transcendentals=0
        ),
        name="history",
    )(flags, clip, caches, weights, *more)


def tick_call(tick, segments, bands, cut, flags, clip, own, inner, cross, weights, biases, sums0, sums1, behind, done):
    layers, _, _, channels, _ = weights.shape
    rows, width = clip.shape[1:3]
    every = (layers, 3 * rows, width, channels)
    pixels = sum(rows + 2 * level for level in range(layers)) * width
    zero, one = tick < segments, tick > 0
    extra = (list(sums0) if zero else []) + (list(sums1) + [behind] if one else [])
    outs = [jax.ShapeDtypeStruct((rows, width, channels), BF16)]
    if zero:
        outs.append(jax.ShapeDtypeStruct(every, BF16))
    specs = in_vmem(len(outs)) + [anywhere()]
    outs.append(jax.ShapeDtypeStruct(done.shape, BF16))
    return pl.pallas_call(
        functools.partial(tick_kernel, tick, segments, bands, cut),
        out_shape=tuple(outs),
        in_specs=[in_smem()] + in_vmem(6 + len(extra)) + [anywhere()],
        out_specs=tuple(specs),
        scratch_shapes=[
            pltpu.VMEM((3 * rows, width, channels), BF16),
            pltpu.VMEM((3 * rows, width, 3 * channels), BF16),
            pltpu.VMEM(every, BF16),
            pltpu.SemaphoreType.DMA,
        ],
        input_output_aliases={7 + len(extra): len(outs) - 1},
        compiler_params=pltpu.CompilerParams(vmem_limit_bytes=LIMIT),
        cost_estimate=pl.CostEstimate(
            flops=pixels * 18 * 2 * channels * channels, bytes_accessed=4000000, transcendentals=pixels * channels
        ),
        name="tick",
    )(flags, clip, own, inner, cross, weights, biases, *extra, done)


def per_device(clip, caches, weights, biases, section_layers):
    segments = lax.axis_size("segment")
    bands = lax.axis_size("band")
    caches, weights, biases = caches[0], weights[0], biases[0]
    layers = weights.shape[0]
    cut = layers // 2
    flags = jnp.stack([lax.axis_index("segment"), lax.axis_index("band"), section_layers[0]]).astype(jnp.int32)
    axes = ("segment", "band")
    in_chip = [(b, b ^ 1) for b in range(bands)]
    between = [(b, b + 1) for b in range(1, bands - 1, 2)] + [(b + 1, b) for b in range(1, bands - 1, 2)]
    straight = [(b, b) for b in range(bands)]

    def swap(value, pairs, chosen):
        return lax.ppermute(value, axes, [(s * bands + a, s * bands + b) for s in chosen for a, b in pairs])

    def ahead(value, pairs, sources):
        return lax.ppermute(value, axes, [(s * bands + a, (s + 1) * bands + b) for s in sources for a, b in pairs])

    everyone = range(segments)
    sums0a, sums1a, in0a, cross0a, done = history_call(0, cut, flags, clip, caches, weights)
    cross0a = swap(cross0a, between, everyone)
    in0a = swap(in0a, in_chip, everyone)
    sums0b, sums1b, in0b, cross0b, in1, cross1 = history_call(cut, layers, flags, clip, caches, weights, sums1a)
    cross0b = swap(cross0b, between, everyone)
    in0b = swap(in0b, in_chip, everyone)
    cross1 = swap(cross1, between, everyone)
    in1 = swap(in1, in_chip, everyone)
    sums0 = (sums0a, sums0b, in0a, cross0a, in0b, cross0b)
    sums1 = (sums1a, sums1b, in1, cross1)
    own, inner, cross = clip, in0a, cross0a
    behind = None
    for tick in range(segments + 1):
        x, *later, done = tick_call(
            tick, segments, bands, cut, flags, clip, own, inner, cross, weights, biases, sums0, sums1, behind, done
        )
        if tick < segments:
            (behind,) = later
            sources = [s for s in (tick, tick - 1) if 0 <= s < segments - 1]
            own, cross = ahead(x, straight, sources), ahead(x, between, sources)
            inner = swap(own, in_chip, [s + 1 for s in sources])
    return done[None]


def solution(mesh):
    placed = (
        P(None, "band", None, None),
        P("segment", None, None, "band", None, None),
        P("segment", None, None, None, None, None),
        P("segment", None, None),
        P("segment"),
    )
    return jax.shard_map(
        per_device,
        mesh=mesh,
        in_specs=placed,
        out_specs=P("segment", None, "band", None, None),
        check_vma=False,
    )
```

```python
import functools

import jax
import jax.numpy as jnp
from jax import lax
from jax.experimental import pallas as pl
from jax.experimental.pallas import tpu as pltpu
from jax.sharding import PartitionSpec as P

LIMIT = 28 * 1024 * 1024
HISTORY_LIMIT = 52 * 1024 * 1024
F32 = jnp.float32
BF16 = jnp.bfloat16


def message_starts(layers, first=0, last=None):
    starts = [0]
    for level in range(first, layers if last is None else last):
        starts.append(starts[-1] + layers - level)
    return starts


def taps_into(s_ref, row, a):
    width, channels = a.shape
    tile = 16
    place = lax.broadcasted_iota(jnp.int32, (tile, channels), 0)
    left = pltpu.roll(a, 1, 0)
    right = pltpu.roll(a, width - 1, 0)
    s_ref[row, 0:tile, 0:channels] = jnp.where(place == 0, 0.0, left[:tile]).astype(BF16)
    s_ref[row, tile:, 0:channels] = left[tile:].astype(BF16)
    s_ref[row, :, channels : 2 * channels] = a.astype(BF16)
    s_ref[row, : width - tile, 2 * channels : 3 * channels] = right[: width - tile].astype(BF16)
    s_ref[row, width - tile :, 2 * channels : 3 * channels] = jnp.where(
        place == tile - 1, 0.0, right[width - tile :]
    ).astype(BF16)


def rows_dot(s_ref, first, count, w, layer, times):
    width, depth = s_ref.shape[1:]
    taps = jnp.concatenate([s_ref[pl.ds(first + i, count)].reshape(count * width, depth) for i in range(3)], axis=1)
    weights = jnp.concatenate([jnp.concatenate([w[layer, k, t] for t in times], axis=1) for k in range(9)], axis=0)
    return jnp.dot(taps, weights, preferred_element_type=F32)


def pairs_dot(s_ref, first, count, w, layer, time):
    width, depth = s_ref.shape[1:]
    channels = depth // 3
    taps = jnp.concatenate(
        [jnp.concatenate([s_ref[first + i + 2 * p] for p in range(count)], axis=0) for i in range(4)], axis=1
    )
    zero = jnp.zeros((channels, channels), BF16)

    def tap(i, j):
        return w[layer, 3 * i + j, time] if 0 <= i < 3 else zero

    weights = jnp.concatenate(
        [jnp.concatenate([tap(i, j), tap(i - 1, j)], axis=1) for i in range(4) for j in range(3)], axis=0
    )
    total = jnp.dot(taps, weights, preferred_element_type=F32)
    upper = total[:, :channels].reshape(count, 1, width, channels)
    lower = total[:, channels:].reshape(count, 1, width, channels)
    return jnp.concatenate([upper, lower], axis=1)


def history_kernel(first, last, flags, clip, caches, w, *refs):
    layers, _, rows, width, channels = caches.shape
    final = last == layers
    if final:
        former, sums0, sums1, in0, cross0, in1, cross1, c, wb, s, sems = refs
    else:
        sums0, sums1, in0, cross0, done, c, wb, s, sems = refs

    band_start = message_starts(layers)[-1] if final else message_starts(layers, first, last)[-1]
    clip_copies = [
        pltpu.make_async_copy(clip.at[int(final)], message.at[band_start : band_start + rows], sems.at[i, 2])
        for i, message in enumerate((in1, cross1) if final else (in0, cross0))
    ]
    for copy in clip_copies:
        copy.start()

    begin = layers - flags[2]

    def loads(slot, layer):
        return [
            pltpu.make_async_copy(caches.at[layer], c.at[slot], sems.at[slot, 0]),
            pltpu.make_async_copy(w.at[layer, :, 0:2], wb.at[slot], sems.at[slot, 1]),
        ]

    for level in range(first, last):

        @pl.when(level >= begin)
        def _(level=level):
            for copy in loads(level - first, level - begin):
                copy.start()

    for f in range(2):
        s[f, 0:2] = jnp.zeros((2,) + s.shape[2:], BF16)
        s[f, rows + 2 : rows + 4] = jnp.zeros((2,) + s.shape[2:], BF16)

    def level_step(level, _):
        slot = level - first
        for copy in loads(slot, level - begin):
            copy.wait()

        def build(row, _):
            taps_into(s.at[0], row + 2, c[slot, 0, row].astype(F32))
            taps_into(s.at[1], row + 2, c[slot, 1, row].astype(F32))
            return 0

        lax.fori_loop(0, rows, build, 0)
        newer = rows_dot(s.at[1], 0, rows + 2, wb, slot, (1, 0))
        older = pairs_dot(s.at[0], 0, (rows + 2) // 2, wb, slot, 0).reshape(rows + 2, width, channels)
        sums0[slot] = (newer[:, :channels].reshape(rows + 2, width, channels) + older).astype(BF16)
        sums1[slot] = newer[:, channels:].reshape(rows + 2, width, channels).astype(BF16)
        return 0

    lax.fori_loop(jnp.maximum(begin, first), last, level_step, 0)

    def pack(of_level, starts, levels, up, down):
        for i, level in enumerate(levels):
            reach = layers - level
            sums, at = of_level(level)
            up[starts[i] : starts[i + 1]] = sums[at, 0:reach]
            down[starts[i] : starts[i + 1]] = sums[at, rows + 2 - reach : rows + 2]

    def messages(up0, down0, up1, down1):
        starts = message_starts(layers, first, last)
        pack(lambda level: (sums0, level - first), starts, range(first, last), up0, down0)
        if final:
            starts = message_starts(layers)
            pack(
                lambda level: (former, level) if level < first else (sums1, level - first),
                starts, range(layers), up1, down1,
            )
    @pl.when(flags[1] % 2 == 0)
    def _():
        messages(cross0, in0, *((cross1, in1) if final else (None, None)))

    @pl.when(flags[1] % 2 != 0)
    def _():
        messages(in0, cross0, *((in1, cross1) if final else (None, None)))

    for copy in clip_copies:
        copy.wait()


def tick_kernel(tick, segments, bands, cut, flags, clip, own, inner, cross, w, bias, *refs):
    zero, one = tick < segments, tick > 0
    refs = list(refs)

    def take(count):
        found, refs[:count] = refs[:count], []
        return found

    sums0 = take(6) if zero else None
    sums1 = take(4) if one else None
    behind = take(1)[0] if one else None
    done = take(1)
    x_out = take(1)[0]
    ahead = take(1)[0] if zero else None
    done_out, x, taps_even, taps_odd, product, part, sem = refs
    rows, width, channels = x_out.shape
    layers = w.shape[0]
    band = flags[1]
    begin = layers - flags[2]
    low = jnp.where(band == 0, rows, 0)
    high = jnp.where(band == bands - 1, 2 * rows, 3 * rows)

    def run(frame, fresh, own, inner, cross, halo, level_sums, level_messages):
        x[rows : 2 * rows] = own[frame] if fresh else own[...]

        def gather(above, below, side_above, side_below):
            x[0:rows] = above[halo : halo + rows]
            x[2 * rows : 3 * rows] = below[halo : halo + rows]
            for level in range(layers):

                @pl.when(level >= begin)
                def _(level=level):
                    reach = layers - level
                    sums, at = level_sums(level)
                    start, sums_above, sums_below = level_messages(level, side_above, side_below)
                    part[level, rows + 1 - reach : rows + 1] = sums_above[start : start + reach]
                    part[level, 2 * rows - 1 : 2 * rows - 1 + reach] = sums_below[start : start + reach]
                    part[level, rows + 1 : 2 * rows - 1] = sums[at, 2:rows]
                    part[level, rows] += sums[at, 1]
                    part[level, 2 * rows - 1] += sums[at, rows]
                    if reach > 1:
                        part[level, rows - 1] += sums[at, 0]
                        part[level, 2 * rows] += sums[at, rows + 1]

        @pl.when(band % 2 == 0)
        def _():
            gather(cross, inner, 1, 0)

        @pl.when(band % 2 != 0)
        def _():
            gather(inner, cross, 0, 1)

        taps = (taps_even, taps_odd)
        times = (2, 1) if frame == 0 else (2,)

        def activate(s, row, value):
            half = value * 0.5
            inside = jnp.logical_and(row >= low, row < high).astype(F32)
            taps_into(s, row, (half + half * jnp.tanh(half)) * inside)

        for level in range(layers):

            @pl.when(level >= begin)
            def _(level=level):
                layer = level - begin
                source, following = taps[level % 2], taps[(level + 1) % 2]
                first = rows - layers + 1 + level
                count = rows + 2 * (layers - 1 - level)
                offset = bias[pl.ds(layer, 1), :]

                def multiply(at):
                    return rows_dot(source, at - 1, 2, w, layer, times)

                def finish(at):
                    for i in range(2):
                        row = at + i
                        total = product[i * width : (i + 1) * width]
                        known = part[level, row].astype(F32) + offset
                        if frame == 0:
                            ahead[level, row] = total[:, channels:].astype(BF16)
                        else:
                            known = known + behind[level, row].astype(F32)
                        value = (x[row].astype(F32) + (total[:, :channels] + known)).astype(BF16)
                        x[row] = value
                        if level + 1 < layers:
                            activate(following, row, value.astype(F32))

                @pl.when(level == begin)
                def _():
                    def two(i, _):
                        for row in (first - 1 + 2 * i, first + 2 * i):
                            activate(source, row, x[row].astype(F32))
                        return 0

                    lax.fori_loop(0, count // 2 + 1, two, 0)

                product[:, : len(times) * channels] = multiply(first)

                def chunk(c, _):
                    at = first + 2 * c
                    finish(at - 2)
                    product[:, : len(times) * channels] = multiply(at)
                    return 0

                lax.fori_loop(1, count // 2, chunk, 0)
                finish(first + count - 2)

        copy = pltpu.make_async_copy(x.at[rows : 2 * rows], done_out.at[frame], sem)
        copy.start()
        x_out[...] = x[rows : 2 * rows]
        copy.wait()

    if zero:
        sums_a, sums_b, in_a, cross_a, in_b, cross_b = sums0
        starts_a, starts_b = message_starts(layers, 0, cut), message_starts(layers, cut)

        def messages0(level, above, below):
            if level < cut:
                return starts_a[level], (in_a, cross_a)[above], (in_a, cross_a)[below]
            return starts_b[level - cut], (in_b, cross_b)[above], (in_b, cross_b)[below]

        @pl.when(flags[0] == tick)
        def _():
            run(
                0, tick == 0, clip if tick == 0 else own, inner, cross, starts_a[-1] if tick == 0 else 0,
                lambda level: (sums_a, level) if level < cut else (sums_b, level - cut), messages0,
            )

    if one:
        sums_c, sums_d, in1, cross1 = sums1
        starts = message_starts(layers)

        def messages1(level, above, below):
            return starts[level], (in1, cross1)[above], (in1, cross1)[below]

        @pl.when(flags[0] == tick - 1)
        def _():
            fresh = tick == 1
            run(
                1, fresh, clip if fresh else own, in1 if fresh else inner, cross1 if fresh else cross,
                starts[-1] if fresh else 0,
                lambda level: (sums_c, level) if level < cut else (sums_d, level - cut), messages1,
            )


def in_vmem(count):
    return [pl.BlockSpec(memory_space=pltpu.VMEM)] * count


def anywhere():
    return pl.BlockSpec(memory_space=pl.ANY)


def in_smem():
    return pl.BlockSpec(memory_space=pltpu.SMEM)


def history_call(first, last, flags, clip, caches, weights, *more):
    layers, _, rows, width, channels = caches.shape
    count = last - first
    sums = jax.ShapeDtypeStruct((count, rows + 2, width, channels), BF16)
    final = last == layers

    def message(band, *levels):
        return [jax.ShapeDtypeStruct((message_starts(layers, *levels)[-1] + band, width, channels), BF16)] * 2

    outs = [sums, sums] + message(0 if final else rows, first, last) + (message(rows) if final else [])
    specs = in_vmem(len(outs))
    if not final:
        outs.append(jax.ShapeDtypeStruct(clip.shape, BF16))
        specs.append(anywhere())
    pixels = count * (rows + 2) * width
    return pl.pallas_call(
        functools.partial(history_kernel, first, last),
        out_shape=tuple(outs),
        in_specs=[in_smem(), anywhere(), anywhere(), anywhere()] + in_vmem(len(more)),
        out_specs=tuple(specs),
        scratch_shapes=[
            pltpu.VMEM((count,) + caches.shape[1:], BF16),
            pltpu.VMEM((count, 9, 2, channels, channels), BF16),
            pltpu.VMEM((2, rows + 4, width, 3 * channels), BF16),
            pltpu.SemaphoreType.DMA((max(count, 2), 3)),
        ],
        compiler_params=pltpu.CompilerParams(vmem_limit_bytes=HISTORY_LIMIT),
        cost_estimate=pl.CostEstimate(
            flops=pixels * 27 * 2 * channels * channels, bytes_accessed=4000000, transcendentals=0
        ),
        name="history",
    )(flags, clip, caches, weights, *more)


def tick_call(tick, segments, bands, cut, flags, clip, own, inner, cross, weights, biases, sums0, sums1, behind, done):
    layers, _, _, channels, _ = weights.shape
    rows, width = clip.shape[1:3]
    every = (layers, 3 * rows, width, channels)
    pixels = sum(rows + 2 * level for level in range(layers)) * width
    zero, one = tick < segments, tick > 0
    extra = (list(sums0) if zero else []) + (list(sums1) + [behind] if one else [])
    outs = [jax.ShapeDtypeStruct((rows, width, channels), BF16)]
    if zero:
        outs.append(jax.ShapeDtypeStruct(every, BF16))
    specs = in_vmem(len(outs)) + [anywhere()]
    outs.append(jax.ShapeDtypeStruct(done.shape, BF16))
    return pl.pallas_call(
        functools.partial(tick_kernel, tick, segments, bands, cut),
        out_shape=tuple(outs),
        in_specs=[in_smem()] + in_vmem(6 + len(extra)) + [anywhere()],
        out_specs=tuple(specs),
        scratch_shapes=[
            pltpu.VMEM((3 * rows, width, channels), BF16),
            pltpu.VMEM((3 * rows, width, 3 * channels), BF16),
            pltpu.VMEM((3 * rows, width, 3 * channels), BF16),
            pltpu.VMEM((2 * width, 2 * channels), F32),
            pltpu.VMEM(every, BF16),
            pltpu.SemaphoreType.DMA,
        ],
        input_output_aliases={7 + len(extra): len(outs) - 1},
        compiler_params=pltpu.CompilerParams(vmem_limit_bytes=LIMIT),
        cost_estimate=pl.CostEstimate(
            flops=pixels * 18 * 2 * channels * channels, bytes_accessed=4000000, transcendentals=pixels * channels
        ),
        name="tick",
    )(flags, clip, own, inner, cross, weights, biases, *extra, done)


def per_device(clip, caches, weights, biases, section_layers):
    segments = lax.axis_size("segment")
    bands = lax.axis_size("band")
    caches, weights, biases = caches[0], weights[0], biases[0]
    layers = weights.shape[0]
    cut = layers // 2
    flags = jnp.stack([lax.axis_index("segment"), lax.axis_index("band"), section_layers[0]]).astype(jnp.int32)
    axes = ("segment", "band")
    in_chip = [(b, b ^ 1) for b in range(bands)]
    between = [(b, b + 1) for b in range(1, bands - 1, 2)] + [(b + 1, b) for b in range(1, bands - 1, 2)]
    straight = [(b, b) for b in range(bands)]

    def swap(value, pairs, chosen):
        return lax.ppermute(value, axes, [(s * bands + a, s * bands + b) for s in chosen for a, b in pairs])

    def ahead(value, pairs, sources):
        return lax.ppermute(value, axes, [(s * bands + a, (s + 1) * bands + b) for s in sources for a, b in pairs])

    everyone = range(segments)
    sums0a, sums1a, in0a, cross0a, done = history_call(0, cut, flags, clip, caches, weights)
    cross0a = swap(cross0a, between, everyone)
    in0a = swap(in0a, in_chip, everyone)
    sums0b, sums1b, in0b, cross0b, in1, cross1 = history_call(cut, layers, flags, clip, caches, weights, sums1a)
    cross0b = swap(cross0b, between, everyone)
    in0b = swap(in0b, in_chip, everyone)
    cross1 = swap(cross1, between, everyone)
    in1 = swap(in1, in_chip, everyone)
    sums0 = (sums0a, sums0b, in0a, cross0a, in0b, cross0b)
    sums1 = (sums1a, sums1b, in1, cross1)
    own, inner, cross = clip, in0a, cross0a
    behind = None
    for tick in range(segments + 1):
        x, *later, done = tick_call(
            tick, segments, bands, cut, flags, clip, own, inner, cross, weights, biases, sums0, sums1, behind, done
        )
        if tick < segments:
            (behind,) = later
            sources = [s for s in (tick, tick - 1) if 0 <= s < segments - 1]
            own, cross = ahead(x, straight, sources), ahead(x, between, sources)
            inner = swap(own, in_chip, [s + 1 for s in sources])
    return done[None]


def solution(mesh):
    placed = (
        P(None, "band", None, None),
        P("segment", None, None, "band", None, None),
        P("segment", None, None, None, None, None),
        P("segment", None, None),
        P("segment"),
    )
    return jax.shard_map(
        per_device,
        mesh=mesh,
        in_specs=placed,
        out_specs=P("segment", None, "band", None, None),
        check_vma=False,
    )
```

```python
import functools

import jax
import jax.numpy as jnp
from jax import lax
from jax.experimental import pallas as pl
from jax.experimental.pallas import tpu as pltpu
from jax.sharding import PartitionSpec as P

LIMIT = 28 * 1024 * 1024
HISTORY_LIMIT = 52 * 1024 * 1024
F32 = jnp.float32
PAD = 8
BF16 = jnp.bfloat16


def message_starts(layers, first=0, last=None):
    starts = [0]
    for level in range(first, layers if last is None else last):
        starts.append(starts[-1] + layers - level)
    return starts


def taps_into(s_ref, row, a, line):
    width, channels = a.shape
    line[PAD : PAD + width] = a
    s_ref[row, :, 0:channels] = line[PAD - 1 : PAD - 1 + width].astype(BF16)
    s_ref[row, :, channels : 2 * channels] = a.astype(BF16)
    s_ref[row, :, 2 * channels : 3 * channels] = line[PAD + 1 : PAD + 1 + width].astype(BF16)


def clear_lines(lines):
    edge = jnp.zeros((PAD, lines.shape[2]), F32)
    for i in range(lines.shape[0]):
        lines[i, 0:PAD] = edge
        lines[i, lines.shape[1] - PAD :] = edge


def rows_dot(s_ref, first, count, w, layer, times):
    width, depth = s_ref.shape[1:]
    taps = jnp.concatenate([s_ref[pl.ds(first + i, count)].reshape(count * width, depth) for i in range(3)], axis=1)
    weights = jnp.concatenate([jnp.concatenate([w[layer, k, t] for t in times], axis=1) for k in range(9)], axis=0)
    return jnp.dot(taps, weights, preferred_element_type=F32)


def pairs_dot(s_ref, first, count, w, layer, time):
    width, depth = s_ref.shape[1:]
    channels = depth // 3
    taps = jnp.concatenate(
        [jnp.concatenate([s_ref[first + i + 2 * p] for p in range(count)], axis=0) for i in range(4)], axis=1
    )
    zero = jnp.zeros((channels, channels), BF16)

    def tap(i, j):
        return w[layer, 3 * i + j, time] if 0 <= i < 3 else zero

    weights = jnp.concatenate(
        [jnp.concatenate([tap(i, j), tap(i - 1, j)], axis=1) for i in range(4) for j in range(3)], axis=0
    )
    total = jnp.dot(taps, weights, preferred_element_type=F32)
    upper = total[:, :channels].reshape(count, 1, width, channels)
    lower = total[:, channels:].reshape(count, 1, width, channels)
    return jnp.concatenate([upper, lower], axis=1)


def history_kernel(first, last, flags, clip, caches, w, *refs):
    layers, _, rows, width, channels = caches.shape
    final = last == layers
    if final:
        former, sums0, sums1, in0, cross0, in1, cross1, c, wb, s, lines, sems = refs
    else:
        sums0, sums1, in0, cross0, done, c, wb, s, lines, sems = refs

    band_start = message_starts(layers)[-1] if final else message_starts(layers, first, last)[-1]
    clip_copies = [
        pltpu.make_async_copy(clip.at[int(final)], message.at[band_start : band_start + rows], sems.at[i, 2])
        for i, message in enumerate((in1, cross1) if final else (in0, cross0))
    ]
    for copy in clip_copies:
        copy.start()

    begin = layers - flags[2]

    def loads(slot, layer):
        return [
            pltpu.make_async_copy(caches.at[layer], c.at[slot], sems.at[slot, 0]),
            pltpu.make_async_copy(w.at[layer, :, 0:2], wb.at[slot], sems.at[slot, 1]),
        ]

    for level in range(first, last):

        @pl.when(level >= begin)
        def _(level=level):
            for copy in loads(level - first, level - begin):
                copy.start()

    clear_lines(lines)
    for f in range(2):
        s[f, 0:2] = jnp.zeros((2,) + s.shape[2:], BF16)
        s[f, rows + 2 : rows + 4] = jnp.zeros((2,) + s.shape[2:], BF16)

    def level_step(level, _):
        slot = level - first
        for copy in loads(slot, level - begin):
            copy.wait()

        def build(row, _):
            taps_into(s.at[0], row + 2, c[slot, 0, row].astype(F32), lines.at[0])
            taps_into(s.at[1], row + 2, c[slot, 1, row].astype(F32), lines.at[1])
            return 0

        lax.fori_loop(0, rows, build, 0)
        newer = rows_dot(s.at[1], 0, rows + 2, wb, slot, (1, 0))
        older = pairs_dot(s.at[0], 0, (rows + 2) // 2, wb, slot, 0).reshape(rows + 2, width, channels)
        sums0[slot] = (newer[:, :channels].reshape(rows + 2, width, channels) + older).astype(BF16)
        sums1[slot] = newer[:, channels:].reshape(rows + 2, width, channels).astype(BF16)
        return 0

    lax.fori_loop(jnp.maximum(begin, first), last, level_step, 0)

    def pack(of_level, starts, levels, up, down):
        for i, level in enumerate(levels):
            reach = layers - level
            sums, at = of_level(level)
            up[starts[i] : starts[i + 1]] = sums[at, 0:reach]
            down[starts[i] : starts[i + 1]] = sums[at, rows + 2 - reach : rows + 2]

    def messages(up0, down0, up1, down1):
        starts = message_starts(layers, first, last)
        pack(lambda level: (sums0, level - first), starts, range(first, last), up0, down0)
        if final:
            starts = message_starts(layers)
            pack(
                lambda level: (former, level) if level < first else (sums1, level - first),
                starts, range(layers), up1, down1,
            )
    @pl.when(flags[1] % 2 == 0)
    def _():
        messages(cross0, in0, *((cross1, in1) if final else (None, None)))

    @pl.when(flags[1] % 2 != 0)
    def _():
        messages(in0, cross0, *((in1, cross1) if final else (None, None)))

    for copy in clip_copies:
        copy.wait()


def pieces(count):
    parts, at = [], 0
    while at < count:
        step = 4 if count - at in (4, 8) else min(6, count - at)
        parts.append((at, step))
        at += step
    return parts


def tick_kernel(tick, segments, bands, cut, flags, clip, own, inner, cross, w, bias, *refs):
    zero, one = tick < segments, tick > 0
    refs = list(refs)

    def take(count):
        found, refs[:count] = refs[:count], []
        return found

    sums0 = take(6) if zero else None
    sums1 = take(4) if one else None
    behind = take(1)[0] if one else None
    done = take(1)
    x_out = take(1)[0]
    ahead = take(1)[0] if zero else None
    done_out, x, s, lines, part, sem = refs
    rows, width, channels = x_out.shape
    layers = w.shape[0]
    band = flags[1]
    begin = layers - flags[2]
    low = jnp.where(band == 0, rows, 0)
    high = jnp.where(band == bands - 1, 2 * rows, 3 * rows)

    def run(frame, fresh, own, inner, cross, halo, level_sums, level_messages):
        x[rows : 2 * rows] = own[frame] if fresh else own[...]

        def gather(above, below, side_above, side_below):
            x[0:rows] = above[halo : halo + rows]
            x[2 * rows : 3 * rows] = below[halo : halo + rows]
            for level in range(layers):

                @pl.when(level >= begin)
                def _(level=level):
                    reach = layers - level
                    sums, at = level_sums(level)
                    start, sums_above, sums_below = level_messages(level, side_above, side_below)
                    part[level, rows + 1 - reach : rows + 1] = sums_above[start : start + reach]
                    part[level, 2 * rows - 1 : 2 * rows - 1 + reach] = sums_below[start : start + reach]
                    part[level, rows + 1 : 2 * rows - 1] = sums[at, 2:rows]
                    part[level, rows] += sums[at, 1]
                    part[level, 2 * rows - 1] += sums[at, rows]
                    if reach > 1:
                        part[level, rows - 1] += sums[at, 0]
                        part[level, 2 * rows] += sums[at, rows + 1]

        @pl.when(band % 2 == 0)
        def _():
            gather(cross, inner, 1, 0)

        @pl.when(band % 2 != 0)
        def _():
            gather(inner, cross, 0, 1)

        clear_lines(lines)

        def build(row, line):
            half = x[row].astype(F32) * 0.5
            inside = jnp.logical_and(row >= low, row < high).astype(F32)
            taps_into(s, row, (half + half * jnp.tanh(half)) * inside, line)

        for level in range(layers):

            @pl.when(level >= begin)
            def _(level=level):
                layer = level - begin
                first = rows - layers + 1 + level
                count = rows + 2 * (layers - 1 - level)

                def two(i, _):
                    build(first - 1 + 2 * i, lines.at[0])
                    build(first + 2 * i, lines.at[1])
                    return 0

                lax.fori_loop(0, count // 2 + 1, two, 0)
                offset = bias[pl.ds(layer, 1), :].reshape(1, 1, channels)
                for start, step in [(0, count)] if frame == 0 else pieces(count):
                    at = first + start
                    known = part[level, at : at + step].astype(F32) + offset
                    if frame == 0:
                        total = rows_dot(s, at - 1, step, w, layer, (2, 1))
                        mine = total[:, :channels].reshape(step, width, channels)
                        ahead[level, at : at + step] = total[:, channels:].reshape(step, width, channels).astype(BF16)
                    else:
                        mine = pairs_dot(s, at - 1, step // 2, w, layer, 2).reshape(step, width, channels)
                        known = known + behind[level, at : at + step].astype(F32)
                    x[at : at + step] = (x[at : at + step].astype(F32) + (mine + known)).astype(BF16)

        copy = pltpu.make_async_copy(x.at[rows : 2 * rows], done_out.at[frame], sem)
        copy.start()
        x_out[...] = x[rows : 2 * rows]
        copy.wait()

    if zero:
        sums_a, sums_b, in_a, cross_a, in_b, cross_b = sums0
        starts_a, starts_b = message_starts(layers, 0, cut), message_starts(layers, cut)

        def messages0(level, above, below):
            if level < cut:
                return starts_a[level], (in_a, cross_a)[above], (in_a, cross_a)[below]
            return starts_b[level - cut], (in_b, cross_b)[above], (in_b, cross_b)[below]

        @pl.when(flags[0] == tick)
        def _():
            run(
                0, tick == 0, clip if tick == 0 else own, inner, cross, starts_a[-1] if tick == 0 else 0,
                lambda level: (sums_a, level) if level < cut else (sums_b, level - cut), messages0,
            )

    if one:
        sums_c, sums_d, in1, cross1 = sums1
        starts = message_starts(layers)

        def messages1(level, above, below):
            return starts[level], (in1, cross1)[above], (in1, cross1)[below]

        @pl.when(flags[0] == tick - 1)
        def _():
            fresh = tick == 1
            run(
                1, fresh, clip if fresh else own, in1 if fresh else inner, cross1 if fresh else cross,
                starts[-1] if fresh else 0,
                lambda level: (sums_c, level) if level < cut else (sums_d, level - cut), messages1,
            )


def in_vmem(count):
    return [pl.BlockSpec(memory_space=pltpu.VMEM)] * count


def anywhere():
    return pl.BlockSpec(memory_space=pl.ANY)


def in_smem():
    return pl.BlockSpec(memory_space=pltpu.SMEM)


def history_call(first, last, flags, clip, caches, weights, *more):
    layers, _, rows, width, channels = caches.shape
    count = last - first
    sums = jax.ShapeDtypeStruct((count, rows + 2, width, channels), BF16)
    final = last == layers

    def message(band, *levels):
        return [jax.ShapeDtypeStruct((message_starts(layers, *levels)[-1] + band, width, channels), BF16)] * 2

    outs = [sums, sums] + message(0 if final else rows, first, last) + (message(rows) if final else [])
    specs = in_vmem(len(outs))
    if not final:
        outs.append(jax.ShapeDtypeStruct(clip.shape, BF16))
        specs.append(anywhere())
    pixels = count * (rows + 2) * width
    return pl.pallas_call(
        functools.partial(history_kernel, first, last),
        out_shape=tuple(outs),
        in_specs=[in_smem(), anywhere(), anywhere(), anywhere()] + in_vmem(len(more)),
        out_specs=tuple(specs),
        scratch_shapes=[
            pltpu.VMEM((count,) + caches.shape[1:], BF16),
            pltpu.VMEM((count, 9, 2, channels, channels), BF16),
            pltpu.VMEM((2, rows + 4, width, 3 * channels), BF16),
            pltpu.VMEM((2, width + 2 * PAD, channels), F32),
            pltpu.SemaphoreType.DMA((max(count, 2), 3)),
        ],
        compiler_params=pltpu.CompilerParams(vmem_limit_bytes=HISTORY_LIMIT),
        cost_estimate=pl.CostEstimate(
            flops=pixels * 27 * 2 * channels * channels, bytes_accessed=4000000, transcendentals=0
        ),
        name="history",
    )(flags, clip, caches, weights, *more)


def tick_call(tick, segments, bands, cut, flags, clip, own, inner, cross, weights, biases, sums0, sums1, behind, done):
    layers, _, _, channels, _ = weights.shape
    rows, width = clip.shape[1:3]
    every = (layers, 3 * rows, width, channels)
    pixels = sum(rows + 2 * level for level in range(layers)) * width
    zero, one = tick < segments, tick > 0
    extra = (list(sums0) if zero else []) + (list(sums1) + [behind] if one else [])
    outs = [jax.ShapeDtypeStruct((rows, width, channels), BF16)]
    if zero:
        outs.append(jax.ShapeDtypeStruct(every, BF16))
    specs = in_vmem(len(outs)) + [anywhere()]
    outs.append(jax.ShapeDtypeStruct(done.shape, BF16))
    return pl.pallas_call(
        functools.partial(tick_kernel, tick, segments, bands, cut),
        out_shape=tuple(outs),
        in_specs=[in_smem()] + in_vmem(6 + len(extra)) + [anywhere()],
        out_specs=tuple(specs),
        scratch_shapes=[
            pltpu.VMEM((3 * rows, width, channels), BF16),
            pltpu.VMEM((3 * rows, width, 3 * channels), BF16),
            pltpu.VMEM((2, width + 2 * PAD, channels), F32),
            pltpu.VMEM(every, BF16),
            pltpu.SemaphoreType.DMA,
        ],
        input_output_aliases={7 + len(extra): len(outs) - 1},
        compiler_params=pltpu.CompilerParams(vmem_limit_bytes=LIMIT),
        cost_estimate=pl.CostEstimate(
            flops=pixels * 18 * 2 * channels * channels, bytes_accessed=4000000, transcendentals=pixels * channels
        ),
        name="tick",
    )(flags, clip, own, inner, cross, weights, biases, *extra, done)


def per_device(clip, caches, weights, biases, section_layers):
    segments = lax.axis_size("segment")
    bands = lax.axis_size("band")
    caches, weights, biases = caches[0], weights[0], biases[0]
    layers = weights.shape[0]
    cut = layers // 2
    flags = jnp.stack([lax.axis_index("segment"), lax.axis_index("band"), section_layers[0]]).astype(jnp.int32)
    axes = ("segment", "band")
    in_chip = [(b, b ^ 1) for b in range(bands)]
    between = [(b, b + 1) for b in range(1, bands - 1, 2)] + [(b + 1, b) for b in range(1, bands - 1, 2)]
    straight = [(b, b) for b in range(bands)]

    def swap(value, pairs, chosen):
        return lax.ppermute(value, axes, [(s * bands + a, s * bands + b) for s in chosen for a, b in pairs])

    def ahead(value, pairs, sources):
        return lax.ppermute(value, axes, [(s * bands + a, (s + 1) * bands + b) for s in sources for a, b in pairs])

    everyone = range(segments)
    sums0a, sums1a, in0a, cross0a, done = history_call(0, cut, flags, clip, caches, weights)
    cross0a = swap(cross0a, between, everyone)
    in0a = swap(in0a, in_chip, everyone)
    sums0b, sums1b, in0b, cross0b, in1, cross1 = history_call(cut, layers, flags, clip, caches, weights, sums1a)
    cross0b = swap(cross0b, between, everyone)
    in0b = swap(in0b, in_chip, everyone)
    cross1 = swap(cross1, between, everyone)
    in1 = swap(in1, in_chip, everyone)
    sums0 = (sums0a, sums0b, in0a, cross0a, in0b, cross0b)
    sums1 = (sums1a, sums1b, in1, cross1)
    own, inner, cross = clip, in0a, cross0a
    behind = None
    for tick in range(segments + 1):
        x, *later, done = tick_call(
            tick, segments, bands, cut, flags, clip, own, inner, cross, weights, biases, sums0, sums1, behind, done
        )
        if tick < segments:
            (behind,) = later
            sources = [s for s in (tick, tick - 1) if 0 <= s < segments - 1]
            own, cross = ahead(x, straight, sources), ahead(x, between, sources)
            inner = swap(own, in_chip, [s + 1 for s in sources])
    return done[None]


def solution(mesh):
    placed = (
        P(None, "band", None, None),
        P("segment", None, None, "band", None, None),
        P("segment", None, None, None, None, None),
        P("segment", None, None),
        P("segment"),
    )
    return jax.shard_map(
        per_device,
        mesh=mesh,
        in_specs=placed,
        out_specs=P("segment", None, "band", None, None),
        check_vma=False,
    )
```

```python
import functools

import jax
import jax.numpy as jnp
from jax import lax
from jax.experimental import pallas as pl
from jax.experimental.pallas import tpu as pltpu
from jax.sharding import PartitionSpec as P

LIMIT = 28 * 1024 * 1024
HISTORY_LIMIT = 52 * 1024 * 1024
F32 = jnp.float32
PAD = 8
BF16 = jnp.bfloat16


def message_starts(layers, first=0, last=None):
    starts = [0]
    for level in range(first, layers if last is None else last):
        starts.append(starts[-1] + layers - level)
    return starts


def taps_into(s_ref, row, a, line):
    width, channels = a.shape
    line[PAD : PAD + width] = a
    s_ref[row, :, 0:channels] = line[PAD - 1 : PAD - 1 + width].astype(BF16)
    s_ref[row, :, channels : 2 * channels] = a.astype(BF16)
    s_ref[row, :, 2 * channels : 3 * channels] = line[PAD + 1 : PAD + 1 + width].astype(BF16)


def clear_lines(lines):
    edge = jnp.zeros((PAD, lines.shape[2]), F32)
    for i in range(lines.shape[0]):
        lines[i, 0:PAD] = edge
        lines[i, lines.shape[1] - PAD :] = edge


def rows_dot(s_ref, first, count, w, layer, times):
    width, depth = s_ref.shape[1:]
    taps = jnp.concatenate([s_ref[pl.ds(first + i, count)].reshape(count * width, depth) for i in range(3)], axis=1)
    weights = jnp.concatenate([jnp.concatenate([w[layer, k, t] for t in times], axis=1) for k in range(9)], axis=0)
    return jnp.dot(taps, weights, preferred_element_type=F32)


def pairs_dot(s_ref, first, count, w, layer, time):
    width, depth = s_ref.shape[1:]
    channels = depth // 3
    taps = jnp.concatenate(
        [jnp.concatenate([s_ref[first + i + 2 * p] for p in range(count)], axis=0) for i in range(4)], axis=1
    )
    zero = jnp.zeros((channels, channels), BF16)

    def tap(i, j):
        return w[layer, 3 * i + j, time] if 0 <= i < 3 else zero

    weights = jnp.concatenate(
        [jnp.concatenate([tap(i, j), tap(i - 1, j)], axis=1) for i in range(4) for j in range(3)], axis=0
    )
    total = jnp.dot(taps, weights, preferred_element_type=F32)
    upper = total[:, :channels].reshape(count, 1, width, channels)
    lower = total[:, channels:].reshape(count, 1, width, channels)
    return jnp.concatenate([upper, lower], axis=1)


def history_kernel(first, last, flags, caches, w, *refs):
    layers, _, rows, width, channels = caches.shape
    final = last == layers
    if final:
        former, sums0, sums1, in0, cross0, in1, cross1, s, lines = refs
        c, wb = caches, w
    else:
        sums0, sums1, in0, cross0, done, c, wb, s, lines, sems = refs

    begin = layers - flags[2]

    def loads(slot, layer):
        return [
            pltpu.make_async_copy(caches.at[layer], c.at[slot], sems.at[slot, 0]),
            pltpu.make_async_copy(w.at[layer, :, 0:2], wb.at[slot], sems.at[slot, 1]),
        ]

    if not final:
        for level in range(first, last):

            @pl.when(level >= begin)
            def _(level=level):
                for copy in loads(level - first, level - begin):
                    copy.start()

    clear_lines(lines)
    for f in range(2):
        s[f, 0:2] = jnp.zeros((2,) + s.shape[2:], BF16)
        s[f, rows + 2 : rows + 4] = jnp.zeros((2,) + s.shape[2:], BF16)

    def level_step(level, _):
        slot = level - first
        held = slot
        if final:
            held = level - begin
        else:
            for copy in loads(slot, level - begin):
                copy.wait()

        def build(row, _):
            taps_into(s.at[0], row + 2, c[held, 0, row].astype(F32), lines.at[0])
            taps_into(s.at[1], row + 2, c[held, 1, row].astype(F32), lines.at[1])
            return 0

        lax.fori_loop(0, rows, build, 0)
        newer = rows_dot(s.at[1], 0, rows + 2, wb, held, (1, 0))
        older = pairs_dot(s.at[0], 0, (rows + 2) // 2, wb, held, 0).reshape(rows + 2, width, channels)
        sums0[slot] = (newer[:, :channels].reshape(rows + 2, width, channels) + older).astype(BF16)
        sums1[slot] = newer[:, channels:].reshape(rows + 2, width, channels).astype(BF16)
        return 0

    lax.fori_loop(jnp.maximum(begin, first), last, level_step, 0)

    def pack(of_level, starts, levels, up, down):
        for i, level in enumerate(levels):
            reach = layers - level
            sums, at = of_level(level)
            up[starts[i] : starts[i + 1]] = sums[at, 0:reach]
            down[starts[i] : starts[i + 1]] = sums[at, rows + 2 - reach : rows + 2]

    def messages(up0, down0, up1, down1):
        starts = message_starts(layers, first, last)
        pack(lambda level: (sums0, level - first), starts, range(first, last), up0, down0)
        if final:
            starts = message_starts(layers)
            pack(
                lambda level: (former, level) if level < first else (sums1, level - first),
                starts, range(layers), up1, down1,
            )
    @pl.when(flags[1] % 2 == 0)
    def _():
        messages(cross0, in0, *((cross1, in1) if final else (None, None)))

    @pl.when(flags[1] % 2 != 0)
    def _():
        messages(in0, cross0, *((in1, cross1) if final else (None, None)))


def pieces(count):
    parts, at = [], 0
    while at < count:
        step = 4 if count - at in (4, 8) else min(6, count - at)
        parts.append((at, step))
        at += step
    return parts


def tick_kernel(tick, segments, bands, cut, flags, w, bias, *refs):
    zero, one = tick < segments, tick > 0
    refs = list(refs)

    def take(count):
        found, refs[:count] = refs[:count], []
        return found

    clip = take(3) if tick < 2 else None
    own, inner, cross = take(3) if one else (None, None, None)
    sums0 = take(6) if zero else None
    sums1 = take(4) if one else None
    behind = take(1)[0] if one else None
    done = take(1)
    x_out = take(1)[0]
    ahead = take(1)[0] if zero else None
    done_out, x, s, lines, part, sem = refs
    rows, width, channels = x_out.shape
    layers = w.shape[0]
    band = flags[1]
    begin = layers - flags[2]
    low = jnp.where(band == 0, rows, 0)
    high = jnp.where(band == bands - 1, 2 * rows, 3 * rows)

    def run(frame, fresh, own, inner, cross, level_sums, level_messages):
        def of(source):
            return source[frame] if fresh else source[...]

        x[rows : 2 * rows] = of(own)

        def gather(above, below, side_above, side_below):
            x[0:rows] = of(above)
            x[2 * rows : 3 * rows] = of(below)
            for level in range(layers):

                @pl.when(level >= begin)
                def _(level=level):
                    reach = layers - level
                    sums, at = level_sums(level)
                    start, sums_above, sums_below = level_messages(level, side_above, side_below)
                    part[level, rows + 1 - reach : rows + 1] = sums_above[start : start + reach]
                    part[level, 2 * rows - 1 : 2 * rows - 1 + reach] = sums_below[start : start + reach]
                    part[level, rows + 1 : 2 * rows - 1] = sums[at, 2:rows]
                    part[level, rows] += sums[at, 1]
                    part[level, 2 * rows - 1] += sums[at, rows]
                    if reach > 1:
                        part[level, rows - 1] += sums[at, 0]
                        part[level, 2 * rows] += sums[at, rows + 1]

        @pl.when(band % 2 == 0)
        def _():
            gather(cross, inner, 1, 0)

        @pl.when(band % 2 != 0)
        def _():
            gather(inner, cross, 0, 1)

        clear_lines(lines)

        def build(row, line):
            half = x[row].astype(F32) * 0.5
            inside = jnp.logical_and(row >= low, row < high).astype(F32)
            taps_into(s, row, (half + half * jnp.tanh(half)) * inside, line)

        for level in range(layers):

            @pl.when(level >= begin)
            def _(level=level):
                layer = level - begin
                first = rows - layers + 1 + level
                count = rows + 2 * (layers - 1 - level)

                def two(i, _):
                    build(first - 1 + 2 * i, lines.at[0])
                    build(first + 2 * i, lines.at[1])
                    return 0

                lax.fori_loop(0, count // 2 + 1, two, 0)
                offset = bias[pl.ds(layer, 1), :].reshape(1, 1, channels)
                for start, step in [(0, count)] if frame == 0 else pieces(count):
                    at = first + start
                    known = part[level, at : at + step].astype(F32) + offset
                    if frame == 0:
                        total = rows_dot(s, at - 1, step, w, layer, (2, 1))
                        mine = total[:, :channels].reshape(step, width, channels)
                        ahead[level, at : at + step] = total[:, channels:].reshape(step, width, channels).astype(BF16)
                    else:
                        mine = pairs_dot(s, at - 1, step // 2, w, layer, 2).reshape(step, width, channels)
                        known = known + behind[level, at : at + step].astype(F32)
                    x[at : at + step] = (x[at : at + step].astype(F32) + (mine + known)).astype(BF16)

        copy = pltpu.make_async_copy(x.at[rows : 2 * rows], done_out.at[frame], sem)
        copy.start()
        x_out[...] = x[rows : 2 * rows]
        copy.wait()

    if zero:
        sums_a, sums_b, in_a, cross_a, in_b, cross_b = sums0
        starts_a, starts_b = message_starts(layers, 0, cut), message_starts(layers, cut)

        def messages0(level, above, below):
            if level < cut:
                return starts_a[level], (in_a, cross_a)[above], (in_a, cross_a)[below]
            return starts_b[level - cut], (in_b, cross_b)[above], (in_b, cross_b)[below]

        @pl.when(flags[0] == tick)
        def _():
            run(
                0, tick == 0, clip[0] if tick == 0 else own, clip[1] if tick == 0 else inner,
                clip[2] if tick == 0 else cross,
                lambda level: (sums_a, level) if level < cut else (sums_b, level - cut), messages0,
            )

    if one:
        sums_c, sums_d, in1, cross1 = sums1
        starts = message_starts(layers)

        def messages1(level, above, below):
            return starts[level], (in1, cross1)[above], (in1, cross1)[below]

        @pl.when(flags[0] == tick - 1)
        def _():
            fresh = tick == 1
            run(
                1, fresh, clip[0] if fresh else own, clip[1] if fresh else inner, clip[2] if fresh else cross,
                lambda level: (sums_c, level) if level < cut else (sums_d, level - cut), messages1,
            )


def in_vmem(count):
    return [pl.BlockSpec(memory_space=pltpu.VMEM)] * count


def anywhere():
    return pl.BlockSpec(memory_space=pl.ANY)


def in_smem():
    return pl.BlockSpec(memory_space=pltpu.SMEM)


def history_call(first, last, flags, clip, caches, weights, *more):
    layers, _, rows, width, channels = caches.shape
    count = last - first
    sums = jax.ShapeDtypeStruct((count, rows + 2, width, channels), BF16)
    final = last == layers

    def message(*levels):
        return [jax.ShapeDtypeStruct((message_starts(layers, *levels)[-1], width, channels), BF16)] * 2

    outs = [sums, sums] + message(first, last) + (message() if final else [])
    specs = in_vmem(len(outs))
    scratch = [
        pltpu.VMEM((2, rows + 4, width, 3 * channels), BF16),
        pltpu.VMEM((2, width + 2 * PAD, channels), F32),
    ]
    if not final:
        outs.append(jax.ShapeDtypeStruct(clip.shape, BF16))
        specs.append(anywhere())
        scratch = [
            pltpu.VMEM((count,) + caches.shape[1:], BF16),
            pltpu.VMEM((count, 9, 2, channels, channels), BF16),
            *scratch,
            pltpu.SemaphoreType.DMA((count, 2)),
        ]
    pixels = count * (rows + 2) * width
    return pl.pallas_call(
        functools.partial(history_kernel, first, last),
        out_shape=tuple(outs),
        in_specs=[in_smem()] + (in_vmem(2) if final else [anywhere()] * 2) + in_vmem(len(more)),
        out_specs=tuple(specs),
        scratch_shapes=scratch,
        compiler_params=pltpu.CompilerParams(vmem_limit_bytes=LIMIT if final else HISTORY_LIMIT),
        cost_estimate=pl.CostEstimate(
            flops=pixels * 27 * 2 * channels * channels, bytes_accessed=4000000, transcendentals=0
        ),
        name="history",
    )(flags, caches, weights, *more)


def tick_call(tick, segments, bands, cut, flags, clip, received, weights, biases, sums0, sums1, behind, done):
    layers, _, _, channels, _ = weights.shape
    rows, width = done.shape[1:3]
    every = (layers, 3 * rows, width, channels)
    pixels = sum(rows + 2 * level for level in range(layers)) * width
    zero, one = tick < segments, tick > 0
    extra = (list(clip) if tick < 2 else []) + (list(received) if one else [])
    extra += (list(sums0) if zero else []) + (list(sums1) + [behind] if one else [])
    outs = [jax.ShapeDtypeStruct((rows, width, channels), BF16)]
    if zero:
        outs.append(jax.ShapeDtypeStruct(every, BF16))
    specs = in_vmem(len(outs)) + [anywhere()]
    outs.append(jax.ShapeDtypeStruct(done.shape, BF16))
    return pl.pallas_call(
        functools.partial(tick_kernel, tick, segments, bands, cut),
        out_shape=tuple(outs),
        in_specs=[in_smem()] + in_vmem(2 + len(extra)) + [anywhere()],
        out_specs=tuple(specs),
        scratch_shapes=[
            pltpu.VMEM((3 * rows, width, channels), BF16),
            pltpu.VMEM((3 * rows, width, 3 * channels), BF16),
            pltpu.VMEM((2, width + 2 * PAD, channels), F32),
            pltpu.VMEM(every, BF16),
            pltpu.SemaphoreType.DMA,
        ],
        input_output_aliases={3 + len(extra): len(outs) - 1},
        compiler_params=pltpu.CompilerParams(vmem_limit_bytes=LIMIT),
        cost_estimate=pl.CostEstimate(
            flops=pixels * 18 * 2 * channels * channels, bytes_accessed=4000000, transcendentals=pixels * channels
        ),
        name="tick",
    )(flags, weights, biases, *extra, done)


def per_device(clip, caches, weights, biases, section_layers):
    segments = lax.axis_size("segment")
    bands = lax.axis_size("band")
    caches, weights, biases = caches[0], weights[0], biases[0]
    layers = weights.shape[0]
    cut = layers // 2
    flags = jnp.stack([lax.axis_index("segment"), lax.axis_index("band"), section_layers[0]]).astype(jnp.int32)
    axes = ("segment", "band")
    in_chip = [(b, b ^ 1) for b in range(bands)]
    between = [(b, b + 1) for b in range(1, bands - 1, 2)] + [(b + 1, b) for b in range(1, bands - 1, 2)]
    straight = [(b, b) for b in range(bands)]

    def swap(value, pairs, chosen):
        return lax.ppermute(value, axes, [(s * bands + a, s * bands + b) for s in chosen for a, b in pairs])

    def ahead(value, pairs, sources):
        return lax.ppermute(value, axes, [(s * bands + a, (s + 1) * bands + b) for s in sources for a, b in pairs])

    everyone = range(segments)
    clip_cross = swap(clip, between, [0])
    clip_in = swap(clip, in_chip, [0])
    sums0a, sums1a, in0a, cross0a, done = history_call(0, cut, flags, clip, caches, weights)
    cross0a = swap(cross0a, between, everyone)
    in0a = swap(in0a, in_chip, everyone)
    former, clip_cross, clip_in = lax.optimization_barrier((sums1a, clip_cross, clip_in))
    sums0b, sums1b, in0b, cross0b, in1, cross1 = history_call(cut, layers, flags, clip, caches, weights, former)
    cross0b = swap(cross0b, between, everyone)
    in0b = swap(in0b, in_chip, everyone)
    cross1 = swap(cross1, between, everyone)
    in1 = swap(in1, in_chip, everyone)
    sums0 = (sums0a, sums0b, in0a, cross0a, in0b, cross0b)
    sums1 = (sums1a, sums1b, in1, cross1)
    halves = (clip, clip_in, clip_cross)
    received = behind = None
    for tick in range(segments + 1):
        x, *later, done = tick_call(
            tick, segments, bands, cut, flags, halves, received, weights, biases, sums0, sums1, behind, done
        )
        if tick < segments:
            (behind,) = later
            sources = [s for s in (tick, tick - 1) if 0 <= s < segments - 1]
            own, cross = ahead(x, straight, sources), ahead(x, between, sources)
            received = (own, swap(own, in_chip, [s + 1 for s in sources]), cross)
    return done[None]


def solution(mesh):
    placed = (
        P(None, "band", None, None),
        P("segment", None, None, "band", None, None),
        P("segment", None, None, None, None, None),
        P("segment", None, None),
        P("segment"),
    )
    return jax.shard_map(
        per_device,
        mesh=mesh,
        in_specs=placed,
        out_specs=P("segment", None, "band", None, None),
        check_vma=False,
    )
```

```python
import functools

import jax
import jax.numpy as jnp
from jax import lax
from jax.experimental import pallas as pl
from jax.experimental.pallas import tpu as pltpu
from jax.sharding import PartitionSpec as P

LIMIT = 28 * 1024 * 1024
HISTORY_LIMIT = 52 * 1024 * 1024
F32 = jnp.float32
PAD = 8
BF16 = jnp.bfloat16


def message_starts(layers, first=0, last=None):
    starts = [0]
    for level in range(first, layers if last is None else last):
        starts.append(starts[-1] + layers - level)
    return starts


def taps_into(s_ref, row, a, line):
    width, channels = a.shape
    line[PAD : PAD + width] = a
    s_ref[row, :, 0:channels] = line[PAD - 1 : PAD - 1 + width].astype(BF16)
    s_ref[row, :, channels : 2 * channels] = a.astype(BF16)
    s_ref[row, :, 2 * channels : 3 * channels] = line[PAD + 1 : PAD + 1 + width].astype(BF16)


def clear_lines(lines):
    edge = jnp.zeros((PAD, lines.shape[2]), F32)
    for i in range(lines.shape[0]):
        lines[i, 0:PAD] = edge
        lines[i, lines.shape[1] - PAD :] = edge


def rows_dot(s_ref, first, count, w, layer, times):
    width, depth = s_ref.shape[1:]
    taps = jnp.concatenate([s_ref[pl.ds(first + i, count)].reshape(count * width, depth) for i in range(3)], axis=1)
    weights = jnp.concatenate([jnp.concatenate([w[layer, k, t] for t in times], axis=1) for k in range(9)], axis=0)
    return jnp.dot(taps, weights, preferred_element_type=F32)


def pairs_dot(s_ref, first, count, w, layer, time):
    width, depth = s_ref.shape[1:]
    channels = depth // 3
    taps = jnp.concatenate(
        [jnp.concatenate([s_ref[first + i + 2 * p] for p in range(count)], axis=0) for i in range(4)], axis=1
    )
    zero = jnp.zeros((channels, channels), BF16)

    def tap(i, j):
        return w[layer, 3 * i + j, time] if 0 <= i < 3 else zero

    weights = jnp.concatenate(
        [jnp.concatenate([tap(i, j), tap(i - 1, j)], axis=1) for i in range(4) for j in range(3)], axis=0
    )
    total = jnp.dot(taps, weights, preferred_element_type=F32)
    upper = total[:, :channels].reshape(count, 1, width, channels)
    lower = total[:, channels:].reshape(count, 1, width, channels)
    return jnp.concatenate([upper, lower], axis=1)


def history_kernel(first, last, flags, caches, w, *refs):
    layers, _, rows, width, channels = caches.shape
    final = last == layers
    if final:
        former, sums0, sums1, in0, cross0, in1, cross1, s, lines = refs
        c, wb = caches, w
    else:
        sums0, sums1, in0, cross0, done, c, wb, s, lines, sems = refs

    begin = layers - flags[2]

    def loads(slot, layer):
        return [
            pltpu.make_async_copy(caches.at[layer], c.at[slot], sems.at[slot, 0]),
            pltpu.make_async_copy(w.at[layer, :, 0:2], wb.at[slot], sems.at[slot, 1]),
        ]

    if not final:
        for level in range(first, last):

            @pl.when(level >= begin)
            def _(level=level):
                for copy in loads(level - first, level - begin):
                    copy.start()

    clear_lines(lines)
    for f in range(2):
        s[f, 0:2] = jnp.zeros((2,) + s.shape[2:], BF16)
        s[f, rows + 2 : rows + 4] = jnp.zeros((2,) + s.shape[2:], BF16)

    def level_step(level, _):
        slot = level - first
        held = slot
        if final:
            held = level - begin
        else:
            history, taps = loads(slot, level - begin)
            history.wait()

        def build(row, _):
            taps_into(s.at[0], row + 2, c[held, 0, row].astype(F32), lines.at[0])
            taps_into(s.at[1], row + 2, c[held, 1, row].astype(F32), lines.at[1])
            return 0

        lax.fori_loop(0, rows, build, 0)
        if not final:
            taps.wait()
        newer = rows_dot(s.at[1], 0, rows + 2, wb, held, (1, 0))
        older = pairs_dot(s.at[0], 0, (rows + 2) // 2, wb, held, 0).reshape(rows + 2, width, channels)
        sums0[slot] = (newer[:, :channels].reshape(rows + 2, width, channels) + older).astype(BF16)
        sums1[slot] = newer[:, channels:].reshape(rows + 2, width, channels).astype(BF16)
        return 0

    lax.fori_loop(jnp.maximum(begin, first), last, level_step, 0)

    def pack(of_level, starts, levels, up, down):
        for i, level in enumerate(levels):
            reach = layers - level
            sums, at = of_level(level)
            up[starts[i] : starts[i + 1]] = sums[at, 0:reach]
            down[starts[i] : starts[i + 1]] = sums[at, rows + 2 - reach : rows + 2]

    def messages(up0, down0, up1, down1):
        starts = message_starts(layers, first, last)
        pack(lambda level: (sums0, level - first), starts, range(first, last), up0, down0)
        if final:
            starts = message_starts(layers)
            pack(
                lambda level: (former, level) if level < first else (sums1, level - first),
                starts, range(layers), up1, down1,
            )
    @pl.when(flags[1] % 2 == 0)
    def _():
        messages(cross0, in0, *((cross1, in1) if final else (None, None)))

    @pl.when(flags[1] % 2 != 0)
    def _():
        messages(in0, cross0, *((in1, cross1) if final else (None, None)))


def pieces(count):
    parts, at = [], 0
    while at < count:
        step = 4 if count - at in (4, 8) else min(6, count - at)
        parts.append((at, step))
        at += step
    return parts


def tick_kernel(tick, segments, bands, cut, flags, w, bias, *refs):
    zero, one = tick < segments, tick > 0
    refs = list(refs)

    def take(count):
        found, refs[:count] = refs[:count], []
        return found

    clip = take(3) if tick < 2 else None
    own, inner, cross = take(3) if one else (None, None, None)
    sums0 = take(6) if zero else None
    sums1 = take(4) if one else None
    behind = take(1)[0] if one else None
    done = take(1)
    x_out = take(1)[0]
    ahead = take(1)[0] if zero else None
    done_out, x, s, lines, part, sem = refs
    rows, width, channels = x_out.shape
    layers = w.shape[0]
    band = flags[1]
    begin = layers - flags[2]
    low = jnp.where(band == 0, rows, 0)
    high = jnp.where(band == bands - 1, 2 * rows, 3 * rows)

    def run(frame, fresh, own, inner, cross, level_sums, level_messages):
        def of(source):
            return source[frame] if fresh else source[...]

        x[rows : 2 * rows] = of(own)

        def gather(above, below, side_above, side_below):
            x[0:rows] = of(above)
            x[2 * rows : 3 * rows] = of(below)
            for level in range(layers):

                @pl.when(level >= begin)
                def _(level=level):
                    reach = layers - level
                    sums, at = level_sums(level)
                    start, sums_above, sums_below = level_messages(level, side_above, side_below)
                    part[level, rows + 1 - reach : rows + 1] = sums_above[start : start + reach]
                    part[level, 2 * rows - 1 : 2 * rows - 1 + reach] = sums_below[start : start + reach]
                    part[level, rows + 1 : 2 * rows - 1] = sums[at, 2:rows]
                    part[level, rows] += sums[at, 1]
                    part[level, 2 * rows - 1] += sums[at, rows]
                    if reach > 1:
                        part[level, rows - 1] += sums[at, 0]
                        part[level, 2 * rows] += sums[at, rows + 1]

        @pl.when(band % 2 == 0)
        def _():
            gather(cross, inner, 1, 0)

        @pl.when(band % 2 != 0)
        def _():
            gather(inner, cross, 0, 1)

        clear_lines(lines)

        def build(row, line):
            half = x[row].astype(F32) * 0.5
            inside = jnp.logical_and(row >= low, row < high).astype(F32)
            taps_into(s, row, (half + half * jnp.tanh(half)) * inside, line)

        for level in range(layers):

            @pl.when(level >= begin)
            def _(level=level):
                layer = level - begin
                first = rows - layers + 1 + level
                count = rows + 2 * (layers - 1 - level)

                def two(i, _):
                    build(first - 1 + 2 * i, lines.at[0])
                    build(first + 2 * i, lines.at[1])
                    return 0

                lax.fori_loop(0, count // 2 + 1, two, 0)
                offset = bias[pl.ds(layer, 1), :].reshape(1, 1, channels)
                for start, step in [(0, count)] if frame == 0 else pieces(count):
                    at = first + start
                    known = part[level, at : at + step].astype(F32) + offset
                    if frame == 0:
                        total = rows_dot(s, at - 1, step, w, layer, (2, 1))
                        mine = total[:, :channels].reshape(step, width, channels)
                        ahead[level, at : at + step] = total[:, channels:].reshape(step, width, channels).astype(BF16)
                    else:
                        mine = pairs_dot(s, at - 1, step // 2, w, layer, 2).reshape(step, width, channels)
                        known = known + behind[level, at : at + step].astype(F32)
                    x[at : at + step] = (x[at : at + step].astype(F32) + (mine + known)).astype(BF16)

        copy = pltpu.make_async_copy(x.at[rows : 2 * rows], done_out.at[frame], sem)
        copy.start()
        x_out[...] = x[rows : 2 * rows]
        copy.wait()

    if zero:
        sums_a, sums_b, in_a, cross_a, in_b, cross_b = sums0
        starts_a, starts_b = message_starts(layers, 0, cut), message_starts(layers, cut)

        def messages0(level, above, below):
            if level < cut:
                return starts_a[level], (in_a, cross_a)[above], (in_a, cross_a)[below]
            return starts_b[level - cut], (in_b, cross_b)[above], (in_b, cross_b)[below]

        @pl.when(flags[0] == tick)
        def _():
            run(
                0, tick == 0, clip[0] if tick == 0 else own, clip[1] if tick == 0 else inner,
                clip[2] if tick == 0 else cross,
                lambda level: (sums_a, level) if level < cut else (sums_b, level - cut), messages0,
            )

    if one:
        sums_c, sums_d, in1, cross1 = sums1
        starts = message_starts(layers)

        def messages1(level, above, below):
            return starts[level], (in1, cross1)[above], (in1, cross1)[below]

        @pl.when(flags[0] == tick - 1)
        def _():
            fresh = tick == 1
            run(
                1, fresh, clip[0] if fresh else own, clip[1] if fresh else inner, clip[2] if fresh else cross,
                lambda level: (sums_c, level) if level < cut else (sums_d, level - cut), messages1,
            )


def in_vmem(count):
    return [pl.BlockSpec(memory_space=pltpu.VMEM)] * count


def anywhere():
    return pl.BlockSpec(memory_space=pl.ANY)


def in_smem():
    return pl.BlockSpec(memory_space=pltpu.SMEM)


def history_call(first, last, flags, clip, caches, weights, *more):
    layers, _, rows, width, channels = caches.shape
    count = last - first
    sums = jax.ShapeDtypeStruct((count, rows + 2, width, channels), BF16)
    final = last == layers

    def message(*levels):
        return [jax.ShapeDtypeStruct((message_starts(layers, *levels)[-1], width, channels), BF16)] * 2

    outs = [sums, sums] + message(first, last) + (message() if final else [])
    specs = in_vmem(len(outs))
    scratch = [
        pltpu.VMEM((2, rows + 4, width, 3 * channels), BF16),
        pltpu.VMEM((2, width + 2 * PAD, channels), F32),
    ]
    if not final:
        outs.append(jax.ShapeDtypeStruct(clip.shape, BF16))
        specs.append(anywhere())
        scratch = [
            pltpu.VMEM((count,) + caches.shape[1:], BF16),
            pltpu.VMEM((count, 9, 2, channels, channels), BF16),
            *scratch,
            pltpu.SemaphoreType.DMA((count, 2)),
        ]
    pixels = count * (rows + 2) * width
    return pl.pallas_call(
        functools.partial(history_kernel, first, last),
        out_shape=tuple(outs),
        in_specs=[in_smem()] + (in_vmem(2) if final else [anywhere()] * 2) + in_vmem(len(more)),
        out_specs=tuple(specs),
        scratch_shapes=scratch,
        compiler_params=pltpu.CompilerParams(vmem_limit_bytes=LIMIT if final else HISTORY_LIMIT),
        cost_estimate=pl.CostEstimate(
            flops=pixels * 27 * 2 * channels * channels, bytes_accessed=4000000, transcendentals=0
        ),
        name="history",
    )(flags, caches, weights, *more)


def tick_call(tick, segments, bands, cut, flags, clip, received, weights, biases, sums0, sums1, behind, done):
    layers, _, _, channels, _ = weights.shape
    rows, width = done.shape[1:3]
    every = (layers, 3 * rows, width, channels)
    pixels = sum(rows + 2 * level for level in range(layers)) * width
    zero, one = tick < segments, tick > 0
    extra = (list(clip) if tick < 2 else []) + (list(received) if one else [])
    extra += (list(sums0) if zero else []) + (list(sums1) + [behind] if one else [])
    outs = [jax.ShapeDtypeStruct((rows, width, channels), BF16)]
    if zero:
        outs.append(jax.ShapeDtypeStruct(every, BF16))
    specs = in_vmem(len(outs)) + [anywhere()]
    outs.append(jax.ShapeDtypeStruct(done.shape, BF16))
    return pl.pallas_call(
        functools.partial(tick_kernel, tick, segments, bands, cut),
        out_shape=tuple(outs),
        in_specs=[in_smem()] + in_vmem(2 + len(extra)) + [anywhere()],
        out_specs=tuple(specs),
        scratch_shapes=[
            pltpu.VMEM((3 * rows, width, channels), BF16),
            pltpu.VMEM((3 * rows, width, 3 * channels), BF16),
            pltpu.VMEM((2, width + 2 * PAD, channels), F32),
            pltpu.VMEM(every, BF16),
            pltpu.SemaphoreType.DMA,
        ],
        input_output_aliases={3 + len(extra): len(outs) - 1},
        compiler_params=pltpu.CompilerParams(vmem_limit_bytes=LIMIT),
        cost_estimate=pl.CostEstimate(
            flops=pixels * 18 * 2 * channels * channels, bytes_accessed=4000000, transcendentals=pixels * channels
        ),
        name="tick",
    )(flags, weights, biases, *extra, done)


def per_device(clip, caches, weights, biases, section_layers):
    segments = lax.axis_size("segment")
    bands = lax.axis_size("band")
    caches, weights, biases = caches[0], weights[0], biases[0]
    layers = weights.shape[0]
    cut = layers // 2
    flags = jnp.stack([lax.axis_index("segment"), lax.axis_index("band"), section_layers[0]]).astype(jnp.int32)
    axes = ("segment", "band")
    in_chip = [(b, b ^ 1) for b in range(bands)]
    between = [(b, b + 1) for b in range(1, bands - 1, 2)] + [(b + 1, b) for b in range(1, bands - 1, 2)]
    straight = [(b, b) for b in range(bands)]

    def swap(value, pairs, chosen):
        return lax.ppermute(value, axes, [(s * bands + a, s * bands + b) for s in chosen for a, b in pairs])

    def ahead(value, pairs, sources):
        return lax.ppermute(value, axes, [(s * bands + a, (s + 1) * bands + b) for s in sources for a, b in pairs])

    def lender(value, pairs):
        source = min(1, segments - 1)
        return lax.ppermute(value, axes, [(source * bands + a, b) for a, b in pairs])

    everyone = range(segments)
    clip_cross = lender(clip, between)
    clip_in = lender(clip, in_chip)
    sums0a, sums1a, in0a, cross0a, done = history_call(0, cut, flags, clip, caches, weights)
    cross0a = swap(cross0a, between, everyone)
    in0a = swap(in0a, in_chip, everyone)
    former, clip_cross, clip_in = lax.optimization_barrier((sums1a, clip_cross, clip_in))
    sums0b, sums1b, in0b, cross0b, in1, cross1 = history_call(cut, layers, flags, clip, caches, weights, former)
    cross0b = swap(cross0b, between, everyone)
    in0b = swap(in0b, in_chip, everyone)
    cross1 = swap(cross1, between, everyone)
    in1 = swap(in1, in_chip, everyone)
    sums0 = (sums0a, sums0b, in0a, cross0a, in0b, cross0b)
    sums1 = (sums1a, sums1b, in1, cross1)
    halves = (clip, clip_in, clip_cross)
    received = behind = None
    for tick in range(segments + 1):
        x, *later, done = tick_call(
            tick, segments, bands, cut, flags, halves, received, weights, biases, sums0, sums1, behind, done
        )
        if tick < segments:
            (behind,) = later
            sources = [s for s in (tick, tick - 1) if 0 <= s < segments - 1]
            own, cross = ahead(x, straight, sources), ahead(x, between, sources)
            received = (own, swap(own, in_chip, [s + 1 for s in sources]), cross)
    return done[None]


def solution(mesh):
    placed = (
        P(None, "band", None, None),
        P("segment", None, None, "band", None, None),
        P("segment", None, None, None, None, None),
        P("segment", None, None),
        P("segment"),
    )
    return jax.shard_map(
        per_device,
        mesh=mesh,
        in_specs=placed,
        out_specs=P("segment", None, "band", None, None),
        check_vma=False,
    )
```

```python
import functools

import jax
import jax.numpy as jnp
from jax import lax
from jax.experimental import pallas as pl
from jax.experimental.pallas import tpu as pltpu
from jax.sharding import PartitionSpec as P

LIMIT = 28 * 1024 * 1024
HISTORY_LIMIT = 52 * 1024 * 1024
F32 = jnp.float32
PAD = 8
BF16 = jnp.bfloat16


def message_starts(layers, first=0, last=None):
    starts = [0]
    for level in range(first, layers if last is None else last):
        starts.append(starts[-1] + layers - level)
    return starts


def taps_into(s_ref, row, a, line):
    width, channels = a.shape
    line[PAD : PAD + width] = a
    s_ref[row, :, 0:channels] = line[PAD - 1 : PAD - 1 + width].astype(BF16)
    s_ref[row, :, channels : 2 * channels] = a.astype(BF16)
    s_ref[row, :, 2 * channels : 3 * channels] = line[PAD + 1 : PAD + 1 + width].astype(BF16)


def clear_lines(lines):
    edge = jnp.zeros((PAD, lines.shape[2]), F32)
    for i in range(lines.shape[0]):
        lines[i, 0:PAD] = edge
        lines[i, lines.shape[1] - PAD :] = edge


def rows_dot(s_ref, first, count, w, layer, times):
    width, depth = s_ref.shape[1:]
    taps = jnp.concatenate([s_ref[pl.ds(first + i, count)].reshape(count * width, depth) for i in range(3)], axis=1)
    weights = jnp.concatenate([jnp.concatenate([w[layer, k, t] for t in times], axis=1) for k in range(9)], axis=0)
    return jnp.dot(taps, weights, preferred_element_type=F32)


def pairs_dot(s_ref, first, count, w, layer, time):
    width, depth = s_ref.shape[1:]
    channels = depth // 3
    taps = jnp.concatenate(
        [jnp.concatenate([s_ref[first + i + 2 * p] for p in range(count)], axis=0) for i in range(4)], axis=1
    )
    zero = jnp.zeros((channels, channels), BF16)

    def tap(i, j):
        return w[layer, 3 * i + j, time] if 0 <= i < 3 else zero

    weights = jnp.concatenate(
        [jnp.concatenate([tap(i, j), tap(i - 1, j)], axis=1) for i in range(4) for j in range(3)], axis=0
    )
    total = jnp.dot(taps, weights, preferred_element_type=F32)
    upper = total[:, :channels].reshape(count, 1, width, channels)
    lower = total[:, channels:].reshape(count, 1, width, channels)
    return jnp.concatenate([upper, lower], axis=1)


def history_kernel(first, last, flags, clip, caches, w, *refs):
    layers, _, rows, width, channels = caches.shape
    final = last == layers
    if final:
        former, sums0, sums1, in0, cross0, in1, cross1, s, lines, sems = refs
        c, wb = caches, w
    else:
        sums0, sums1, in0, cross0, done, c, wb, s, lines, sems = refs

    begin = layers - flags[2]
    message = in1 if final else in0
    rest = message_starts(layers)[-1] if final else message_starts(layers, first, last)[-1]
    clip_copy = pltpu.make_async_copy(clip.at[int(final)], message.at[rest : rest + rows], sems.at[0, 2])
    clip_copy.start()

    def loads(slot, layer):
        return [
            pltpu.make_async_copy(caches.at[layer], c.at[slot], sems.at[slot, 0]),
            pltpu.make_async_copy(w.at[layer, :, 0:2], wb.at[slot], sems.at[slot, 1]),
        ]

    if not final:
        for level in range(first, last):

            @pl.when(level >= begin)
            def _(level=level):
                for copy in loads(level - first, level - begin):
                    copy.start()

    clear_lines(lines)
    for f in range(2):
        s[f, 0:2] = jnp.zeros((2,) + s.shape[2:], BF16)
        s[f, rows + 2 : rows + 4] = jnp.zeros((2,) + s.shape[2:], BF16)

    def level_step(level, _):
        slot = level - first
        held = slot
        if final:
            held = level - begin
        else:
            history, taps = loads(slot, level - begin)
            history.wait()

        def build(row, _):
            taps_into(s.at[0], row + 2, c[held, 0, row].astype(F32), lines.at[0])
            taps_into(s.at[1], row + 2, c[held, 1, row].astype(F32), lines.at[1])
            return 0

        lax.fori_loop(0, rows, build, 0)
        if not final:
            taps.wait()
        newer = rows_dot(s.at[1], 0, rows + 2, wb, held, (1, 0))
        older = pairs_dot(s.at[0], 0, (rows + 2) // 2, wb, held, 0).reshape(rows + 2, width, channels)
        sums0[slot] = (newer[:, :channels].reshape(rows + 2, width, channels) + older).astype(BF16)
        sums1[slot] = newer[:, channels:].reshape(rows + 2, width, channels).astype(BF16)
        return 0

    lax.fori_loop(jnp.maximum(begin, first), last, level_step, 0)

    def pack(of_level, starts, levels, up, down):
        for i, level in enumerate(levels):
            reach = layers - level
            sums, at = of_level(level)
            up[starts[i] : starts[i + 1]] = sums[at, 0:reach]
            down[starts[i] : starts[i + 1]] = sums[at, rows + 2 - reach : rows + 2]

    def messages(up0, down0, up1, down1):
        starts = message_starts(layers, first, last)
        pack(lambda level: (sums0, level - first), starts, range(first, last), up0, down0)
        if final:
            starts = message_starts(layers)
            pack(
                lambda level: (former, level) if level < first else (sums1, level - first),
                starts, range(layers), up1, down1,
            )
    @pl.when(flags[1] % 2 == 0)
    def _():
        messages(cross0, in0, *((cross1, in1) if final else (None, None)))

    @pl.when(flags[1] % 2 != 0)
    def _():
        messages(in0, cross0, *((in1, cross1) if final else (None, None)))

    clip_copy.wait()


def pieces(count):
    parts, at = [], 0
    while at < count:
        step = 4 if count - at in (4, 8) else min(6, count - at)
        parts.append((at, step))
        at += step
    return parts


def tick_kernel(tick, segments, bands, cut, flags, w, bias, *refs):
    zero, one = tick < segments, tick > 0
    refs = list(refs)

    def take(count):
        found, refs[:count] = refs[:count], []
        return found

    clip = take(2) if tick < 2 else None
    own, inner, cross = take(3) if one else (None, None, None)
    sums0 = take(6) if zero else None
    sums1 = take(4) if one else None
    behind = take(1)[0] if one else None
    done = take(1)
    x_out = take(1)[0]
    ahead = take(1)[0] if zero else None
    done_out, x, s, lines, part, sem = refs
    rows, width, channels = x_out.shape
    layers = w.shape[0]
    band = flags[1]
    begin = layers - flags[2]
    low = jnp.where(band == 0, rows, 0)
    high = jnp.where(band == bands - 1, 2 * rows, 3 * rows)

    def run(frame, fresh, own, inner, cross, halo, level_sums, level_messages):
        def of(source):
            if source is inner:
                return source[halo : halo + rows]
            return source[frame] if fresh else source[...]

        x[rows : 2 * rows] = of(own)

        def gather(above, below, side_above, side_below):
            x[0:rows] = of(above)
            x[2 * rows : 3 * rows] = of(below)
            for level in range(layers):

                @pl.when(level >= begin)
                def _(level=level):
                    reach = layers - level
                    sums, at = level_sums(level)
                    start, sums_above, sums_below = level_messages(level, side_above, side_below)
                    part[level, rows + 1 - reach : rows + 1] = sums_above[start : start + reach]
                    part[level, 2 * rows - 1 : 2 * rows - 1 + reach] = sums_below[start : start + reach]
                    part[level, rows + 1 : 2 * rows - 1] = sums[at, 2:rows]
                    part[level, rows] += sums[at, 1]
                    part[level, 2 * rows - 1] += sums[at, rows]
                    if reach > 1:
                        part[level, rows - 1] += sums[at, 0]
                        part[level, 2 * rows] += sums[at, rows + 1]

        @pl.when(band % 2 == 0)
        def _():
            gather(cross, inner, 1, 0)

        @pl.when(band % 2 != 0)
        def _():
            gather(inner, cross, 0, 1)

        clear_lines(lines)

        def build(row, line):
            half = x[row].astype(F32) * 0.5
            inside = jnp.logical_and(row >= low, row < high).astype(F32)
            taps_into(s, row, (half + half * jnp.tanh(half)) * inside, line)

        for level in range(layers):

            @pl.when(level >= begin)
            def _(level=level):
                layer = level - begin
                first = rows - layers + 1 + level
                count = rows + 2 * (layers - 1 - level)

                def two(i, _):
                    build(first - 1 + 2 * i, lines.at[0])
                    build(first + 2 * i, lines.at[1])
                    return 0

                lax.fori_loop(0, count // 2 + 1, two, 0)
                offset = bias[pl.ds(layer, 1), :].reshape(1, 1, channels)
                for start, step in [(0, count)] if frame == 0 else pieces(count):
                    at = first + start
                    known = part[level, at : at + step].astype(F32) + offset
                    if frame == 0:
                        total = rows_dot(s, at - 1, step, w, layer, (2, 1))
                        mine = total[:, :channels].reshape(step, width, channels)
                        ahead[level, at : at + step] = total[:, channels:].reshape(step, width, channels).astype(BF16)
                    else:
                        mine = pairs_dot(s, at - 1, step // 2, w, layer, 2).reshape(step, width, channels)
                        known = known + behind[level, at : at + step].astype(F32)
                    x[at : at + step] = (x[at : at + step].astype(F32) + (mine + known)).astype(BF16)

        copy = pltpu.make_async_copy(x.at[rows : 2 * rows], done_out.at[frame], sem)
        copy.start()
        x_out[...] = x[rows : 2 * rows]
        copy.wait()

    if zero:
        sums_a, sums_b, in_a, cross_a, in_b, cross_b = sums0
        starts_a, starts_b = message_starts(layers, 0, cut), message_starts(layers, cut)

        def messages0(level, above, below):
            if level < cut:
                return starts_a[level], (in_a, cross_a)[above], (in_a, cross_a)[below]
            return starts_b[level - cut], (in_b, cross_b)[above], (in_b, cross_b)[below]

        @pl.when(flags[0] == tick)
        def _():
            run(
                0, tick == 0, clip[0] if tick == 0 else own, in_a if tick == 0 else inner,
                clip[1] if tick == 0 else cross, starts_a[-1] if tick == 0 else 0,
                lambda level: (sums_a, level) if level < cut else (sums_b, level - cut), messages0,
            )

    if one:
        sums_c, sums_d, in1, cross1 = sums1
        starts = message_starts(layers)

        def messages1(level, above, below):
            return starts[level], (in1, cross1)[above], (in1, cross1)[below]

        @pl.when(flags[0] == tick - 1)
        def _():
            fresh = tick == 1
            run(
                1, fresh, clip[0] if fresh else own, in1 if fresh else inner, clip[1] if fresh else cross,
                starts[-1] if fresh else 0,
                lambda level: (sums_c, level) if level < cut else (sums_d, level - cut), messages1,
            )


def in_vmem(count):
    return [pl.BlockSpec(memory_space=pltpu.VMEM)] * count


def anywhere():
    return pl.BlockSpec(memory_space=pl.ANY)


def in_smem():
    return pl.BlockSpec(memory_space=pltpu.SMEM)


def history_call(first, last, flags, clip, caches, weights, *more):
    layers, _, rows, width, channels = caches.shape
    count = last - first
    sums = jax.ShapeDtypeStruct((count, rows + 2, width, channels), BF16)
    final = last == layers

    def message(band, *levels):
        reach = message_starts(layers, *levels)[-1]
        return [jax.ShapeDtypeStruct((reach + more, width, channels), BF16) for more in (band, 0)]

    outs = [sums, sums] + message(0 if final else rows, first, last) + (message(rows) if final else [])
    specs = in_vmem(len(outs))
    scratch = [
        pltpu.VMEM((2, rows + 4, width, 3 * channels), BF16),
        pltpu.VMEM((2, width + 2 * PAD, channels), F32),
    ]
    if not final:
        outs.append(jax.ShapeDtypeStruct(clip.shape, BF16))
        specs.append(anywhere())
        scratch = [
            pltpu.VMEM((count,) + caches.shape[1:], BF16),
            pltpu.VMEM((count, 9, 2, channels, channels), BF16),
            *scratch,
        ]
    scratch.append(pltpu.SemaphoreType.DMA((count, 3)))
    pixels = count * (rows + 2) * width
    return pl.pallas_call(
        functools.partial(history_kernel, first, last),
        out_shape=tuple(outs),
        in_specs=[in_smem(), anywhere()] + (in_vmem(2) if final else [anywhere()] * 2) + in_vmem(len(more)),
        out_specs=tuple(specs),
        scratch_shapes=scratch,
        compiler_params=pltpu.CompilerParams(vmem_limit_bytes=LIMIT if final else HISTORY_LIMIT),
        cost_estimate=pl.CostEstimate(
            flops=pixels * 27 * 2 * channels * channels, bytes_accessed=4000000, transcendentals=0
        ),
        name="history",
    )(flags, clip, caches, weights, *more)


def tick_call(tick, segments, bands, cut, flags, clip, received, weights, biases, sums0, sums1, behind, done):
    layers, _, _, channels, _ = weights.shape
    rows, width = done.shape[1:3]
    every = (layers, 3 * rows, width, channels)
    pixels = sum(rows + 2 * level for level in range(layers)) * width
    zero, one = tick < segments, tick > 0
    extra = (list(clip) if tick < 2 else []) + (list(received) if one else [])
    extra += (list(sums0) if zero else []) + (list(sums1) + [behind] if one else [])
    outs = [jax.ShapeDtypeStruct((rows, width, channels), BF16)]
    if zero:
        outs.append(jax.ShapeDtypeStruct(every, BF16))
    specs = in_vmem(len(outs)) + [anywhere()]
    outs.append(jax.ShapeDtypeStruct(done.shape, BF16))
    return pl.pallas_call(
        functools.partial(tick_kernel, tick, segments, bands, cut),
        out_shape=tuple(outs),
        in_specs=[in_smem()] + in_vmem(2 + len(extra)) + [anywhere()],
        out_specs=tuple(specs),
        scratch_shapes=[
            pltpu.VMEM((3 * rows, width, channels), BF16),
            pltpu.VMEM((3 * rows, width, 3 * channels), BF16),
            pltpu.VMEM((2, width + 2 * PAD, channels), F32),
            pltpu.VMEM(every, BF16),
            pltpu.SemaphoreType.DMA,
        ],
        input_output_aliases={3 + len(extra): len(outs) - 1},
        compiler_params=pltpu.CompilerParams(vmem_limit_bytes=LIMIT),
        cost_estimate=pl.CostEstimate(
            flops=pixels * 18 * 2 * channels * channels, bytes_accessed=4000000, transcendentals=pixels * channels
        ),
        name="tick",
    )(flags, weights, biases, *extra, done)


def per_device(clip, caches, weights, biases, section_layers):
    segments = lax.axis_size("segment")
    bands = lax.axis_size("band")
    caches, weights, biases = caches[0], weights[0], biases[0]
    layers = weights.shape[0]
    cut = layers // 2
    flags = jnp.stack([lax.axis_index("segment"), lax.axis_index("band"), section_layers[0]]).astype(jnp.int32)
    axes = ("segment", "band")
    in_chip = [(b, b ^ 1) for b in range(bands)]
    between = [(b, b + 1) for b in range(1, bands - 1, 2)] + [(b + 1, b) for b in range(1, bands - 1, 2)]
    straight = [(b, b) for b in range(bands)]

    def swap(value, pairs, chosen):
        return lax.ppermute(value, axes, [(s * bands + a, s * bands + b) for s in chosen for a, b in pairs])

    def ahead(value, pairs, sources):
        return lax.ppermute(value, axes, [(s * bands + a, (s + 1) * bands + b) for s in sources for a, b in pairs])

    def lender(value, pairs):
        source = min(1, segments - 1)
        return lax.ppermute(value, axes, [(source * bands + a, b) for a, b in pairs])

    everyone = range(segments)
    clip_cross = lender(clip, between)
    sums0a, sums1a, in0a, cross0a, done = history_call(0, cut, flags, clip, caches, weights)
    cross0a = swap(cross0a, between, everyone)
    in0a = swap(in0a, in_chip, everyone)
    former, clip_cross = lax.optimization_barrier((sums1a, clip_cross))
    sums0b, sums1b, in0b, cross0b, in1, cross1 = history_call(cut, layers, flags, clip, caches, weights, former)
    cross0b = swap(cross0b, between, everyone)
    in0b = swap(in0b, in_chip, everyone)
    cross1 = swap(cross1, between, everyone)
    in1 = swap(in1, in_chip, everyone)
    sums0 = (sums0a, sums0b, in0a, cross0a, in0b, cross0b)
    sums1 = (sums1a, sums1b, in1, cross1)
    halves = (clip, clip_cross)
    received = behind = None
    for tick in range(segments + 1):
        x, *later, done = tick_call(
            tick, segments, bands, cut, flags, halves, received, weights, biases, sums0, sums1, behind, done
        )
        if tick < segments:
            (behind,) = later
            sources = [s for s in (tick, tick - 1) if 0 <= s < segments - 1]
            own, cross = ahead(x, straight, sources), ahead(x, between, sources)
            received = (own, swap(own, in_chip, [s + 1 for s in sources]), cross)
    return done[None]


def solution(mesh):
    placed = (
        P(None, "band", None, None),
        P("segment", None, None, "band", None, None),
        P("segment", None, None, None, None, None),
        P("segment", None, None),
        P("segment"),
    )
    return jax.shard_map(
        per_device,
        mesh=mesh,
        in_specs=placed,
        out_specs=P("segment", None, "band", None, None),
        check_vma=False,
    )
```

```python
import functools

import jax
import jax.numpy as jnp
from jax import lax
from jax.experimental import pallas as pl
from jax.experimental.pallas import tpu as pltpu
from jax.sharding import PartitionSpec as P

LIMIT = 28 * 1024 * 1024
HISTORY_LIMIT = 52 * 1024 * 1024
F32 = jnp.float32
PAD = 8
BF16 = jnp.bfloat16


def message_starts(layers):
    starts = [0]
    for level in range(layers):
        starts.append(starts[-1] + layers - level)
    return starts


def taps_into(s_ref, row, a, line):
    width, channels = a.shape
    line[PAD : PAD + width] = a
    s_ref[row, :, 0:channels] = line[PAD - 1 : PAD - 1 + width].astype(BF16)
    s_ref[row, :, channels : 2 * channels] = a.astype(BF16)
    s_ref[row, :, 2 * channels : 3 * channels] = line[PAD + 1 : PAD + 1 + width].astype(BF16)


def clear_lines(lines):
    edge = jnp.zeros((PAD, lines.shape[2]), F32)
    for i in range(lines.shape[0]):
        lines[i, 0:PAD] = edge
        lines[i, lines.shape[1] - PAD :] = edge


def rows_dot(s_ref, first, count, w, layer, times):
    width, depth = s_ref.shape[1:]
    taps = jnp.concatenate([s_ref[pl.ds(first + i, count)].reshape(count * width, depth) for i in range(3)], axis=1)
    weights = jnp.concatenate([jnp.concatenate([w[layer, k, t] for t in times], axis=1) for k in range(9)], axis=0)
    return jnp.dot(taps, weights, preferred_element_type=F32)


def pairs_dot(first, count, w, layer, *terms):
    width, depth = terms[0][0].shape[1:]
    channels = depth // 3
    taps = jnp.concatenate(
        [
            jnp.concatenate([s_ref[first + i + 2 * p] for p in range(count)], axis=0)
            for s_ref, _ in terms
            for i in range(4)
        ],
        axis=1,
    )
    zero = jnp.zeros((channels, channels), BF16)

    def tap(i, j, time):
        return w[layer, 3 * i + j, time] if 0 <= i < 3 else zero

    weights = jnp.concatenate(
        [
            jnp.concatenate([tap(i, j, time), tap(i - 1, j, time)], axis=1)
            for _, time in terms
            for i in range(4)
            for j in range(3)
        ],
        axis=0,
    )
    total = jnp.dot(taps, weights, preferred_element_type=F32)
    upper = total[:, :channels].reshape(count, 1, width, channels)
    lower = total[:, channels:].reshape(count, 1, width, channels)
    return jnp.concatenate([upper, lower], axis=1).reshape(2 * count, width, channels)


def history_kernel(frame, flags, caches, w, sums, inner, cross, *refs):
    layers, _, rows, width, channels = caches.shape
    begin = layers - flags[2]
    if frame == 0:
        done, held, wb, s, lines, sems = refs
    else:
        held, wb = caches, w
        s, lines = refs

    def loads(layer):
        return [
            pltpu.make_async_copy(caches.at[layer], held.at[layer], sems.at[layer, 0]),
            pltpu.make_async_copy(w.at[layer, :, 0:2], wb.at[layer], sems.at[layer, 1]),
        ]

    if frame == 0:
        for layer in range(layers):

            @pl.when(layer < flags[2])
            def _(layer=layer):
                for copy in loads(layer):
                    copy.start()

    clear_lines(lines)
    for f in range(frame, 2):
        s[f, 0:2] = jnp.zeros((2,) + s.shape[2:], BF16)
        s[f, rows + 2 : rows + 4] = jnp.zeros((2,) + s.shape[2:], BF16)

    def layer_step(layer, _):
        if frame == 0:
            history, taps = loads(layer)
            history.wait()

        def build(row, _):
            for f in range(frame, 2):
                taps_into(s.at[f], row + 2, held[layer, f, row].astype(F32), lines.at[f])
            return 0

        lax.fori_loop(0, rows, build, 0)
        if frame == 0:
            taps.wait()
        terms = [(s.at[f], f - frame) for f in range(frame, 2)]
        sums[begin + layer] = pairs_dot(0, (rows + 2) // 2, wb, layer, *terms).astype(BF16)
        return 0

    lax.fori_loop(0, flags[2], layer_step, 0)
    starts = message_starts(layers)

    def messages(up, down):
        for level in range(layers):
            reach = layers - level
            up[starts[level] : starts[level + 1]] = sums[level, 0:reach]
            down[starts[level] : starts[level + 1]] = sums[level, rows + 2 - reach : rows + 2]

    @pl.when(flags[1] % 2 == 0)
    def _():
        messages(cross, inner)

    @pl.when(flags[1] % 2 != 0)
    def _():
        messages(inner, cross)


def pieces(count):
    parts, at = [], 0
    while at < count:
        step = 4 if count - at in (4, 8) else min(6, count - at)
        parts.append((at, step))
        at += step
    return parts


def tick_kernel(tick, segments, bands, flags, w, bias, *refs):
    zero, one = tick < segments, tick > 0
    refs = list(refs)

    def take(count):
        found, refs[:count] = refs[:count], []
        return found

    clip = take(3) if tick < 2 else None
    own, inner, cross = take(3) if one else (None, None, None)
    sums0 = take(3) if zero else None
    sums1 = take(3) if one else None
    behind = take(1)[0] if one else None
    done = take(1)
    x_out = take(1)[0]
    ahead = take(1)[0] if zero else None
    done_out, x, s, lines, part, sem = refs
    rows, width, channels = x_out.shape
    layers = w.shape[0]
    starts = message_starts(layers)
    band = flags[1]
    begin = layers - flags[2]
    low = jnp.where(band == 0, rows, 0)
    high = jnp.where(band == bands - 1, 2 * rows, 3 * rows)

    def run(frame, fresh, own, inner, cross, sums, messages):
        def of(source):
            return source[frame] if fresh else source[...]

        x[rows : 2 * rows] = of(own)

        def gather(above, below, side_above, side_below):
            x[0:rows] = of(above)
            x[2 * rows : 3 * rows] = of(below)
            for level in range(layers):

                @pl.when(level >= begin)
                def _(level=level):
                    reach = layers - level
                    start, sums_above, sums_below = starts[level], messages[side_above], messages[side_below]
                    part[level, rows + 1 - reach : rows + 1] = sums_above[start : start + reach]
                    part[level, 2 * rows - 1 : 2 * rows - 1 + reach] = sums_below[start : start + reach]
                    part[level, rows + 1 : 2 * rows - 1] = sums[level, 2:rows]
                    part[level, rows] += sums[level, 1]
                    part[level, 2 * rows - 1] += sums[level, rows]
                    if reach > 1:
                        part[level, rows - 1] += sums[level, 0]
                        part[level, 2 * rows] += sums[level, rows + 1]

        @pl.when(band % 2 == 0)
        def _():
            gather(cross, inner, 1, 0)

        @pl.when(band % 2 != 0)
        def _():
            gather(inner, cross, 0, 1)

        clear_lines(lines)

        def build(row, line):
            half = x[row].astype(F32) * 0.5
            inside = jnp.logical_and(row >= low, row < high).astype(F32)
            taps_into(s, row, (half + half * jnp.tanh(half)) * inside, line)

        for level in range(layers):

            @pl.when(level >= begin)
            def _(level=level):
                layer = level - begin
                first = rows - layers + 1 + level
                count = rows + 2 * (layers - 1 - level)

                def two(i, _):
                    build(first - 1 + 2 * i, lines.at[0])
                    build(first + 2 * i, lines.at[1])
                    return 0

                lax.fori_loop(0, count // 2 + 1, two, 0)
                offset = bias[pl.ds(layer, 1), :].reshape(1, 1, channels)
                for start, step in [(0, count)] if frame == 0 else pieces(count):
                    at = first + start
                    known = part[level, at : at + step].astype(F32) + offset
                    if frame == 0:
                        total = rows_dot(s, at - 1, step, w, layer, (2, 1))
                        mine = total[:, :channels].reshape(step, width, channels)
                        ahead[level, at : at + step] = total[:, channels:].reshape(step, width, channels).astype(BF16)
                    else:
                        mine = pairs_dot(at - 1, step // 2, w, layer, (s, 2))
                        known = known + behind[level, at : at + step].astype(F32)
                    x[at : at + step] = (x[at : at + step].astype(F32) + (mine + known)).astype(BF16)

        copy = pltpu.make_async_copy(x.at[rows : 2 * rows], done_out.at[frame], sem)
        copy.start()
        x_out[...] = x[rows : 2 * rows]
        copy.wait()

    for frame, present, parts in ((0, zero, sums0), (1, one, sums1)):
        if present:
            fresh = tick == frame

            @pl.when(flags[0] == tick - frame)
            def _(frame=frame, fresh=fresh, parts=parts):
                run(frame, fresh, *(clip if fresh else (own, inner, cross)), parts[0], parts[1:])


def in_vmem(count):
    return [pl.BlockSpec(memory_space=pltpu.VMEM)] * count


def anywhere():
    return pl.BlockSpec(memory_space=pl.ANY)


def in_smem():
    return pl.BlockSpec(memory_space=pltpu.SMEM)


def history_call(frame, flags, caches, weights):
    layers, _, rows, width, channels = caches.shape
    row = (width, channels)
    message = jax.ShapeDtypeStruct((message_starts(layers)[-1],) + row, BF16)
    outs = [jax.ShapeDtypeStruct((layers, rows + 2) + row, BF16), message, message]
    specs = in_vmem(3)
    scratch = [pltpu.VMEM((2, rows + 4, width, 3 * channels), BF16), pltpu.VMEM((2, width + 2 * PAD, channels), F32)]
    if frame == 0:
        outs.append(jax.ShapeDtypeStruct((2, rows) + row, BF16))
        specs.append(anywhere())
        scratch = [
            pltpu.VMEM(caches.shape, BF16),
            pltpu.VMEM((layers, 9, 2, channels, channels), BF16),
            *scratch,
            pltpu.SemaphoreType.DMA((layers, 2)),
        ]
    pixels = layers * (rows + 2) * width
    return pl.pallas_call(
        functools.partial(history_kernel, frame),
        out_shape=tuple(outs),
        in_specs=[in_smem()] + ([anywhere()] * 2 if frame == 0 else in_vmem(2)),
        out_specs=tuple(specs),
        scratch_shapes=scratch,
        compiler_params=pltpu.CompilerParams(vmem_limit_bytes=HISTORY_LIMIT if frame == 0 else LIMIT),
        cost_estimate=pl.CostEstimate(
            flops=pixels * 9 * 2 * (2 - frame) * channels * channels, bytes_accessed=4000000, transcendentals=0
        ),
        name="history",
    )(flags, caches, weights)


def tick_call(tick, segments, bands, flags, clip, received, weights, biases, sums0, sums1, behind, done):
    layers, _, _, channels, _ = weights.shape
    rows, width = done.shape[1:3]
    every = (layers, 3 * rows, width, channels)
    pixels = sum(rows + 2 * level for level in range(layers)) * width
    zero, one = tick < segments, tick > 0
    extra = (list(clip) if tick < 2 else []) + (list(received) if one else [])
    extra += (list(sums0) if zero else []) + (list(sums1) + [behind] if one else [])
    outs = [jax.ShapeDtypeStruct((rows, width, channels), BF16)]
    if zero:
        outs.append(jax.ShapeDtypeStruct(every, BF16))
    specs = in_vmem(len(outs)) + [anywhere()]
    outs.append(jax.ShapeDtypeStruct(done.shape, BF16))
    return pl.pallas_call(
        functools.partial(tick_kernel, tick, segments, bands),
        out_shape=tuple(outs),
        in_specs=[in_smem()] + in_vmem(2 + len(extra)) + [anywhere()],
        out_specs=tuple(specs),
        scratch_shapes=[
            pltpu.VMEM((3 * rows, width, channels), BF16),
            pltpu.VMEM((3 * rows, width, 3 * channels), BF16),
            pltpu.VMEM((2, width + 2 * PAD, channels), F32),
            pltpu.VMEM(every, BF16),
            pltpu.SemaphoreType.DMA,
        ],
        input_output_aliases={3 + len(extra): len(outs) - 1},
        compiler_params=pltpu.CompilerParams(vmem_limit_bytes=LIMIT),
        cost_estimate=pl.CostEstimate(
            flops=pixels * 18 * 2 * channels * channels, bytes_accessed=4000000, transcendentals=pixels * channels
        ),
        name="tick",
    )(flags, weights, biases, *extra, done)


def per_device(clip, caches, weights, biases, section_layers):
    segments = lax.axis_size("segment")
    bands = lax.axis_size("band")
    caches, weights, biases = caches[0], weights[0], biases[0]
    flags = jnp.stack([lax.axis_index("segment"), lax.axis_index("band"), section_layers[0]]).astype(jnp.int32)
    axes = ("segment", "band")
    in_chip = [(b, b ^ 1) for b in range(bands)]
    between = [(b, b + 1) for b in range(1, bands - 1, 2)] + [(b + 1, b) for b in range(1, bands - 1, 2)]
    straight = [(b, b) for b in range(bands)]

    def swap(value, pairs, chosen):
        return lax.ppermute(value, axes, [(s * bands + a, s * bands + b) for s in chosen for a, b in pairs])

    def ahead(value, pairs, sources):
        return lax.ppermute(value, axes, [(s * bands + a, (s + 1) * bands + b) for s in sources for a, b in pairs])

    def lender(value, pairs):
        source = min(1, segments - 1)
        return lax.ppermute(value, axes, [(source * bands + a, b) for a, b in pairs])

    everyone = range(segments)
    clip_cross = lender(clip, between)
    clip_in = swap(clip, in_chip, [0])
    sums, inner, cross, done = history_call(0, flags, caches, weights)
    sums0 = (sums, swap(inner, in_chip, everyone), swap(cross, between, everyone))
    caches, clip_cross, _ = lax.optimization_barrier((caches, clip_cross, sums))
    sums, inner, cross = history_call(1, flags, caches, weights)
    sums1 = (sums, swap(inner, in_chip, everyone), swap(cross, between, everyone))
    halves = (clip, clip_in, clip_cross)
    received = behind = None
    for tick in range(segments + 1):
        x, *later, done = tick_call(
            tick, segments, bands, flags, halves, received, weights, biases, sums0, sums1, behind, done
        )
        if tick < segments:
            (behind,) = later
            sources = [s for s in (tick, tick - 1) if 0 <= s < segments - 1]
            own, cross = ahead(x, straight, sources), ahead(x, between, sources)
            received = (own, swap(own, in_chip, [s + 1 for s in sources]), cross)
    return done[None]


def solution(mesh):
    placed = (
        P(None, "band", None, None),
        P("segment", None, None, "band", None, None),
        P("segment", None, None, None, None, None),
        P("segment", None, None),
        P("segment"),
    )
    return jax.shard_map(
        per_device,
        mesh=mesh,
        in_specs=placed,
        out_specs=P("segment", None, "band", None, None),
        check_vma=False,
    )
```

```python
import functools

import jax
import jax.numpy as jnp
from jax import lax
from jax.experimental import pallas as pl
from jax.experimental.pallas import tpu as pltpu
from jax.sharding import PartitionSpec as P

LIMIT = 28 * 1024 * 1024
HISTORY_LIMIT = 52 * 1024 * 1024
F32 = jnp.float32
PAD = 8
BF16 = jnp.bfloat16


def message_starts(layers):
    starts = [0]
    for level in range(layers):
        starts.append(starts[-1] + layers - level)
    return starts


def taps_into(s_ref, row, a, line):
    width, channels = a.shape
    line[PAD : PAD + width] = a
    s_ref[row, :, 0:channels] = line[PAD - 1 : PAD - 1 + width].astype(BF16)
    s_ref[row, :, channels : 2 * channels] = a.astype(BF16)
    s_ref[row, :, 2 * channels : 3 * channels] = line[PAD + 1 : PAD + 1 + width].astype(BF16)


def clear_lines(lines):
    edge = jnp.zeros((PAD, lines.shape[2]), F32)
    for i in range(lines.shape[0]):
        lines[i, 0:PAD] = edge
        lines[i, lines.shape[1] - PAD :] = edge


def rows_dot(s_ref, first, count, w, layer, times):
    width, depth = s_ref.shape[1:]
    taps = jnp.concatenate([s_ref[pl.ds(first + i, count)].reshape(count * width, depth) for i in range(3)], axis=1)
    weights = jnp.concatenate([jnp.concatenate([w[layer, k, t] for t in times], axis=1) for k in range(9)], axis=0)
    return jnp.dot(taps, weights, preferred_element_type=F32)


def pairs_dot(first, count, w, layer, *terms):
    width, depth = terms[0][0].shape[1:]
    channels = depth // 3
    taps = jnp.concatenate(
        [
            jnp.concatenate([s_ref[first + i + 2 * p] for p in range(count)], axis=0)
            for s_ref, _ in terms
            for i in range(4)
        ],
        axis=1,
    )
    zero = jnp.zeros((channels, channels), BF16)

    def tap(i, j, time):
        return w[layer, 3 * i + j, time] if 0 <= i < 3 else zero

    weights = jnp.concatenate(
        [
            jnp.concatenate([tap(i, j, time), tap(i - 1, j, time)], axis=1)
            for _, time in terms
            for i in range(4)
            for j in range(3)
        ],
        axis=0,
    )
    total = jnp.dot(taps, weights, preferred_element_type=F32)
    upper = total[:, :channels].reshape(count, 1, width, channels)
    lower = total[:, channels:].reshape(count, 1, width, channels)
    return jnp.concatenate([upper, lower], axis=1).reshape(2 * count, width, channels)


def history_kernel(frame, flags, caches, w, sums, inner, cross, *refs):
    layers, _, rows, width, channels = caches.shape
    begin = layers - flags[2]
    if frame == 0:
        held, wb, s, lines, sems = refs
    else:
        held, wb = caches, w
        s, lines = refs

    def loads(layer):
        return [
            pltpu.make_async_copy(caches.at[layer], held.at[layer], sems.at[layer, 0]),
            pltpu.make_async_copy(w.at[layer, :, 0:2], wb.at[layer], sems.at[layer, 1]),
        ]

    if frame == 0:
        for layer in range(layers):

            @pl.when(layer < flags[2])
            def _(layer=layer):
                for copy in loads(layer):
                    copy.start()

    clear_lines(lines)
    for f in range(frame, 2):
        s[f, 0:2] = jnp.zeros((2,) + s.shape[2:], BF16)
        s[f, rows + 2 : rows + 4] = jnp.zeros((2,) + s.shape[2:], BF16)

    def layer_step(layer, _):
        if frame == 0:
            history, taps = loads(layer)
            history.wait()

        def build(row, _):
            for f in range(frame, 2):
                taps_into(s.at[f], row + 2, held[layer, f, row].astype(F32), lines.at[f])
            return 0

        lax.fori_loop(0, rows, build, 0)
        if frame == 0:
            taps.wait()
        terms = [(s.at[f], f - frame) for f in range(frame, 2)]
        sums[begin + layer] = pairs_dot(0, (rows + 2) // 2, wb, layer, *terms).astype(BF16)
        return 0

    lax.fori_loop(0, flags[2], layer_step, 0)
    starts = message_starts(layers)

    def messages(up, down):
        for level in range(layers):
            reach = layers - level
            up[starts[level] : starts[level + 1]] = sums[level, 0:reach]
            down[starts[level] : starts[level + 1]] = sums[level, rows + 2 - reach : rows + 2]

    @pl.when(flags[1] % 2 == 0)
    def _():
        messages(cross, inner)

    @pl.when(flags[1] % 2 != 0)
    def _():
        messages(inner, cross)


def pieces(count):
    parts, at = [], 0
    while at < count:
        step = 4 if count - at in (4, 8) else min(6, count - at)
        parts.append((at, step))
        at += step
    return parts


def tick_kernel(tick, segments, bands, flags, w, bias, *refs):
    zero, one = tick < segments, tick > 0
    refs = list(refs)

    def take(count):
        found, refs[:count] = refs[:count], []
        return found

    clip = take(3) if tick < 2 else None
    own, inner, cross = take(3) if one else (None, None, None)
    sums0 = take(3) if zero else None
    sums1 = take(3) if one else None
    behind = take(1)[0] if one else None
    results = take(segments) if not zero else []
    out = take(1)[0]
    ahead = take(1)[0] if zero else None
    x, s, lines, part, sems = refs
    rows, width, channels = out.shape[-3:]
    layers = w.shape[0]
    starts = message_starts(layers)
    band = flags[1]
    begin = layers - flags[2]
    low = jnp.where(band == 0, rows, 0)
    high = jnp.where(band == bands - 1, 2 * rows, 3 * rows)

    def run(frame, fresh, own, inner, cross, sums, messages):
        def of(source):
            return source[frame] if fresh else source[...]

        x[rows : 2 * rows] = of(own)

        def gather(above, below, side_above, side_below):
            x[0:rows] = of(above)
            x[2 * rows : 3 * rows] = of(below)
            for level in range(layers):

                @pl.when(level >= begin)
                def _(level=level):
                    reach = layers - level
                    start, sums_above, sums_below = starts[level], messages[side_above], messages[side_below]
                    part[level, rows + 1 - reach : rows + 1] = sums_above[start : start + reach]
                    part[level, 2 * rows - 1 : 2 * rows - 1 + reach] = sums_below[start : start + reach]
                    part[level, rows + 1 : 2 * rows - 1] = sums[level, 2:rows]
                    part[level, rows] += sums[level, 1]
                    part[level, 2 * rows - 1] += sums[level, rows]
                    if reach > 1:
                        part[level, rows - 1] += sums[level, 0]
                        part[level, 2 * rows] += sums[level, rows + 1]

        @pl.when(band % 2 == 0)
        def _():
            gather(cross, inner, 1, 0)

        @pl.when(band % 2 != 0)
        def _():
            gather(inner, cross, 0, 1)

        clear_lines(lines)

        def build(row, line):
            half = x[row].astype(F32) * 0.5
            inside = jnp.logical_and(row >= low, row < high).astype(F32)
            taps_into(s, row, (half + half * jnp.tanh(half)) * inside, line)

        for level in range(layers):

            @pl.when(level >= begin)
            def _(level=level):
                layer = level - begin
                first = rows - layers + 1 + level
                count = rows + 2 * (layers - 1 - level)

                def two(i, _):
                    build(first - 1 + 2 * i, lines.at[0])
                    build(first + 2 * i, lines.at[1])
                    return 0

                lax.fori_loop(0, count // 2 + 1, two, 0)
                offset = bias[pl.ds(layer, 1), :].reshape(1, 1, channels)
                for start, step in [(0, count)] if frame == 0 else pieces(count):
                    at = first + start
                    known = part[level, at : at + step].astype(F32) + offset
                    if frame == 0:
                        total = rows_dot(s, at - 1, step, w, layer, (2, 1))
                        mine = total[:, :channels].reshape(step, width, channels)
                        ahead[level, at : at + step] = total[:, channels:].reshape(step, width, channels).astype(BF16)
                    else:
                        mine = pairs_dot(at - 1, step // 2, w, layer, (s, 2))
                        known = known + behind[level, at : at + step].astype(F32)
                    x[at : at + step] = (x[at : at + step].astype(F32) + (mine + known)).astype(BF16)

        if zero:
            out[...] = x[rows : 2 * rows]
        else:
            copy = pltpu.make_async_copy(x.at[rows : 2 * rows], out.at[frame], sems.at[1])
            copy.start()
            copy.wait()

    def finished(section):
        count = 2 if section + 1 < segments else 1
        return [
            pltpu.make_async_copy(results[section + f], out.at[f], sems.at[f]) for f in range(count)
        ]

    for section in range(len(results)):

        @pl.when(flags[0] == section)
        def _(section=section):
            for copy in finished(section):
                copy.start()

    for frame, present, parts in ((0, zero, sums0), (1, one, sums1)):
        if present:
            fresh = tick == frame

            @pl.when(flags[0] == tick - frame)
            def _(frame=frame, fresh=fresh, parts=parts):
                run(frame, fresh, *(clip if fresh else (own, inner, cross)), parts[0], parts[1:])

    for section in range(len(results)):

        @pl.when(flags[0] == section)
        def _(section=section):
            for copy in finished(section):
                copy.wait()


def in_vmem(count):
    return [pl.BlockSpec(memory_space=pltpu.VMEM)] * count


def anywhere():
    return pl.BlockSpec(memory_space=pl.ANY)


def in_smem():
    return pl.BlockSpec(memory_space=pltpu.SMEM)


def history_call(frame, flags, caches, weights):
    layers, _, rows, width, channels = caches.shape
    row = (width, channels)
    message = jax.ShapeDtypeStruct((message_starts(layers)[-1],) + row, BF16)
    outs = [jax.ShapeDtypeStruct((layers, rows + 2) + row, BF16), message, message]
    specs = in_vmem(3)
    scratch = [pltpu.VMEM((2, rows + 4, width, 3 * channels), BF16), pltpu.VMEM((2, width + 2 * PAD, channels), F32)]
    if frame == 0:
        scratch = [
            pltpu.VMEM(caches.shape, BF16),
            pltpu.VMEM((layers, 9, 2, channels, channels), BF16),
            *scratch,
            pltpu.SemaphoreType.DMA((layers, 2)),
        ]
    pixels = layers * (rows + 2) * width
    return pl.pallas_call(
        functools.partial(history_kernel, frame),
        out_shape=tuple(outs),
        in_specs=[in_smem()] + ([anywhere()] * 2 if frame == 0 else in_vmem(2)),
        out_specs=tuple(specs),
        scratch_shapes=scratch,
        compiler_params=pltpu.CompilerParams(vmem_limit_bytes=HISTORY_LIMIT if frame == 0 else LIMIT),
        cost_estimate=pl.CostEstimate(
            flops=pixels * 9 * 2 * (2 - frame) * channels * channels, bytes_accessed=4000000, transcendentals=0
        ),
        name="history",
    )(flags, caches, weights)


def tick_call(tick, segments, bands, flags, clip, received, weights, biases, sums0, sums1, behind, results):
    layers, _, _, channels, _ = weights.shape
    rows, width = clip[0].shape[1:3]
    every = (layers, 3 * rows, width, channels)
    pixels = sum(rows + 2 * level for level in range(layers)) * width
    zero, one = tick < segments, tick > 0
    extra = (list(clip) if tick < 2 else []) + (list(received) if one else [])
    extra += (list(sums0) if zero else []) + (list(sums1) + [behind] if one else [])
    if zero:
        outs = [jax.ShapeDtypeStruct((rows, width, channels), BF16), jax.ShapeDtypeStruct(every, BF16)]
        specs = in_vmem(2)
    else:
        extra += results
        outs, specs = [jax.ShapeDtypeStruct(clip[0].shape, BF16)], [anywhere()]
    return pl.pallas_call(
        functools.partial(tick_kernel, tick, segments, bands),
        out_shape=tuple(outs),
        in_specs=[in_smem()] + in_vmem(2 + len(extra)),
        out_specs=tuple(specs),
        scratch_shapes=[
            pltpu.VMEM((3 * rows, width, channels), BF16),
            pltpu.VMEM((3 * rows, width, 3 * channels), BF16),
            pltpu.VMEM((2, width + 2 * PAD, channels), F32),
            pltpu.VMEM(every, BF16),
            pltpu.SemaphoreType.DMA((2,)),
        ],
        compiler_params=pltpu.CompilerParams(vmem_limit_bytes=LIMIT),
        cost_estimate=pl.CostEstimate(
            flops=pixels * 18 * 2 * channels * channels, bytes_accessed=4000000, transcendentals=pixels * channels
        ),
        name="tick",
    )(flags, weights, biases, *extra)


def per_device(clip, caches, weights, biases, section_layers):
    segments = lax.axis_size("segment")
    bands = lax.axis_size("band")
    caches, weights, biases = caches[0], weights[0], biases[0]
    flags = jnp.stack([lax.axis_index("segment"), lax.axis_index("band"), section_layers[0]]).astype(jnp.int32)
    axes = ("segment", "band")
    in_chip = [(b, b ^ 1) for b in range(bands)]
    between = [(b, b + 1) for b in range(1, bands - 1, 2)] + [(b + 1, b) for b in range(1, bands - 1, 2)]
    straight = [(b, b) for b in range(bands)]

    def swap(value, pairs, chosen):
        return lax.ppermute(value, axes, [(s * bands + a, s * bands + b) for s in chosen for a, b in pairs])

    def ahead(value, pairs, sources):
        return lax.ppermute(value, axes, [(s * bands + a, (s + 1) * bands + b) for s in sources for a, b in pairs])

    def lender(value, pairs):
        source = min(1, segments - 1)
        return lax.ppermute(value, axes, [(source * bands + a, b) for a, b in pairs])

    everyone = range(segments)
    clip_cross = lender(clip, between)
    clip_in = swap(clip, in_chip, [0])
    sums, inner, cross = history_call(0, flags, caches, weights)
    sums0 = (sums, swap(inner, in_chip, everyone), swap(cross, between, everyone))
    caches, clip_cross, _ = lax.optimization_barrier((caches, clip_cross, sums))
    sums, inner, cross = history_call(1, flags, caches, weights)
    sums1 = (sums, swap(inner, in_chip, everyone), swap(cross, between, everyone))
    halves = (clip, clip_in, clip_cross)
    received = behind = None
    results = []
    for tick in range(segments + 1):
        x, *later = tick_call(
            tick, segments, bands, flags, halves, received, weights, biases, sums0, sums1, behind, results
        )
        if tick < segments:
            (behind,) = later
            results.append(x)
            sources = [s for s in (tick, tick - 1) if 0 <= s < segments - 1]
            own, cross = ahead(x, straight, sources), ahead(x, between, sources)
            received = (own, swap(own, in_chip, [s + 1 for s in sources]), cross)
    return x[None]


def solution(mesh):
    placed = (
        P(None, "band", None, None),
        P("segment", None, None, "band", None, None),
        P("segment", None, None, None, None, None),
        P("segment", None, None),
        P("segment"),
    )
    return jax.shard_map(
        per_device,
        mesh=mesh,
        in_specs=placed,
        out_specs=P("segment", None, "band", None, None),
        check_vma=False,
    )
```

```python
import functools

import jax
import jax.numpy as jnp
from jax import lax
from jax.experimental import pallas as pl
from jax.experimental.pallas import tpu as pltpu
from jax.sharding import PartitionSpec as P

LIMIT = 28 * 1024 * 1024
HISTORY_LIMIT = 52 * 1024 * 1024
F32 = jnp.float32
PAD = 8
BF16 = jnp.bfloat16


def message_starts(layers):
    starts = [0]
    for level in range(layers):
        starts.append(starts[-1] + layers - level)
    return starts


def taps_into(s_ref, row, a, line):
    width, channels = a.shape
    line[PAD : PAD + width] = a
    s_ref[row, :, 0:channels] = line[PAD - 1 : PAD - 1 + width].astype(BF16)
    s_ref[row, :, channels : 2 * channels] = a.astype(BF16)
    s_ref[row, :, 2 * channels : 3 * channels] = line[PAD + 1 : PAD + 1 + width].astype(BF16)


def clear_lines(lines):
    edge = jnp.zeros((PAD, lines.shape[2]), F32)
    for i in range(lines.shape[0]):
        lines[i, 0:PAD] = edge
        lines[i, lines.shape[1] - PAD :] = edge


def pairs_dot(first, count, w, layer, *terms):
    width, depth = terms[0][0].shape[1:]
    channels = depth // 3
    taps = jnp.concatenate(
        [
            jnp.concatenate([s_ref[first + i + 2 * p] for p in range(count)], axis=0)
            for s_ref, _ in terms
            for i in range(4)
        ],
        axis=1,
    )
    zero = jnp.zeros((channels, channels), BF16)

    def tap(i, j, time):
        return w[layer, 3 * i + j, time] if 0 <= i < 3 else zero

    weights = jnp.concatenate(
        [
            jnp.concatenate([tap(i, j, time), tap(i - 1, j, time)], axis=1)
            for _, time in terms
            for i in range(4)
            for j in range(3)
        ],
        axis=0,
    )
    total = jnp.dot(taps, weights, preferred_element_type=F32)
    upper = total[:, :channels].reshape(count, 1, width, channels)
    lower = total[:, channels:].reshape(count, 1, width, channels)
    return jnp.concatenate([upper, lower], axis=1).reshape(2 * count, width, channels)


def history_kernel(frame, flags, caches, w, sums, inner, cross, *refs):
    layers, _, rows, width, channels = caches.shape
    begin = layers - flags[2]
    if frame == 0:
        held, wb, s, lines, sems = refs
    else:
        held, wb = caches, w
        s, lines = refs

    def loads(layer):
        return [
            pltpu.make_async_copy(caches.at[layer], held.at[layer], sems.at[layer, 0]),
            pltpu.make_async_copy(w.at[layer, :, 0:2], wb.at[layer], sems.at[layer, 1]),
        ]

    if frame == 0:
        for layer in range(layers):

            @pl.when(layer < flags[2])
            def _(layer=layer):
                for copy in loads(layer):
                    copy.start()

    clear_lines(lines)
    for f in range(frame, 2):
        s[f, 0:2] = jnp.zeros((2,) + s.shape[2:], BF16)
        s[f, rows + 2 : rows + 4] = jnp.zeros((2,) + s.shape[2:], BF16)

    def layer_step(layer, _):
        if frame == 0:
            history, taps = loads(layer)
            history.wait()

        def build(row, _):
            for f in range(frame, 2):
                taps_into(s.at[f], row + 2, held[layer, f, row].astype(F32), lines.at[f])
            return 0

        lax.fori_loop(0, rows, build, 0)
        if frame == 0:
            taps.wait()
        terms = [(s.at[f], f - frame) for f in range(frame, 2)]
        sums[begin + layer] = pairs_dot(0, (rows + 2) // 2, wb, layer, *terms).astype(BF16)
        return 0

    lax.fori_loop(0, flags[2], layer_step, 0)
    starts = message_starts(layers)

    def messages(up, down):
        for level in range(layers):
            reach = layers - level
            up[starts[level] : starts[level + 1]] = sums[level, 0:reach]
            down[starts[level] : starts[level + 1]] = sums[level, rows + 2 - reach : rows + 2]

    @pl.when(flags[1] % 2 == 0)
    def _():
        messages(cross, inner)

    @pl.when(flags[1] % 2 != 0)
    def _():
        messages(inner, cross)


def level_rows(rows, layers, level):
    return rows - layers + 1 + level, rows + 2 * (layers - 1 - level)


def pieces(count):
    parts, at = [], 0
    while at < count:
        step = 4 if count - at in (4, 8) else min(6, count - at)
        parts.append((at, step))
        at += step
    return parts


def tick_kernel(tick, segments, bands, flags, w, bias, *refs):
    zero, one = tick < segments, tick > 0
    refs = list(refs)

    def take(count):
        found, refs[:count] = refs[:count], []
        return found

    clip = take(3) if tick < 2 else None
    own, inner, cross = take(3) if one else (None, None, None)
    sums0 = take(3) if zero else None
    sums1 = take(3) if one else None
    behind = take(1)[0] if one else None
    results = take(segments) if not zero else []
    out = take(1)[0]
    kept = take(1)[0] if zero else None
    x, scratch, lines, part, sems = refs
    rows, width, channels = out.shape[-3:]
    layers = w.shape[0]
    starts = message_starts(layers)
    band = flags[1]
    begin = layers - flags[2]
    low = jnp.where(band == 0, rows, 0)
    high = jnp.where(band == bands - 1, 2 * rows, 3 * rows)

    def run(frame, fresh, own, inner, cross, sums, messages):
        def of(source):
            return source[frame] if fresh else source[...]

        x[rows : 2 * rows] = of(own)

        def gather(above, below, side_above, side_below):
            x[0:rows] = of(above)
            x[2 * rows : 3 * rows] = of(below)
            for level in range(layers):

                @pl.when(level >= begin)
                def _(level=level):
                    reach = layers - level
                    start, sums_above, sums_below = starts[level], messages[side_above], messages[side_below]
                    part[level, rows + 1 - reach : rows + 1] = sums_above[start : start + reach]
                    part[level, 2 * rows - 1 : 2 * rows - 1 + reach] = sums_below[start : start + reach]
                    part[level, rows + 1 : 2 * rows - 1] = sums[level, 2:rows]
                    part[level, rows] += sums[level, 1]
                    part[level, 2 * rows - 1] += sums[level, rows]
                    if reach > 1:
                        part[level, rows - 1] += sums[level, 0]
                        part[level, 2 * rows] += sums[level, rows + 1]

        @pl.when(band % 2 == 0)
        def _():
            gather(cross, inner, 1, 0)

        @pl.when(band % 2 != 0)
        def _():
            gather(inner, cross, 0, 1)

        clear_lines(lines)

        def build(s, row, line):
            half = x[row].astype(F32) * 0.5
            inside = jnp.logical_and(row >= low, row < high).astype(F32)
            taps_into(s, row, (half + half * jnp.tanh(half)) * inside, line)

        for level in range(layers):

            @pl.when(level >= begin)
            def _(level=level):
                layer = level - begin
                first, count = level_rows(rows, layers, level)
                s = kept.at[level] if frame == 0 else scratch

                def two(i, _):
                    build(s, first - 1 + 2 * i, lines.at[0])
                    build(s, first + 2 * i, lines.at[1])
                    return 0

                lax.fori_loop(0, count // 2 + 1, two, 0)
                offset = bias[pl.ds(layer, 1), :].reshape(1, 1, channels)
                for start, step in pieces(count):
                    at = first + start
                    mine = pairs_dot(at - 1, step // 2, w, layer, (s, 2))
                    known = part[level, at : at + step].astype(F32) + offset
                    if frame == 1:
                        known = known + behind[level, at : at + step].astype(F32)
                    x[at : at + step] = (x[at : at + step].astype(F32) + (mine + known)).astype(BF16)

        if zero:
            out[...] = x[rows : 2 * rows]
        else:
            copy = pltpu.make_async_copy(x.at[rows : 2 * rows], out.at[frame], sems.at[1])
            copy.start()
            copy.wait()

    def finished(section):
        count = 2 if section + 1 < segments else 1
        return [
            pltpu.make_async_copy(results[section + f], out.at[f], sems.at[f]) for f in range(count)
        ]

    for section in range(len(results)):

        @pl.when(flags[0] == section)
        def _(section=section):
            for copy in finished(section):
                copy.start()

    for frame, present, parts in ((0, zero, sums0), (1, one, sums1)):
        if present:
            fresh = tick == frame

            @pl.when(flags[0] == tick - frame)
            def _(frame=frame, fresh=fresh, parts=parts):
                run(frame, fresh, *(clip if fresh else (own, inner, cross)), parts[0], parts[1:])

    for section in range(len(results)):

        @pl.when(flags[0] == section)
        def _(section=section):
            for copy in finished(section):
                copy.wait()


def ahead_kernel(tick, flags, w, kept, ahead):
    layers, rows = kept.shape[0], kept.shape[1] // 3
    begin = layers - flags[2]

    @pl.when(flags[0] == tick)
    def _():
        for level in range(layers):

            @pl.when(level >= begin)
            def _(level=level):
                first, count = level_rows(rows, layers, level)
                for start, step in pieces(count):
                    at = first + start
                    ahead[level, at : at + step] = pairs_dot(
                        at - 1, step // 2, w, level - begin, (kept.at[level], 1)
                    ).astype(BF16)


def in_vmem(count):
    return [pl.BlockSpec(memory_space=pltpu.VMEM)] * count


def anywhere():
    return pl.BlockSpec(memory_space=pl.ANY)


def in_smem():
    return pl.BlockSpec(memory_space=pltpu.SMEM)


def history_call(frame, flags, caches, weights):
    layers, _, rows, width, channels = caches.shape
    row = (width, channels)
    message = jax.ShapeDtypeStruct((message_starts(layers)[-1],) + row, BF16)
    outs = [jax.ShapeDtypeStruct((layers, rows + 2) + row, BF16), message, message]
    specs = in_vmem(3)
    scratch = [pltpu.VMEM((2, rows + 4, width, 3 * channels), BF16), pltpu.VMEM((2, width + 2 * PAD, channels), F32)]
    if frame == 0:
        scratch = [
            pltpu.VMEM(caches.shape, BF16),
            pltpu.VMEM((layers, 9, 2, channels, channels), BF16),
            *scratch,
            pltpu.SemaphoreType.DMA((layers, 2)),
        ]
    pixels = layers * (rows + 2) * width
    return pl.pallas_call(
        functools.partial(history_kernel, frame),
        out_shape=tuple(outs),
        in_specs=[in_smem()] + ([anywhere()] * 2 if frame == 0 else in_vmem(2)),
        out_specs=tuple(specs),
        scratch_shapes=scratch,
        compiler_params=pltpu.CompilerParams(vmem_limit_bytes=HISTORY_LIMIT if frame == 0 else LIMIT),
        cost_estimate=pl.CostEstimate(
            flops=pixels * 9 * 2 * (2 - frame) * channels * channels, bytes_accessed=4000000, transcendentals=0
        ),
        name="history",
    )(flags, caches, weights)


def tick_call(tick, segments, bands, flags, clip, received, weights, biases, sums0, sums1, behind, results):
    layers, _, _, channels, _ = weights.shape
    rows, width = clip[0].shape[1:3]
    every = (layers, 3 * rows, width, channels)
    pixels = sum(rows + 2 * level for level in range(layers)) * width
    zero, one = tick < segments, tick > 0
    extra = (list(clip) if tick < 2 else []) + (list(received) if one else [])
    extra += (list(sums0) if zero else []) + (list(sums1) + [behind] if one else [])
    if zero:
        outs = [jax.ShapeDtypeStruct((rows, width, channels), BF16), jax.ShapeDtypeStruct(every[:3] + (3 * channels,), BF16)]
        specs = in_vmem(2)
    else:
        extra += results
        outs, specs = [jax.ShapeDtypeStruct(clip[0].shape, BF16)], [anywhere()]
    return pl.pallas_call(
        functools.partial(tick_kernel, tick, segments, bands),
        out_shape=tuple(outs),
        in_specs=[in_smem()] + in_vmem(2 + len(extra)),
        out_specs=tuple(specs),
        scratch_shapes=[
            pltpu.VMEM((3 * rows, width, channels), BF16),
            pltpu.VMEM((3 * rows, width, 3 * channels), BF16),
            pltpu.VMEM((2, width + 2 * PAD, channels), F32),
            pltpu.VMEM(every, BF16),
            pltpu.SemaphoreType.DMA((2,)),
        ],
        compiler_params=pltpu.CompilerParams(vmem_limit_bytes=LIMIT),
        cost_estimate=pl.CostEstimate(
            flops=pixels * 9 * 2 * channels * channels, bytes_accessed=4000000, transcendentals=pixels * channels
        ),
        name="tick",
    )(flags, weights, biases, *extra)


def ahead_call(tick, flags, weights, kept):
    layers, extent, width, depth = kept.shape
    return pl.pallas_call(
        functools.partial(ahead_kernel, tick),
        out_shape=jax.ShapeDtypeStruct((layers, extent, width, depth // 3), BF16),
        in_specs=[in_smem()] + in_vmem(2),
        out_specs=in_vmem(1)[0],
        compiler_params=pltpu.CompilerParams(vmem_limit_bytes=LIMIT),
        cost_estimate=pl.CostEstimate(
            flops=layers * extent * width * 6 * depth * depth // 3, bytes_accessed=4000000, transcendentals=0
        ),
        name="ahead",
    )(flags, weights, kept)


def per_device(clip, caches, weights, biases, section_layers):
    segments = lax.axis_size("segment")
    bands = lax.axis_size("band")
    caches, weights, biases = caches[0], weights[0], biases[0]
    flags = jnp.stack([lax.axis_index("segment"), lax.axis_index("band"), section_layers[0]]).astype(jnp.int32)
    axes = ("segment", "band")
    in_chip = [(b, b ^ 1) for b in range(bands)]
    between = [(b, b + 1) for b in range(1, bands - 1, 2)] + [(b + 1, b) for b in range(1, bands - 1, 2)]
    straight = [(b, b) for b in range(bands)]

    def swap(value, pairs, chosen):
        return lax.ppermute(value, axes, [(s * bands + a, s * bands + b) for s in chosen for a, b in pairs])

    def ahead(value, pairs, sources):
        return lax.ppermute(value, axes, [(s * bands + a, (s + 1) * bands + b) for s in sources for a, b in pairs])

    def lender(value, pairs):
        source = min(1, segments - 1)
        return lax.ppermute(value, axes, [(source * bands + a, b) for a, b in pairs])

    everyone = range(segments)
    clip_cross = lender(clip, between)
    clip_in = swap(clip, in_chip, [0])
    sums, inner, cross = history_call(0, flags, caches, weights)
    sums0 = (sums, swap(inner, in_chip, everyone), swap(cross, between, everyone))
    caches, clip_cross, _ = lax.optimization_barrier((caches, clip_cross, sums))
    sums, inner, cross = history_call(1, flags, caches, weights)
    sums1 = (sums, swap(inner, in_chip, everyone), swap(cross, between, everyone))
    halves = (clip, clip_in, clip_cross)
    received = behind = None
    results = []
    for tick in range(segments + 1):
        x, *later = tick_call(
            tick, segments, bands, flags, halves, received, weights, biases, sums0, sums1, behind, results
        )
        if tick < segments:
            behind = ahead_call(tick, flags, weights, later[0])
            results.append(x)
            sources = [s for s in (tick, tick - 1) if 0 <= s < segments - 1]
            own, cross = ahead(x, straight, sources), ahead(x, between, sources)
            own, behind = lax.optimization_barrier((own, behind))
            received = (own, swap(own, in_chip, [s + 1 for s in sources]), cross)
    return x[None]


def solution(mesh):
    placed = (
        P(None, "band", None, None),
        P("segment", None, None, "band", None, None),
        P("segment", None, None, None, None, None),
        P("segment", None, None),
        P("segment"),
    )
    return jax.shard_map(
        per_device,
        mesh=mesh,
        in_specs=placed,
        out_specs=P("segment", None, "band", None, None),
        check_vma=False,
    )
```

```python
import functools

import jax
import jax.numpy as jnp
from jax import lax
from jax.experimental import pallas as pl
from jax.experimental.pallas import tpu as pltpu
from jax.sharding import PartitionSpec as P

LIMIT = 28 * 1024 * 1024
HISTORY_LIMIT = 52 * 1024 * 1024
F32 = jnp.float32
PAD = 8
BF16 = jnp.bfloat16


def message_starts(layers):
    starts = [0]
    for level in range(layers):
        starts.append(starts[-1] + layers - level)
    return starts


def taps_into(s_ref, row, a, line):
    width, channels = a.shape
    line[PAD : PAD + width] = a
    s_ref[row, :, 0:channels] = line[PAD - 1 : PAD - 1 + width].astype(BF16)
    s_ref[row, :, channels : 2 * channels] = a.astype(BF16)
    s_ref[row, :, 2 * channels : 3 * channels] = line[PAD + 1 : PAD + 1 + width].astype(BF16)


def clear_lines(lines):
    edge = jnp.zeros((PAD, lines.shape[2]), F32)
    for i in range(lines.shape[0]):
        lines[i, 0:PAD] = edge
        lines[i, lines.shape[1] - PAD :] = edge


def pairs_dot(first, count, w, layer, *terms):
    width, depth = terms[0][0].shape[1:]
    channels = depth // 3
    taps = jnp.concatenate(
        [
            jnp.concatenate([s_ref[first + i + 2 * p] for p in range(count)], axis=0)
            for s_ref, _ in terms
            for i in range(4)
        ],
        axis=1,
    )
    zero = jnp.zeros((channels, channels), BF16)

    def tap(i, j, time):
        return w[layer, 3 * i + j, time] if 0 <= i < 3 else zero

    weights = jnp.concatenate(
        [
            jnp.concatenate([tap(i, j, time), tap(i - 1, j, time)], axis=1)
            for _, time in terms
            for i in range(4)
            for j in range(3)
        ],
        axis=0,
    )
    total = jnp.dot(taps, weights, preferred_element_type=F32)
    upper = total[:, :channels].reshape(count, 1, width, channels)
    lower = total[:, channels:].reshape(count, 1, width, channels)
    return jnp.concatenate([upper, lower], axis=1).reshape(2 * count, width, channels)


def history_kernel(frame, flags, caches, w, sums, inner, cross, *refs):
    layers, _, rows, width, channels = caches.shape
    begin = layers - flags[2]
    if frame == 0:
        held, wb, s, lines, sems = refs
    else:
        held, wb = caches, w
        s, lines = refs

    def loads(layer):
        return [
            pltpu.make_async_copy(caches.at[layer], held.at[layer], sems.at[layer, 0]),
            pltpu.make_async_copy(w.at[layer, :, 0:2], wb.at[layer], sems.at[layer, 1]),
        ]

    if frame == 0:
        for layer in range(layers):

            @pl.when(layer < flags[2])
            def _(layer=layer):
                for copy in loads(layer):
                    copy.start()

    clear_lines(lines)
    for f in range(frame, 2):
        s[f, 0:2] = jnp.zeros((2,) + s.shape[2:], BF16)
        s[f, rows + 2 : rows + 4] = jnp.zeros((2,) + s.shape[2:], BF16)

    def layer_step(layer, _):
        if frame == 0:
            history, taps = loads(layer)
            history.wait()

        def build(row, _):
            for f in range(frame, 2):
                taps_into(s.at[f], row + 2, held[layer, f, row].astype(F32), lines.at[f])
            return 0

        lax.fori_loop(0, rows, build, 0)
        if frame == 0:
            taps.wait()
        terms = [(s.at[f], f - frame) for f in range(frame, 2)]
        sums[begin + layer] = pairs_dot(0, (rows + 2) // 2, wb, layer, *terms).astype(BF16)
        return 0

    lax.fori_loop(0, flags[2], layer_step, 0)
    starts = message_starts(layers)

    def messages(up, down):
        for level in range(layers):
            reach = layers - level
            up[starts[level] : starts[level + 1]] = sums[level, 0:reach]
            down[starts[level] : starts[level + 1]] = sums[level, rows + 2 - reach : rows + 2]

    @pl.when(flags[1] % 2 == 0)
    def _():
        messages(cross, inner)

    @pl.when(flags[1] % 2 != 0)
    def _():
        messages(inner, cross)


def level_rows(rows, layers, level):
    return rows - layers + 1 + level, rows + 2 * (layers - 1 - level)


def pieces(count):
    parts, at = [], 0
    while at < count:
        step = 4 if count - at in (4, 8) else min(6, count - at)
        parts.append((at, step))
        at += step
    return parts


def tick_kernel(tick, segments, bands, flags, w, bias, *refs):
    zero, one = tick < segments, tick > 0
    refs = list(refs)

    def take(count):
        found, refs[:count] = refs[:count], []
        return found

    clip = take(3) if tick < 2 else None
    own, inner, cross = take(3) if one else (None, None, None)
    sums0 = take(3) if zero else None
    sums1 = take(3) if one else None
    behind = take(1)[0] if one else None
    results = take(segments) if not zero else []
    out = take(1)[0]
    kept = take(1)[0] if zero else None
    x, scratch, lines, part, sems = refs
    rows, width, channels = out.shape[-3:]
    layers = w.shape[0]
    starts = message_starts(layers)
    band = flags[1]
    begin = layers - flags[2]
    low = jnp.where(band == 0, rows, 0)
    high = jnp.where(band == bands - 1, 2 * rows, 3 * rows)

    def run(frame, fresh, own, inner, cross, sums, messages):
        def of(source):
            return source[frame] if fresh else source[...]

        x[rows : 2 * rows] = of(own)

        def gather(above, below, side_above, side_below):
            x[0:rows] = of(above)
            x[2 * rows : 3 * rows] = of(below)
            for level in range(layers):

                @pl.when(level >= begin)
                def _(level=level):
                    reach = layers - level
                    start, sums_above, sums_below = starts[level], messages[side_above], messages[side_below]
                    part[level, rows + 1 - reach : rows + 1] = sums_above[start : start + reach]
                    part[level, 2 * rows - 1 : 2 * rows - 1 + reach] = sums_below[start : start + reach]
                    part[level, rows + 1 : 2 * rows - 1] = sums[level, 2:rows]
                    part[level, rows] += sums[level, 1]
                    part[level, 2 * rows - 1] += sums[level, rows]
                    if reach > 1:
                        part[level, rows - 1] += sums[level, 0]
                        part[level, 2 * rows] += sums[level, rows + 1]

        @pl.when(band % 2 == 0)
        def _():
            gather(cross, inner, 1, 0)

        @pl.when(band % 2 != 0)
        def _():
            gather(inner, cross, 0, 1)

        clear_lines(lines)

        def build(s, row, line):
            half = x[row].astype(F32) * 0.5
            inside = jnp.logical_and(row >= low, row < high).astype(F32)
            taps_into(s, row, (half + half * jnp.tanh(half)) * inside, line)

        for level in range(layers):

            @pl.when(level >= begin)
            def _(level=level):
                layer = level - begin
                first, count = level_rows(rows, layers, level)
                s = kept.at[level] if frame == 0 else scratch

                def two(i, _):
                    build(s, first - 1 + 2 * i, lines.at[0])
                    build(s, first + 2 * i, lines.at[1])
                    return 0

                lax.fori_loop(0, count // 2 + 1, two, 0)
                offset = bias[pl.ds(layer, 1), :].reshape(1, 1, channels)
                for start, step in pieces(count):
                    at = first + start
                    mine = pairs_dot(at - 1, step // 2, w, layer, (s, 2))
                    known = part[level, at : at + step].astype(F32) + offset
                    if frame == 1:
                        known = known + behind[level, at : at + step].astype(F32)
                    x[at : at + step] = (x[at : at + step].astype(F32) + (mine + known)).astype(BF16)

        if zero:
            out[...] = x[rows : 2 * rows]
        else:
            copy = pltpu.make_async_copy(x.at[rows : 2 * rows], out.at[frame], sems.at[1])
            copy.start()
            copy.wait()

    def finished(section):
        count = 2 if section + 1 < segments else 1
        return [
            pltpu.make_async_copy(results[section + f], out.at[f], sems.at[f]) for f in range(count)
        ]

    for section in range(len(results)):

        @pl.when(flags[0] == section)
        def _(section=section):
            for copy in finished(section):
                copy.start()

    for frame, present, parts in ((0, zero, sums0), (1, one, sums1)):
        if present:
            fresh = tick == frame

            @pl.when(flags[0] == tick - frame)
            def _(frame=frame, fresh=fresh, parts=parts):
                run(frame, fresh, *(clip if fresh else (own, inner, cross)), parts[0], parts[1:])

    for section in range(len(results)):

        @pl.when(flags[0] == section)
        def _(section=section):
            for copy in finished(section):
                copy.wait()


def ahead_kernel(tick, flags, w, kept, ahead):
    layers, rows = kept.shape[0], kept.shape[1] // 3
    begin = layers - flags[2]

    @pl.when(flags[0] == tick)
    def _():
        for level in range(layers):

            @pl.when(level >= begin)
            def _(level=level):
                first, count = level_rows(rows, layers, level)
                for start, step in pieces(count):
                    at = first + start
                    ahead[level, at : at + step] = pairs_dot(
                        at - 1, step // 2, w, level - begin, (kept.at[level], 1)
                    ).astype(BF16)


def in_vmem(count):
    return [pl.BlockSpec(memory_space=pltpu.VMEM)] * count


def anywhere():
    return pl.BlockSpec(memory_space=pl.ANY)


def in_smem():
    return pl.BlockSpec(memory_space=pltpu.SMEM)


def history_call(frame, flags, caches, weights):
    layers, _, rows, width, channels = caches.shape
    row = (width, channels)
    message = jax.ShapeDtypeStruct((message_starts(layers)[-1],) + row, BF16)
    outs = [jax.ShapeDtypeStruct((layers, rows + 2) + row, BF16), message, message]
    specs = in_vmem(3)
    scratch = [pltpu.VMEM((2, rows + 4, width, 3 * channels), BF16), pltpu.VMEM((2, width + 2 * PAD, channels), F32)]
    if frame == 0:
        scratch = [
            pltpu.VMEM(caches.shape, BF16),
            pltpu.VMEM((layers, 9, 2, channels, channels), BF16),
            *scratch,
            pltpu.SemaphoreType.DMA((layers, 2)),
        ]
    pixels = layers * (rows + 2) * width
    return pl.pallas_call(
        functools.partial(history_kernel, frame),
        out_shape=tuple(outs),
        in_specs=[in_smem()] + ([anywhere()] * 2 if frame == 0 else in_vmem(2)),
        out_specs=tuple(specs),
        scratch_shapes=scratch,
        compiler_params=pltpu.CompilerParams(vmem_limit_bytes=HISTORY_LIMIT if frame == 0 else LIMIT),
        cost_estimate=pl.CostEstimate(
            flops=pixels * 9 * 2 * (2 - frame) * channels * channels, bytes_accessed=4000000, transcendentals=0
        ),
        name="history",
    )(flags, caches, weights)


def tick_call(tick, segments, bands, flags, clip, received, weights, biases, sums0, sums1, behind, results):
    layers, _, _, channels, _ = weights.shape
    rows, width = clip[0].shape[1:3]
    every = (layers, 3 * rows, width, channels)
    pixels = sum(rows + 2 * level for level in range(layers)) * width
    zero, one = tick < segments, tick > 0
    extra = (list(clip) if tick < 2 else []) + (list(received) if one else [])
    extra += (list(sums0) if zero else []) + (list(sums1) + [behind] if one else [])
    if zero:
        outs = [jax.ShapeDtypeStruct((rows, width, channels), BF16), jax.ShapeDtypeStruct(every[:3] + (3 * channels,), BF16)]
        specs = in_vmem(2)
    else:
        extra += results
        outs, specs = [jax.ShapeDtypeStruct(clip[0].shape, BF16)], [anywhere()]
    return pl.pallas_call(
        functools.partial(tick_kernel, tick, segments, bands),
        out_shape=tuple(outs),
        in_specs=[in_smem()] + in_vmem(2 + len(extra)),
        out_specs=tuple(specs),
        scratch_shapes=[
            pltpu.VMEM((3 * rows, width, channels), BF16),
            pltpu.VMEM((3 * rows, width, 3 * channels), BF16),
            pltpu.VMEM((2, width + 2 * PAD, channels), F32),
            pltpu.VMEM(every, BF16),
            pltpu.SemaphoreType.DMA((2,)),
        ],
        compiler_params=pltpu.CompilerParams(vmem_limit_bytes=LIMIT),
        cost_estimate=pl.CostEstimate(
            flops=pixels * 9 * 2 * channels * channels, bytes_accessed=4000000, transcendentals=pixels * channels
        ),
        name="tick",
    )(flags, weights, biases, *extra)


def ahead_call(tick, flags, weights, kept):
    layers, extent, width, depth = kept.shape
    return pl.pallas_call(
        functools.partial(ahead_kernel, tick),
        out_shape=jax.ShapeDtypeStruct((layers, extent, width, depth // 3), BF16),
        in_specs=[in_smem()] + in_vmem(2),
        out_specs=in_vmem(1)[0],
        compiler_params=pltpu.CompilerParams(vmem_limit_bytes=LIMIT),
        cost_estimate=pl.CostEstimate(
            flops=1000000, bytes_accessed=1000000, transcendentals=0
        ),
        name="ahead",
    )(flags, weights, kept)


def per_device(clip, caches, weights, biases, section_layers):
    segments = lax.axis_size("segment")
    bands = lax.axis_size("band")
    caches, weights, biases = caches[0], weights[0], biases[0]
    flags = jnp.stack([lax.axis_index("segment"), lax.axis_index("band"), section_layers[0]]).astype(jnp.int32)
    axes = ("segment", "band")
    in_chip = [(b, b ^ 1) for b in range(bands)]
    between = [(b, b + 1) for b in range(1, bands - 1, 2)] + [(b + 1, b) for b in range(1, bands - 1, 2)]
    straight = [(b, b) for b in range(bands)]

    def swap(value, pairs, chosen):
        return lax.ppermute(value, axes, [(s * bands + a, s * bands + b) for s in chosen for a, b in pairs])

    def ahead(value, pairs, sources):
        return lax.ppermute(value, axes, [(s * bands + a, (s + 1) * bands + b) for s in sources for a, b in pairs])

    def lender(value, pairs):
        source = min(1, segments - 1)
        return lax.ppermute(value, axes, [(source * bands + a, b) for a, b in pairs])

    everyone = range(segments)
    clip_cross = lender(clip, between)
    clip_in = swap(clip, in_chip, [0])
    sums, inner, cross = history_call(0, flags, caches, weights)
    sums0 = (sums, swap(inner, in_chip, everyone), swap(cross, between, everyone))
    caches, clip_cross, _ = lax.optimization_barrier((caches, clip_cross, sums))
    sums, inner, cross = history_call(1, flags, caches, weights)
    sums1 = (sums, swap(inner, in_chip, everyone), swap(cross, between, everyone))
    halves = (clip, clip_in, clip_cross)
    received = behind = None
    results = []
    for tick in range(segments + 1):
        x, *later = tick_call(
            tick, segments, bands, flags, halves, received, weights, biases, sums0, sums1, behind, results
        )
        if tick < segments:
            behind = ahead_call(tick, flags, weights, later[0])
            results.append(x)
            sources = [s for s in (tick, tick - 1) if 0 <= s < segments - 1]
            own, cross = ahead(x, straight, sources), ahead(x, between, sources)
            own, behind = lax.optimization_barrier((own, behind))
            received = (own, swap(own, in_chip, [s + 1 for s in sources]), cross)
    return x[None]


def solution(mesh):
    placed = (
        P(None, "band", None, None),
        P("segment", None, None, "band", None, None),
        P("segment", None, None, None, None, None),
        P("segment", None, None),
        P("segment"),
    )
    return jax.shard_map(
        per_device,
        mesh=mesh,
        in_specs=placed,
        out_specs=P("segment", None, "band", None, None),
        check_vma=False,
    )
```

```python
import functools

import jax
import jax.numpy as jnp
from jax import lax
from jax.experimental import pallas as pl
from jax.experimental.pallas import tpu as pltpu
from jax.sharding import PartitionSpec as P

LIMIT = 28 * 1024 * 1024
HISTORY_LIMIT = 52 * 1024 * 1024
F32 = jnp.float32
PAD = 8
BF16 = jnp.bfloat16


def message_starts(layers):
    starts = [0]
    for level in range(layers):
        starts.append(starts[-1] + layers - level)
    return starts


def taps_into(s_ref, row, a, line):
    width, channels = a.shape
    line[PAD : PAD + width] = a
    s_ref[row, :, 0:channels] = line[PAD - 1 : PAD - 1 + width].astype(BF16)
    s_ref[row, :, channels : 2 * channels] = a.astype(BF16)
    s_ref[row, :, 2 * channels : 3 * channels] = line[PAD + 1 : PAD + 1 + width].astype(BF16)


def clear_lines(lines):
    edge = jnp.zeros((PAD, lines.shape[2]), F32)
    for i in range(lines.shape[0]):
        lines[i, 0:PAD] = edge
        lines[i, lines.shape[1] - PAD :] = edge


def pairs_dot(first, count, w, layer, *terms):
    width, depth = terms[0][0].shape[1:]
    channels = depth // 3
    taps = jnp.concatenate(
        [
            jnp.concatenate([s_ref[first + i + 2 * p] for p in range(count)], axis=0)
            for s_ref, _ in terms
            for i in range(4)
        ],
        axis=1,
    )
    zero = jnp.zeros((channels, channels), BF16)

    def tap(i, j, time):
        return w[layer, 3 * i + j, time] if 0 <= i < 3 else zero

    weights = jnp.concatenate(
        [
            jnp.concatenate([tap(i, j, time), tap(i - 1, j, time)], axis=1)
            for _, time in terms
            for i in range(4)
            for j in range(3)
        ],
        axis=0,
    )
    total = jnp.dot(taps, weights, preferred_element_type=F32)
    upper = total[:, :channels].reshape(count, 1, width, channels)
    lower = total[:, channels:].reshape(count, 1, width, channels)
    return jnp.concatenate([upper, lower], axis=1).reshape(2 * count, width, channels)


def history_kernel(frame, flags, caches, w, sums, inner, cross, *refs):
    layers, _, rows, width, channels = caches.shape
    begin = layers - flags[2]
    if frame == 0:
        held, wb, s, lines, sems = refs
    else:
        held, wb = caches, w
        s, lines = refs

    def loads(layer):
        return [
            pltpu.make_async_copy(caches.at[layer], held.at[layer], sems.at[layer, 0]),
            pltpu.make_async_copy(w.at[layer, :, 0:2], wb.at[layer], sems.at[layer, 1]),
        ]

    if frame == 0:
        for layer in range(layers):

            @pl.when(layer < flags[2])
            def _(layer=layer):
                for copy in loads(layer):
                    copy.start()

    clear_lines(lines)
    for f in range(frame, 2):
        s[f, 0:2] = jnp.zeros((2,) + s.shape[2:], BF16)
        s[f, rows + 2 : rows + 4] = jnp.zeros((2,) + s.shape[2:], BF16)

    def layer_step(layer, _):
        if frame == 0:
            history, taps = loads(layer)
            history.wait()

        def build(row, _):
            for f in range(frame, 2):
                taps_into(s.at[f], row + 2, held[layer, f, row].astype(F32), lines.at[f])
            return 0

        lax.fori_loop(0, rows, build, 0)
        if frame == 0:
            taps.wait()
        terms = [(s.at[f], f - frame) for f in range(frame, 2)]
        sums[begin + layer] = pairs_dot(0, (rows + 2) // 2, wb, layer, *terms).astype(BF16)
        return 0

    lax.fori_loop(0, flags[2], layer_step, 0)
    starts = message_starts(layers)

    def messages(up, down):
        for level in range(layers):
            reach = layers - level
            up[starts[level] : starts[level + 1]] = sums[level, 0:reach]
            down[starts[level] : starts[level + 1]] = sums[level, rows + 2 - reach : rows + 2]

    @pl.when(flags[1] % 2 == 0)
    def _():
        messages(cross, inner)

    @pl.when(flags[1] % 2 != 0)
    def _():
        messages(inner, cross)


def level_rows(rows, layers, level):
    return rows - layers + 1 + level, rows + 2 * (layers - 1 - level)


def tick_kernel(tick, segments, bands, flags, w, bias, *refs):
    zero, one = tick < segments, tick > 0
    refs = list(refs)

    def take(count):
        found, refs[:count] = refs[:count], []
        return found

    clip = take(3) if tick < 2 else None
    own, inner, cross = take(3) if one else (None, None, None)
    sums0 = take(3) if zero else None
    sums1 = take(3) if one else None
    behind = take(1)[0] if one else None
    results = take(segments) if not zero else []
    out = take(1)[0]
    kept = take(1)[0] if zero else None
    x, scratch, lines, part, sems = refs
    rows, width, channels = out.shape[-3:]
    layers = w.shape[0]
    starts = message_starts(layers)
    band = flags[1]
    begin = layers - flags[2]
    low = jnp.where(band == 0, rows, 0)
    high = jnp.where(band == bands - 1, 2 * rows, 3 * rows)

    def run(frame, fresh, own, inner, cross, sums, messages):
        def of(source):
            return source[frame] if fresh else source[...]

        x[rows : 2 * rows] = of(own)

        def gather(above, below, side_above, side_below):
            x[0:rows] = of(above)
            x[2 * rows : 3 * rows] = of(below)
            for level in range(layers):

                @pl.when(level >= begin)
                def _(level=level):
                    reach = layers - level
                    start, sums_above, sums_below = starts[level], messages[side_above], messages[side_below]
                    part[level, rows + 1 - reach : rows + 1] = sums_above[start : start + reach]
                    part[level, 2 * rows - 1 : 2 * rows - 1 + reach] = sums_below[start : start + reach]
                    part[level, rows + 1 : 2 * rows - 1] = sums[level, 2:rows]
                    part[level, rows] += sums[level, 1]
                    part[level, 2 * rows - 1] += sums[level, rows]
                    if reach > 1:
                        part[level, rows - 1] += sums[level, 0]
                        part[level, 2 * rows] += sums[level, rows + 1]

        @pl.when(band % 2 == 0)
        def _():
            gather(cross, inner, 1, 0)

        @pl.when(band % 2 != 0)
        def _():
            gather(inner, cross, 0, 1)

        clear_lines(lines)

        def build(s, row, line):
            half = x[row].astype(F32) * 0.5
            inside = jnp.logical_and(row >= low, row < high).astype(F32)
            taps_into(s, row, (half + half * jnp.tanh(half)) * inside, line)

        for level in range(layers):

            @pl.when(level >= begin)
            def _(level=level):
                layer = level - begin
                first, count = level_rows(rows, layers, level)
                s = kept.at[level] if frame == 0 else scratch

                def two(i, _):
                    build(s, first - 1 + 2 * i, lines.at[0])
                    build(s, first + 2 * i, lines.at[1])
                    return 0

                lax.fori_loop(0, count // 2 + 1, two, 0)
                offset = bias[pl.ds(layer, 1), :].reshape(1, 1, channels)
                end = first + count
                mine = pairs_dot(first - 1, count // 2, w, layer, (s, 2))
                known = part[level, first:end].astype(F32) + offset
                if frame == 1:
                    known = known + behind[level, first:end].astype(F32)
                x[first:end] = (x[first:end].astype(F32) + (mine + known)).astype(BF16)

        if zero:
            out[...] = x[rows : 2 * rows]
        else:
            copy = pltpu.make_async_copy(x.at[rows : 2 * rows], out.at[frame], sems.at[1])
            copy.start()
            copy.wait()

    def finished(section):
        count = 2 if section + 1 < segments else 1
        return [
            pltpu.make_async_copy(results[section + f], out.at[f], sems.at[f]) for f in range(count)
        ]

    for section in range(len(results)):

        @pl.when(flags[0] == section)
        def _(section=section):
            for copy in finished(section):
                copy.start()

    for frame, present, parts in ((0, zero, sums0), (1, one, sums1)):
        if present:
            fresh = tick == frame

            @pl.when(flags[0] == tick - frame)
            def _(frame=frame, fresh=fresh, parts=parts):
                run(frame, fresh, *(clip if fresh else (own, inner, cross)), parts[0], parts[1:])

    for section in range(len(results)):

        @pl.when(flags[0] == section)
        def _(section=section):
            for copy in finished(section):
                copy.wait()


def ahead_kernel(tick, flags, w, kept, ahead):
    layers, rows = kept.shape[0], kept.shape[1] // 3
    begin = layers - flags[2]

    @pl.when(flags[0] == tick)
    def _():
        for level in range(layers):

            @pl.when(level >= begin)
            def _(level=level):
                first, count = level_rows(rows, layers, level)
                total = pairs_dot(first - 1, count // 2, w, level - begin, (kept.at[level], 1))
                ahead[level, first : first + count] = total.astype(BF16)


def in_vmem(count):
    return [pl.BlockSpec(memory_space=pltpu.VMEM)] * count


def anywhere():
    return pl.BlockSpec(memory_space=pl.ANY)


def in_smem():
    return pl.BlockSpec(memory_space=pltpu.SMEM)


def history_call(frame, flags, caches, weights):
    layers, _, rows, width, channels = caches.shape
    row = (width, channels)
    message = jax.ShapeDtypeStruct((message_starts(layers)[-1],) + row, BF16)
    outs = [jax.ShapeDtypeStruct((layers, rows + 2) + row, BF16), message, message]
    specs = in_vmem(3)
    scratch = [pltpu.VMEM((2, rows + 4, width, 3 * channels), BF16), pltpu.VMEM((2, width + 2 * PAD, channels), F32)]
    if frame == 0:
        scratch = [
            pltpu.VMEM(caches.shape, BF16),
            pltpu.VMEM((layers, 9, 2, channels, channels), BF16),
            *scratch,
            pltpu.SemaphoreType.DMA((layers, 2)),
        ]
    pixels = layers * (rows + 2) * width
    return pl.pallas_call(
        functools.partial(history_kernel, frame),
        out_shape=tuple(outs),
        in_specs=[in_smem()] + ([anywhere()] * 2 if frame == 0 else in_vmem(2)),
        out_specs=tuple(specs),
        scratch_shapes=scratch,
        compiler_params=pltpu.CompilerParams(vmem_limit_bytes=HISTORY_LIMIT if frame == 0 else LIMIT),
        cost_estimate=pl.CostEstimate(
            flops=pixels * 9 * 2 * (2 - frame) * channels * channels, bytes_accessed=4000000, transcendentals=0
        ),
        name="history",
    )(flags, caches, weights)


def tick_call(tick, segments, bands, flags, clip, received, weights, biases, sums0, sums1, behind, results):
    layers, _, _, channels, _ = weights.shape
    rows, width = clip[0].shape[1:3]
    every = (layers, 3 * rows, width, channels)
    pixels = sum(rows + 2 * level for level in range(layers)) * width
    zero, one = tick < segments, tick > 0
    extra = (list(clip) if tick < 2 else []) + (list(received) if one else [])
    extra += (list(sums0) if zero else []) + (list(sums1) + [behind] if one else [])
    if zero:
        outs = [jax.ShapeDtypeStruct((rows, width, channels), BF16), jax.ShapeDtypeStruct(every[:3] + (3 * channels,), BF16)]
        specs = in_vmem(2)
    else:
        extra += results
        outs, specs = [jax.ShapeDtypeStruct(clip[0].shape, BF16)], [anywhere()]
    return pl.pallas_call(
        functools.partial(tick_kernel, tick, segments, bands),
        out_shape=tuple(outs),
        in_specs=[in_smem()] + in_vmem(2 + len(extra)),
        out_specs=tuple(specs),
        scratch_shapes=[
            pltpu.VMEM((3 * rows, width, channels), BF16),
            pltpu.VMEM((3 * rows, width, 3 * channels), BF16),
            pltpu.VMEM((2, width + 2 * PAD, channels), F32),
            pltpu.VMEM(every, BF16),
            pltpu.SemaphoreType.DMA((2,)),
        ],
        compiler_params=pltpu.CompilerParams(vmem_limit_bytes=LIMIT),
        cost_estimate=pl.CostEstimate(
            flops=pixels * 9 * 2 * channels * channels, bytes_accessed=4000000, transcendentals=pixels * channels
        ),
        name="tick",
    )(flags, weights, biases, *extra)


def ahead_call(tick, flags, weights, kept):
    layers, extent, width, depth = kept.shape
    return pl.pallas_call(
        functools.partial(ahead_kernel, tick),
        out_shape=jax.ShapeDtypeStruct((layers, extent, width, depth // 3), BF16),
        in_specs=[in_smem()] + in_vmem(2),
        out_specs=in_vmem(1)[0],
        compiler_params=pltpu.CompilerParams(vmem_limit_bytes=LIMIT),
        cost_estimate=pl.CostEstimate(
            flops=1000000, bytes_accessed=1000000, transcendentals=0
        ),
        name="ahead",
    )(flags, weights, kept)


def per_device(clip, caches, weights, biases, section_layers):
    segments = lax.axis_size("segment")
    bands = lax.axis_size("band")
    caches, weights, biases = caches[0], weights[0], biases[0]
    flags = jnp.stack([lax.axis_index("segment"), lax.axis_index("band"), section_layers[0]]).astype(jnp.int32)
    axes = ("segment", "band")
    in_chip = [(b, b ^ 1) for b in range(bands)]
    between = [(b, b + 1) for b in range(1, bands - 1, 2)] + [(b + 1, b) for b in range(1, bands - 1, 2)]
    straight = [(b, b) for b in range(bands)]

    def swap(value, pairs, chosen):
        return lax.ppermute(value, axes, [(s * bands + a, s * bands + b) for s in chosen for a, b in pairs])

    def ahead(value, pairs, sources):
        return lax.ppermute(value, axes, [(s * bands + a, (s + 1) * bands + b) for s in sources for a, b in pairs])

    def lender(value, pairs):
        source = min(1, segments - 1)
        return lax.ppermute(value, axes, [(source * bands + a, b) for a, b in pairs])

    everyone = range(segments)
    clip_cross = lender(clip, between)
    clip_in = swap(clip, in_chip, [0])
    sums, inner, cross = history_call(0, flags, caches, weights)
    sums0 = (sums, swap(inner, in_chip, everyone), swap(cross, between, everyone))
    caches, clip_cross, _ = lax.optimization_barrier((caches, clip_cross, sums))
    sums, inner, cross = history_call(1, flags, caches, weights)
    sums1 = (sums, swap(inner, in_chip, everyone), swap(cross, between, everyone))
    halves = (clip, clip_in, clip_cross)
    received = behind = None
    results = []
    for tick in range(segments + 1):
        x, *later = tick_call(
            tick, segments, bands, flags, halves, received, weights, biases, sums0, sums1, behind, results
        )
        if tick < segments:
            behind = ahead_call(tick, flags, weights, later[0])
            results.append(x)
            sources = [s for s in (tick, tick - 1) if 0 <= s < segments - 1]
            own, cross = ahead(x, straight, sources), ahead(x, between, sources)
            own, behind = lax.optimization_barrier((own, behind))
            received = (own, swap(own, in_chip, [s + 1 for s in sources]), cross)
    return x[None]


def solution(mesh):
    placed = (
        P(None, "band", None, None),
        P("segment", None, None, "band", None, None),
        P("segment", None, None, None, None, None),
        P("segment", None, None),
        P("segment"),
    )
    return jax.shard_map(
        per_device,
        mesh=mesh,
        in_specs=placed,
        out_specs=P("segment", None, "band", None, None),
        check_vma=False,
    )
```

```python
import functools

import jax
import jax.numpy as jnp
from jax import lax
from jax.experimental import pallas as pl
from jax.experimental.pallas import tpu as pltpu
from jax.sharding import PartitionSpec as P

LIMIT = 28 * 1024 * 1024
HISTORY_LIMIT = 52 * 1024 * 1024
F32 = jnp.float32
PAD = 8
BF16 = jnp.bfloat16


def message_starts(layers):
    starts = [0]
    for level in range(layers):
        starts.append(starts[-1] + layers - level)
    return starts


def taps_into(s_ref, row, a, line):
    width, channels = a.shape
    line[PAD : PAD + width] = a
    s_ref[row, :, 0:channels] = line[PAD - 1 : PAD - 1 + width].astype(BF16)
    s_ref[row, :, channels : 2 * channels] = a.astype(BF16)
    s_ref[row, :, 2 * channels : 3 * channels] = line[PAD + 1 : PAD + 1 + width].astype(BF16)


def clear_lines(lines):
    edge = jnp.zeros((PAD, lines.shape[2]), F32)
    for i in range(lines.shape[0]):
        lines[i, 0:PAD] = edge
        lines[i, lines.shape[1] - PAD :] = edge


def pairs_dot(first, count, w, layer, *terms):
    width, depth = terms[0][0].shape[1:]
    channels = depth // 3
    taps = jnp.concatenate(
        [
            jnp.concatenate([s_ref[first + i + 2 * p] for p in range(count)], axis=0)
            for s_ref, _ in terms
            for i in range(4)
        ],
        axis=1,
    )
    zero = jnp.zeros((channels, channels), BF16)

    def tap(i, j, time):
        return w[layer, 3 * i + j, time] if 0 <= i < 3 else zero

    weights = jnp.concatenate(
        [
            jnp.concatenate([tap(i, j, time), tap(i - 1, j, time)], axis=1)
            for _, time in terms
            for i in range(4)
            for j in range(3)
        ],
        axis=0,
    )
    total = jnp.dot(taps, weights, preferred_element_type=F32)
    upper = total[:, :channels].reshape(count, 1, width, channels)
    lower = total[:, channels:].reshape(count, 1, width, channels)
    return jnp.concatenate([upper, lower], axis=1).reshape(2 * count, width, channels)


def history_kernel(frame, flags, caches, w, sums, inner, cross, *refs):
    layers, _, rows, width, channels = caches.shape
    begin = layers - flags[2]
    if frame == 0:
        held, wb, s, lines, sems = refs
    else:
        held, wb = caches, w
        s, lines = refs

    def loads(layer):
        return [
            pltpu.make_async_copy(caches.at[layer], held.at[layer], sems.at[layer, 0]),
            pltpu.make_async_copy(w.at[layer, :, 0:2], wb.at[layer], sems.at[layer, 1]),
        ]

    if frame == 0:
        for layer in range(layers):

            @pl.when(layer < flags[2])
            def _(layer=layer):
                for copy in loads(layer):
                    copy.start()

    clear_lines(lines)
    for f in range(frame, 2):
        s[f, 0:2] = jnp.zeros((2,) + s.shape[2:], BF16)
        s[f, rows + 2 : rows + 4] = jnp.zeros((2,) + s.shape[2:], BF16)

    def layer_step(layer, _):
        if frame == 0:
            history, taps = loads(layer)
            history.wait()

        def build(row, _):
            for f in range(frame, 2):
                taps_into(s.at[f], row + 2, held[layer, f, row].astype(F32), lines.at[f])
            return 0

        lax.fori_loop(0, rows, build, 0)
        if frame == 0:
            taps.wait()
        terms = [(s.at[f], f - frame) for f in range(frame, 2)]
        sums[begin + layer] = pairs_dot(0, (rows + 2) // 2, wb, layer, *terms).astype(BF16)
        return 0

    lax.fori_loop(0, flags[2], layer_step, 0)
    starts = message_starts(layers)

    def messages(up, down):
        for level in range(layers):
            reach = layers - level
            up[starts[level] : starts[level + 1]] = sums[level, 0:reach]
            down[starts[level] : starts[level + 1]] = sums[level, rows + 2 - reach : rows + 2]

    @pl.when(flags[1] % 2 == 0)
    def _():
        messages(cross, inner)

    @pl.when(flags[1] % 2 != 0)
    def _():
        messages(inner, cross)


def level_rows(rows, layers, level):
    return rows - layers + 1 + level, rows + 2 * (layers - 1 - level)


def parts_of(tick, segments, part_of):
    return tick < segments and part_of != 1, tick > 0 and part_of != 0, tick == segments


def tick_kernel(tick, segments, bands, part_of, flags, w, bias, *refs):
    zero, one, final = parts_of(tick, segments, part_of)
    refs = list(refs)

    def take(count):
        found, refs[:count] = refs[:count], []
        return found

    clip = take(3) if tick < 2 else None
    own, inner, cross = take(3) if tick > 0 else (None, None, None)
    sums0 = take(3) if zero else None
    sums1 = take(3) if one else None
    behind = take(1)[0] if one else None
    results = take(segments + 1) if final else []
    out = take(1)[0]
    kept = take(1)[0] if zero else None
    x, scratch, lines, part, sems = refs
    rows, width, channels = out.shape[-3:]
    layers = w.shape[0]
    starts = message_starts(layers)
    band = flags[1]
    begin = layers - flags[2]
    low = jnp.where(band == 0, rows, 0)
    high = jnp.where(band == bands - 1, 2 * rows, 3 * rows)

    def run(frame, fresh, own, inner, cross, sums, messages):
        def of(source):
            return source[frame] if fresh else source[...]

        x[rows : 2 * rows] = of(own)

        def gather(above, below, side_above, side_below):
            x[0:rows] = of(above)
            x[2 * rows : 3 * rows] = of(below)
            for level in range(layers):

                @pl.when(level >= begin)
                def _(level=level):
                    reach = layers - level
                    start, sums_above, sums_below = starts[level], messages[side_above], messages[side_below]
                    part[level, rows + 1 - reach : rows + 1] = sums_above[start : start + reach]
                    part[level, 2 * rows - 1 : 2 * rows - 1 + reach] = sums_below[start : start + reach]
                    part[level, rows + 1 : 2 * rows - 1] = sums[level, 2:rows]
                    part[level, rows] += sums[level, 1]
                    part[level, 2 * rows - 1] += sums[level, rows]
                    if reach > 1:
                        part[level, rows - 1] += sums[level, 0]
                        part[level, 2 * rows] += sums[level, rows + 1]

        @pl.when(band % 2 == 0)
        def _():
            gather(cross, inner, 1, 0)

        @pl.when(band % 2 != 0)
        def _():
            gather(inner, cross, 0, 1)

        clear_lines(lines)

        def build(s, row, line):
            half = x[row].astype(F32) * 0.5
            inside = jnp.logical_and(row >= low, row < high).astype(F32)
            taps_into(s, row, (half + half * jnp.tanh(half)) * inside, line)

        for level in range(layers):

            @pl.when(level >= begin)
            def _(level=level):
                layer = level - begin
                first, count = level_rows(rows, layers, level)
                s = kept.at[level] if frame == 0 else scratch

                def two(i, _):
                    build(s, first - 1 + 2 * i, lines.at[0])
                    build(s, first + 2 * i, lines.at[1])
                    return 0

                lax.fori_loop(0, count // 2 + 1, two, 0)
                offset = bias[pl.ds(layer, 1), :].reshape(1, 1, channels)
                end = first + count
                mine = pairs_dot(first - 1, count // 2, w, layer, (s, 2))
                known = part[level, first:end].astype(F32) + offset
                if frame == 1:
                    known = known + behind[level, first:end].astype(F32)
                x[first:end] = (x[first:end].astype(F32) + (mine + known)).astype(BF16)

        if not final:
            out[...] = x[rows : 2 * rows]
        else:
            copy = pltpu.make_async_copy(x.at[rows : 2 * rows], out.at[frame], sems.at[1])
            copy.start()
            copy.wait()

    def finished(section):
        count = 2 if section + 1 < segments else 1
        found = [results[segments if count == 1 else section], results[section + 1]]
        return [pltpu.make_async_copy(found[f], out.at[f], sems.at[f]) for f in range(count)]

    for section in range(segments if final else 0):

        @pl.when(flags[0] == section)
        def _(section=section):
            for copy in finished(section):
                copy.start()

    for frame, present, parts in ((0, zero, sums0), (1, one, sums1)):
        if present:
            fresh = tick == frame

            @pl.when(flags[0] == tick - frame)
            def _(frame=frame, fresh=fresh, parts=parts):
                run(frame, fresh, *(clip if fresh else (own, inner, cross)), parts[0], parts[1:])

    for section in range(segments if final else 0):

        @pl.when(flags[0] == section)
        def _(section=section):
            for copy in finished(section):
                copy.wait()


def ahead_kernel(tick, flags, w, kept, ahead):
    layers, rows = kept.shape[0], kept.shape[1] // 3
    begin = layers - flags[2]

    @pl.when(flags[0] == tick)
    def _():
        for level in range(layers):

            @pl.when(level >= begin)
            def _(level=level):
                first, count = level_rows(rows, layers, level)
                total = pairs_dot(first - 1, count // 2, w, level - begin, (kept.at[level], 1))
                ahead[level, first : first + count] = total.astype(BF16)


def in_vmem(count):
    return [pl.BlockSpec(memory_space=pltpu.VMEM)] * count


def anywhere():
    return pl.BlockSpec(memory_space=pl.ANY)


def in_smem():
    return pl.BlockSpec(memory_space=pltpu.SMEM)


def history_call(frame, flags, caches, weights):
    layers, _, rows, width, channels = caches.shape
    row = (width, channels)
    message = jax.ShapeDtypeStruct((message_starts(layers)[-1],) + row, BF16)
    outs = [jax.ShapeDtypeStruct((layers, rows + 2) + row, BF16), message, message]
    specs = in_vmem(3)
    scratch = [pltpu.VMEM((2, rows + 4, width, 3 * channels), BF16), pltpu.VMEM((2, width + 2 * PAD, channels), F32)]
    if frame == 0:
        scratch = [
            pltpu.VMEM(caches.shape, BF16),
            pltpu.VMEM((layers, 9, 2, channels, channels), BF16),
            *scratch,
            pltpu.SemaphoreType.DMA((layers, 2)),
        ]
    pixels = layers * (rows + 2) * width
    return pl.pallas_call(
        functools.partial(history_kernel, frame),
        out_shape=tuple(outs),
        in_specs=[in_smem()] + ([anywhere()] * 2 if frame == 0 else in_vmem(2)),
        out_specs=tuple(specs),
        scratch_shapes=scratch,
        compiler_params=pltpu.CompilerParams(vmem_limit_bytes=HISTORY_LIMIT if frame == 0 else LIMIT),
        cost_estimate=pl.CostEstimate(
            flops=pixels * 9 * 2 * (2 - frame) * channels * channels, bytes_accessed=4000000, transcendentals=0
        ),
        name="history",
    )(flags, caches, weights)


def tick_call(tick, segments, bands, part_of, flags, clip, received, weights, biases, sums0, sums1, behind, results):
    layers, _, _, channels, _ = weights.shape
    rows, width = clip[0].shape[1:3]
    every = (layers, 3 * rows, width, channels)
    pixels = sum(rows + 2 * level for level in range(layers)) * width
    zero, one, final = parts_of(tick, segments, part_of)
    extra = (list(clip) if tick < 2 else []) + (list(received) if tick > 0 else [])
    extra += (list(sums0) if zero else []) + (list(sums1) + [behind] if one else [])
    outs, specs = [jax.ShapeDtypeStruct((rows, width, channels), BF16)], in_vmem(1)
    if zero:
        outs.append(jax.ShapeDtypeStruct(every[:3] + (3 * channels,), BF16))
        specs += in_vmem(1)
    if final:
        extra += results
        outs, specs = [jax.ShapeDtypeStruct(clip[0].shape, BF16)], [anywhere()]
    return pl.pallas_call(
        functools.partial(tick_kernel, tick, segments, bands, part_of),
        out_shape=tuple(outs),
        in_specs=[in_smem()] + in_vmem(2 + len(extra)),
        out_specs=tuple(specs),
        scratch_shapes=[
            pltpu.VMEM((3 * rows, width, channels), BF16),
            pltpu.VMEM((3 * rows, width, 3 * channels), BF16),
            pltpu.VMEM((2, width + 2 * PAD, channels), F32),
            pltpu.VMEM(every, BF16),
            pltpu.SemaphoreType.DMA((2,)),
        ],
        compiler_params=pltpu.CompilerParams(vmem_limit_bytes=LIMIT),
        cost_estimate=pl.CostEstimate(
            flops=pixels * 9 * 2 * channels * channels, bytes_accessed=4000000, transcendentals=pixels * channels
        ),
        name="tick",
    )(flags, weights, biases, *extra)


def ahead_call(tick, flags, weights, kept):
    layers, extent, width, depth = kept.shape
    return pl.pallas_call(
        functools.partial(ahead_kernel, tick),
        out_shape=jax.ShapeDtypeStruct((layers, extent, width, depth // 3), BF16),
        in_specs=[in_smem()] + in_vmem(2),
        out_specs=in_vmem(1)[0],
        compiler_params=pltpu.CompilerParams(vmem_limit_bytes=LIMIT),
        cost_estimate=pl.CostEstimate(
            flops=1000000, bytes_accessed=1000000, transcendentals=0
        ),
        name="ahead",
    )(flags, weights, kept)


def per_device(clip, caches, weights, biases, section_layers):
    segments = lax.axis_size("segment")
    bands = lax.axis_size("band")
    caches, weights, biases = caches[0], weights[0], biases[0]
    flags = jnp.stack([lax.axis_index("segment"), lax.axis_index("band"), section_layers[0]]).astype(jnp.int32)
    axes = ("segment", "band")
    in_chip = [(b, b ^ 1) for b in range(bands)]
    between = [(b, b + 1) for b in range(1, bands - 1, 2)] + [(b + 1, b) for b in range(1, bands - 1, 2)]
    straight = [(b, b) for b in range(bands)]

    def swap(value, pairs, chosen):
        return lax.ppermute(value, axes, [(s * bands + a, s * bands + b) for s in chosen for a, b in pairs])

    def ahead(value, pairs, sources):
        return lax.ppermute(value, axes, [(s * bands + a, (s + 1) * bands + b) for s in sources for a, b in pairs])

    def lender(value, pairs):
        source = min(1, segments - 1)
        return lax.ppermute(value, axes, [(source * bands + a, b) for a, b in pairs])

    everyone = range(segments)
    clip_cross = lender(clip, between)
    clip_in = swap(clip, in_chip, [0])
    sums, inner, cross = history_call(0, flags, caches, weights)
    sums0 = (sums, swap(inner, in_chip, everyone), swap(cross, between, everyone))
    caches, clip_cross, _ = lax.optimization_barrier((caches, clip_cross, sums))
    sums, inner, cross = history_call(1, flags, caches, weights)
    sums1 = (sums, swap(inner, in_chip, everyone), swap(cross, between, everyone))
    halves = (clip, clip_in, clip_cross)
    received = behind = None
    results = []
    for tick in range(segments + 1):
        def call(part_of):
            return tick_call(
                tick, segments, bands, part_of, flags, halves, received, weights, biases, sums0, sums1, behind, results
            )

        sources = [s for s in (tick, tick - 1) if 0 <= s < segments - 1]
        if tick == segments - 1 and sources:
            (x,) = call(1)
            own, cross = ahead(x, straight, sources), ahead(x, between, sources)
            last, kept = call(0)
            results += [x, last]
        else:
            x, *kept = call(None)
            if tick < segments:
                (kept,) = kept
                results.append(x)
                own, cross = ahead(x, straight, sources), ahead(x, between, sources)
        if tick < segments:
            behind = ahead_call(tick, flags, weights, kept)
            own, behind = lax.optimization_barrier((own, behind))
            received = (own, swap(own, in_chip, [s + 1 for s in sources]), cross)
    return x[None]


def solution(mesh):
    placed = (
        P(None, "band", None, None),
        P("segment", None, None, "band", None, None),
        P("segment", None, None, None, None, None),
        P("segment", None, None),
        P("segment"),
    )
    return jax.shard_map(
        per_device,
        mesh=mesh,
        in_specs=placed,
        out_specs=P("segment", None, "band", None, None),
        check_vma=False,
    )
```

```python
import functools

import jax
import jax.numpy as jnp
from jax import lax
from jax.experimental import pallas as pl
from jax.experimental.pallas import tpu as pltpu
from jax.sharding import PartitionSpec as P

LIMIT = 28 * 1024 * 1024
HISTORY_LIMIT = 52 * 1024 * 1024
F32 = jnp.float32
PAD = 8
BF16 = jnp.bfloat16


def message_starts(layers):
    starts = [0]
    for level in range(layers):
        starts.append(starts[-1] + layers - level)
    return starts


def taps_into(s_ref, row, a, line):
    width, channels = a.shape
    line[PAD : PAD + width] = a
    s_ref[row, :, 0:channels] = line[PAD - 1 : PAD - 1 + width].astype(BF16)
    s_ref[row, :, channels : 2 * channels] = a.astype(BF16)
    s_ref[row, :, 2 * channels : 3 * channels] = line[PAD + 1 : PAD + 1 + width].astype(BF16)


def clear_lines(lines):
    edge = jnp.zeros((PAD, lines.shape[2]), F32)
    for i in range(lines.shape[0]):
        lines[i, 0:PAD] = edge
        lines[i, lines.shape[1] - PAD :] = edge


def pairs_dot(first, count, w, layer, *terms):
    width, depth = terms[0][0].shape[1:]
    channels = depth // 3
    taps = jnp.concatenate(
        [
            jnp.concatenate([s_ref[first + i + 2 * p] for p in range(count)], axis=0)
            for s_ref, _ in terms
            for i in range(4)
        ],
        axis=1,
    )
    zero = jnp.zeros((channels, channels), BF16)

    def tap(i, j, time):
        return w[layer, 3 * i + j, time] if 0 <= i < 3 else zero

    weights = jnp.concatenate(
        [
            jnp.concatenate([tap(i, j, time), tap(i - 1, j, time)], axis=1)
            for _, time in terms
            for i in range(4)
            for j in range(3)
        ],
        axis=0,
    )
    total = jnp.dot(taps, weights, preferred_element_type=F32)
    upper = total[:, :channels].reshape(count, 1, width, channels)
    lower = total[:, channels:].reshape(count, 1, width, channels)
    return jnp.concatenate([upper, lower], axis=1).reshape(2 * count, width, channels)


def history_kernel(frame, flags, caches, w, sums, inner, cross, *refs):
    layers, _, rows, width, channels = caches.shape
    begin = layers - flags[2]
    if frame == 0:
        held, wb, s, lines, sems = refs
    else:
        held, wb = caches, w
        s, lines = refs

    def loads(layer):
        return [
            pltpu.make_async_copy(caches.at[layer], held.at[layer], sems.at[layer, 0]),
            pltpu.make_async_copy(w.at[layer, :, 0:2], wb.at[layer], sems.at[layer, 1]),
        ]

    if frame == 0:
        for layer in range(layers):

            @pl.when(layer < flags[2])
            def _(layer=layer):
                for copy in loads(layer):
                    copy.start()

    clear_lines(lines)
    for f in range(frame, 2):
        s[f, 0:2] = jnp.zeros((2,) + s.shape[2:], BF16)
        s[f, rows + 2 : rows + 4] = jnp.zeros((2,) + s.shape[2:], BF16)

    def layer_step(layer, _):
        if frame == 0:
            history, taps = loads(layer)
            history.wait()

        def build(row, _):
            for f in range(frame, 2):
                taps_into(s.at[f], row + 2, held[layer, f, row].astype(F32), lines.at[f])
            return 0

        lax.fori_loop(0, rows, build, 0)
        if frame == 0:
            taps.wait()
        terms = [(s.at[f], f - frame) for f in range(frame, 2)]
        sums[begin + layer] = pairs_dot(0, (rows + 2) // 2, wb, layer, *terms).astype(BF16)
        return 0

    lax.fori_loop(0, flags[2], layer_step, 0)
    starts = message_starts(layers)

    def messages(up, down):
        for level in range(layers):
            reach = layers - level
            up[starts[level] : starts[level + 1]] = sums[level, 0:reach]
            down[starts[level] : starts[level + 1]] = sums[level, rows + 2 - reach : rows + 2]

    @pl.when(flags[1] % 2 == 0)
    def _():
        messages(cross, inner)

    @pl.when(flags[1] % 2 != 0)
    def _():
        messages(inner, cross)


def level_rows(rows, layers, level):
    return rows - layers + 1 + level, rows + 2 * (layers - 1 - level)


def parts_of(tick, segments, part_of):
    return tick < segments and part_of != 1, tick > 0 and part_of != 0, tick == segments


def tick_kernel(tick, segments, bands, part_of, flags, w, bias, *refs):
    zero, one, final = parts_of(tick, segments, part_of)
    refs = list(refs)

    def take(count):
        found, refs[:count] = refs[:count], []
        return found

    clip = take(3) if tick < 2 else None
    own, inner, cross = take(3) if tick > 0 else (None, None, None)
    sums0 = take(3) if zero else None
    sums1 = take(3) if one else None
    behind = take(1)[0] if one else None
    results = take(segments + 1) if final else []
    out = take(1)[0]
    kept = take(1)[0] if zero else None
    x, scratch, lines, part, sems = refs
    rows, width, channels = out.shape[-3:]
    layers = w.shape[0]
    starts = message_starts(layers)
    band = flags[1]
    begin = layers - flags[2]
    low = jnp.where(band == 0, rows, 0)
    high = jnp.where(band == bands - 1, 2 * rows, 3 * rows)

    def run(frame, fresh, own, inner, cross, sums, messages):
        def of(source):
            return source[frame] if fresh else source[...]

        x[rows : 2 * rows] = of(own)

        def gather(above, below, side_above, side_below):
            x[0:rows] = of(above)
            x[2 * rows : 3 * rows] = of(below)
            for level in range(layers):

                @pl.when(level >= begin)
                def _(level=level):
                    reach = layers - level
                    start, sums_above, sums_below = starts[level], messages[side_above], messages[side_below]
                    part[level, rows + 1 - reach : rows + 1] = sums_above[start : start + reach]
                    part[level, 2 * rows - 1 : 2 * rows - 1 + reach] = sums_below[start : start + reach]
                    part[level, rows + 1 : 2 * rows - 1] = sums[level, 2:rows]
                    part[level, rows] += sums[level, 1]
                    part[level, 2 * rows - 1] += sums[level, rows]
                    if reach > 1:
                        part[level, rows - 1] += sums[level, 0]
                        part[level, 2 * rows] += sums[level, rows + 1]

        @pl.when(band % 2 == 0)
        def _():
            gather(cross, inner, 1, 0)

        @pl.when(band % 2 != 0)
        def _():
            gather(inner, cross, 0, 1)

        clear_lines(lines)

        def build(s, row, line):
            half = x[row].astype(F32) * 0.5
            inside = jnp.logical_and(row >= low, row < high).astype(F32)
            taps_into(s, row, (half + half * jnp.tanh(half)) * inside, line)

        for level in range(layers):

            @pl.when(level >= begin)
            def _(level=level):
                layer = level - begin
                first, count = level_rows(rows, layers, level)
                s = kept.at[level] if frame == 0 else scratch

                def two(i, _):
                    build(s, first - 1 + 2 * i, lines.at[0])
                    build(s, first + 2 * i, lines.at[1])
                    return 0

                lax.fori_loop(0, count // 2 + 1, two, 0)
                offset = bias[pl.ds(layer, 1), :].reshape(1, 1, channels)
                end = first + count
                mine = pairs_dot(first - 1, count // 2, w, layer, (s, 2))
                known = part[level, first:end].astype(F32) + offset
                if frame == 1:
                    known = known + behind[level, first:end].astype(F32)
                x[first:end] = (x[first:end].astype(F32) + (mine + known)).astype(BF16)

        if not final:
            out[...] = x[rows : 2 * rows]
        else:
            copy = pltpu.make_async_copy(x.at[rows : 2 * rows], out.at[frame], sems.at[1])
            copy.start()
            copy.wait()

    def finished(section):
        count = 2 if section + 1 < segments else 1
        found = [results[segments if count == 1 else section], results[section + 1]]
        return [pltpu.make_async_copy(found[f], out.at[f], sems.at[f]) for f in range(count)]

    for section in range(segments if final else 0):

        @pl.when(flags[0] == section)
        def _(section=section):
            for copy in finished(section):
                copy.start()

    for frame, present, parts in ((0, zero, sums0), (1, one, sums1)):
        if present:
            fresh = tick == frame

            @pl.when(flags[0] == tick - frame)
            def _(frame=frame, fresh=fresh, parts=parts):
                run(frame, fresh, *(clip if fresh else (own, inner, cross)), parts[0], parts[1:])

    for section in range(segments if final else 0):

        @pl.when(flags[0] == section)
        def _(section=section):
            for copy in finished(section):
                copy.wait()


def ahead_kernel(tick, flags, w, kept, ahead):
    layers, rows = kept.shape[0], kept.shape[1] // 3
    begin = layers - flags[2]

    @pl.when(flags[0] == tick)
    def _():
        for level in range(layers):

            @pl.when(level >= begin)
            def _(level=level):
                first, count = level_rows(rows, layers, level)
                total = pairs_dot(first - 1, count // 2, w, level - begin, (kept.at[level], 1))
                ahead[level, first : first + count] = total.astype(BF16)


def in_vmem(count):
    return [pl.BlockSpec(memory_space=pltpu.VMEM)] * count


def anywhere():
    return pl.BlockSpec(memory_space=pl.ANY)


def in_smem():
    return pl.BlockSpec(memory_space=pltpu.SMEM)


def history_call(frame, flags, caches, weights):
    layers, _, rows, width, channels = caches.shape
    row = (width, channels)
    message = jax.ShapeDtypeStruct((message_starts(layers)[-1],) + row, BF16)
    outs = [jax.ShapeDtypeStruct((layers, rows + 2) + row, BF16), message, message]
    specs = in_vmem(3)
    scratch = [pltpu.VMEM((2, rows + 4, width, 3 * channels), BF16), pltpu.VMEM((2, width + 2 * PAD, channels), F32)]
    if frame == 0:
        scratch = [
            pltpu.VMEM(caches.shape, BF16),
            pltpu.VMEM((layers, 9, 2, channels, channels), BF16),
            *scratch,
            pltpu.SemaphoreType.DMA((layers, 2)),
        ]
    pixels = layers * (rows + 2) * width
    return pl.pallas_call(
        functools.partial(history_kernel, frame),
        out_shape=tuple(outs),
        in_specs=[in_smem()] + ([anywhere()] * 2 if frame == 0 else in_vmem(2)),
        out_specs=tuple(specs),
        scratch_shapes=scratch,
        compiler_params=pltpu.CompilerParams(vmem_limit_bytes=HISTORY_LIMIT if frame == 0 else LIMIT),
        cost_estimate=pl.CostEstimate(
            flops=pixels * 9 * 2 * (2 - frame) * channels * channels, bytes_accessed=4000000, transcendentals=0
        ),
        name="history",
    )(flags, caches, weights)


def tick_call(tick, segments, bands, part_of, flags, clip, received, weights, biases, sums0, sums1, behind, results):
    layers, _, _, channels, _ = weights.shape
    rows, width = clip[0].shape[1:3]
    every = (layers, 3 * rows, width, channels)
    pixels = sum(rows + 2 * level for level in range(layers)) * width
    zero, one, final = parts_of(tick, segments, part_of)
    extra = (list(clip) if tick < 2 else []) + (list(received) if tick > 0 else [])
    extra += (list(sums0) if zero else []) + (list(sums1) + [behind] if one else [])
    outs, specs = [jax.ShapeDtypeStruct((rows, width, channels), BF16)], in_vmem(1)
    if zero:
        outs.append(jax.ShapeDtypeStruct(every[:3] + (3 * channels,), BF16))
        specs += in_vmem(1)
    if final:
        extra += results
        outs, specs = [jax.ShapeDtypeStruct(clip[0].shape, BF16)], [anywhere()]
    return pl.pallas_call(
        functools.partial(tick_kernel, tick, segments, bands, part_of),
        out_shape=tuple(outs),
        in_specs=[in_smem()] + in_vmem(2 + len(extra)),
        out_specs=tuple(specs),
        scratch_shapes=[
            pltpu.VMEM((3 * rows, width, channels), BF16),
            pltpu.VMEM((3 * rows, width, 3 * channels), BF16),
            pltpu.VMEM((2, width + 2 * PAD, channels), F32),
            pltpu.VMEM(every, BF16),
            pltpu.SemaphoreType.DMA((2,)),
        ],
        compiler_params=pltpu.CompilerParams(vmem_limit_bytes=LIMIT),
        cost_estimate=pl.CostEstimate(
            flops=pixels * 9 * 2 * channels * channels, bytes_accessed=4000000, transcendentals=pixels * channels
        ),
        name="tick",
    )(flags, weights, biases, *extra)


def ahead_call(tick, flags, weights, kept):
    layers, extent, width, depth = kept.shape
    return pl.pallas_call(
        functools.partial(ahead_kernel, tick),
        out_shape=jax.ShapeDtypeStruct((layers, extent, width, depth // 3), BF16),
        in_specs=[in_smem()] + in_vmem(2),
        out_specs=in_vmem(1)[0],
        compiler_params=pltpu.CompilerParams(vmem_limit_bytes=LIMIT),
        cost_estimate=pl.CostEstimate(
            flops=1000000, bytes_accessed=1000000, transcendentals=0
        ),
        name="ahead",
    )(flags, weights, kept)


def per_device(clip, caches, weights, biases, section_layers):
    segments = lax.axis_size("segment")
    bands = lax.axis_size("band")
    caches, weights, biases = caches[0], weights[0], biases[0]
    flags = jnp.stack([lax.axis_index("segment"), lax.axis_index("band"), section_layers[0]]).astype(jnp.int32)
    axes = ("segment", "band")
    in_chip = [(b, b ^ 1) for b in range(bands)]
    between = [(b, b + 1) for b in range(1, bands - 1, 2)] + [(b + 1, b) for b in range(1, bands - 1, 2)]
    straight = [(b, b) for b in range(bands)]

    def swap(value, pairs, chosen):
        return lax.ppermute(value, axes, [(s * bands + a, s * bands + b) for s in chosen for a, b in pairs])

    def ahead(value, pairs, sources):
        return lax.ppermute(value, axes, [(s * bands + a, (s + 1) * bands + b) for s in sources for a, b in pairs])

    def lender(value, pairs):
        source = min(1, segments - 1)
        return lax.ppermute(value, axes, [(source * bands + a, b) for a, b in pairs])

    everyone = range(segments)
    clip_cross = lender(clip, between)
    clip_in = swap(clip, in_chip, [0])
    sums, inner, cross = history_call(0, flags, caches, weights)
    cross = swap(cross, between, everyone)
    caches, clip_cross, _ = lax.optimization_barrier((caches, clip_cross, sums))
    inner, clip_cross = lax.optimization_barrier((inner, clip_cross))
    sums0 = (sums, swap(inner, in_chip, everyone), cross)
    sums, inner, cross = history_call(1, flags, caches, weights)
    sums1 = (sums, swap(inner, in_chip, everyone), swap(cross, between, everyone))
    halves = (clip, clip_in, clip_cross)
    received = behind = None
    results = []
    for tick in range(segments + 1):
        def call(part_of):
            return tick_call(
                tick, segments, bands, part_of, flags, halves, received, weights, biases, sums0, sums1, behind, results
            )

        sources = [s for s in (tick, tick - 1) if 0 <= s < segments - 1]
        if tick == segments - 1 and sources:
            (x,) = call(1)
            own, cross = ahead(x, straight, sources), ahead(x, between, sources)
            last, kept = call(0)
            results += [x, last]
        else:
            x, *kept = call(None)
            if tick < segments:
                (kept,) = kept
                results.append(x)
                own, cross = ahead(x, straight, sources), ahead(x, between, sources)
        if tick < segments:
            behind = ahead_call(tick, flags, weights, kept)
            own, behind = lax.optimization_barrier((own, behind))
            received = (own, swap(own, in_chip, [s + 1 for s in sources]), cross)
    return x[None]


def solution(mesh):
    placed = (
        P(None, "band", None, None),
        P("segment", None, None, "band", None, None),
        P("segment", None, None, None, None, None),
        P("segment", None, None),
        P("segment"),
    )
    return jax.shard_map(
        per_device,
        mesh=mesh,
        in_specs=placed,
        out_specs=P("segment", None, "band", None, None),
        check_vma=False,
    )
```
